512 devices in a mesh: lat: 16 (over z_hi, x), lon: 32 (over y, z_lo, core).
Axes of the slice: x: 4, y: 4, z: 16 (z_hi: 4, z_lo: 4; z = z_hi * 4 + z_lo), core: 2. Of those that a mesh axis runs over, the one named last changes fastest.
Arguments:
- tracer: float32 [6, 16, 128, 4096], P(None, None, 'lat', 'lon'), may hold values from -6 to 6
- east_vel: float32 [16, 128, 4096], P(None, 'lat', 'lon'), may hold values from -0.25 to 0.25
- north_vel: float32 [16, 128, 4096], P(None, 'lat', 'lon'), may hold values from -0.25 to 0.25
- wet_mask: int32 [16, 128, 4096], P(None, 'lat', 'lon'), may hold values from 0 to 1, as said below
- bottom_level: int32 [128, 4096], P('lat', 'lon'), may hold values from 0 to 16, as said below
- vertical_mix: float32 [16, 128, 4096], P(None, 'lat', 'lon'), may hold values from 0.05 to 5
Outputs:
- updated: float32 [6, 16, 128, 4096], P(None, None, 'lat', 'lon')
The draws below stay inside these ranges and needn't reach their ends.
Inputs may be any that keep to these rules, and one draw needn't show every extreme that they name: bottom_level is the number of levels above a column's sea floor; 0 on land. wet_mask is 0 at every level at or below its column's bottom_level.
All inputs are finite; a program needn't handle non-finite values.
Results may differ from the reference program's by a relative error of at most 0.00002.
Values sent between devices are 32-bit elements; how exact they have to be, the bound alone decides.
No kernel may reach another device: no remote copies, remote signals or barrier semaphores. Data moves between devices by JAX's collectives and lax.ppermute only.
A program may use at most 64 MiB of HBM per device.

```python
import math
import jax
import jax.numpy as jnp
from jax import lax

NT = 6
K = 16
NY = 128
NX = 4096


def land_columns(key):
    coarse_rows = (NY + 15) // 16
    coarse_cols = (NX + 15) // 16
    blocks = jax.random.randint(jax.random.fold_in(key, 11), (coarse_rows, coarse_cols), 0, 4)
    row_ids = lax.broadcasted_iota(jnp.int32, (NY, NX), 0)
    col_ids = lax.broadcasted_iota(jnp.int32, (NY, NX), 1)
    inner_rows = (row_ids % 4 == 1) | (row_ids % 4 == 2)
    inner_cols = (col_ids % 4 == 1) | (col_ids % 4 == 2)
    land_cells = jnp.repeat(jnp.repeat(blocks == 0, 16, axis=0), 16, axis=1)[:NY, :NX] & inner_rows & inner_cols
    depths = jax.random.randint(jax.random.fold_in(key, 12), (NY, NX), 1, K + 1)
    marker = (col_ids + 3 * row_ids) % 37
    depths = jnp.where(land_cells, 0, depths)
    depths = jnp.where(marker == 0, K, depths)
    depths = jnp.where(marker == 1, 0, depths)
    return depths.astype(jnp.int32)


def draw_bottom_level(key, part):
    columns = land_columns(key)
    return columns


def draw_wet_mask(key, part):
    columns = land_columns(key)
    key = jax.random.fold_in(key, 5)
    sprinkle = jax.random.randint(key, (K, NY, NX), 0, 8) != 0
    level_ids = lax.broadcasted_iota(jnp.int32, (K, NY, NX), 0)
    return ((level_ids < columns[None, :, :]) & sprinkle).astype(jnp.int32)


def block_levels(key, extent, shards, least, top_value):
    loudness = 1.0
    for axis_at, parts in shards:
        steps = jax.random.uniform(jax.random.fold_in(jax.random.fold_in(key, 6), axis_at), (parts,), jnp.float32, least / len(shards), top_value / len(shards))
        loudness = loudness * jnp.repeat(jnp.exp(steps), extent[axis_at] // parts).reshape((-1,) + (1,) * (len(extent) - 1 - axis_at))
    return loudness


def scatter_about(key, extent, spread, reach, cuts=(), kind=jnp.bfloat16):
    gain = block_levels(key, extent, cuts, -0.22, 0.18) if cuts else 1.0
    values = jax.random.normal(key, extent, jnp.float32) * spread * gain
    return jnp.minimum(jnp.maximum(values, -reach), reach).astype(kind)


def setup_inputs(seed: int = 0) -> dict:
    keys = jax.random.split(jax.random.key(seed), 7)
    return {
        "tracer": scatter_about(keys[0], (NT, K, NY, NX), 1.0, 6.0, ((2, 16), (3, 32)), jnp.float32),
        "east_vel": jnp.clip(jax.random.uniform(keys[1], (K, NY, NX), jnp.float32, -0.25, 0.25) * block_levels(keys[1], (K, NY, NX), ((1, 16), (2, 32)), -0.4, 0.0), -0.25, 0.25),
        "north_vel": jnp.clip(jax.random.uniform(keys[2], (K, NY, NX), jnp.float32, -0.25, 0.25) * block_levels(keys[2], (K, NY, NX), ((1, 16), (2, 32)), -0.4, 0.0), -0.25, 0.25),
        "wet_mask": draw_wet_mask(jax.random.fold_in(keys[6], 71), 0),
        "bottom_level": draw_bottom_level(jax.random.fold_in(keys[6], 71), 0),
        "vertical_mix": jnp.clip(jnp.exp(math.log(5.0) - 4.6051702 * jax.random.uniform(keys[5], (K, NY, NX), jnp.float32) ** block_levels(keys[5], (K, NY, NX), ((1, 16), (2, 32)), -0.2, 0.2)), 0.05, 5.0),
    }


lateral_mixing = 0.08


def pad_global(field, sign_value):
    wrapped = jnp.concatenate([field[..., -1:], field, field[..., :1]], axis=-1)
    north_rows = sign_value * wrapped[..., -1:, ::-1]
    south_rows = jnp.zeros_like(north_rows)
    return jnp.concatenate([south_rows, wrapped, north_rows], axis=-2)


def flux_sum(tracer_pad, east_pad, north_pad, mask_pad):
    east_speed = 0.5 * (east_pad[..., 1:-1, :-1] + east_pad[..., 1:-1, 1:])
    east_open = mask_pad[..., 1:-1, :-1] * mask_pad[..., 1:-1, 1:]
    west_side = tracer_pad[..., 1:-1, :-1]
    east_side = tracer_pad[..., 1:-1, 1:]
    east_flux = east_open * (jnp.maximum(east_speed, 0.0) * west_side + jnp.minimum(east_speed, 0.0) * east_side - lateral_mixing * (east_side - west_side))
    north_speed = 0.5 * (north_pad[..., :-1, 1:-1] + north_pad[..., 1:, 1:-1])
    north_open = mask_pad[..., :-1, 1:-1] * mask_pad[..., 1:, 1:-1]
    south_side = tracer_pad[..., :-1, 1:-1]
    north_side = tracer_pad[..., 1:, 1:-1]
    north_flux = north_open * (jnp.maximum(north_speed, 0.0) * south_side + jnp.minimum(north_speed, 0.0) * north_side - lateral_mixing * (north_side - south_side))
    return mask_pad[..., 1:-1, 1:-1] * (((east_flux[..., :-1] - east_flux[..., 1:]) + north_flux[..., :-1, :]) - north_flux[..., 1:, :])


def solve_columns(rhs_field, couple):
    level_count = couple.shape[0]
    ratios = []
    values = []
    upper_c = couple[0]
    denom = 1.0 + upper_c
    ratio_prev = -upper_c / denom
    value_prev = rhs_field[..., 0, :, :] / denom
    ratios.append(ratio_prev)
    values.append(value_prev)
    for level_index in range(1, level_count):
        lower_c = couple[level_index - 1]
        upper_c = couple[level_index]
        denom = 1.0 + lower_c + upper_c + lower_c * ratio_prev
        ratio_prev = -upper_c / denom
        value_prev = (rhs_field[..., level_index, :, :] + lower_c * value_prev) / denom
        ratios.append(ratio_prev)
        values.append(value_prev)
    result_rows = [values[level_count - 1]]
    for level_index in range(level_count - 2, -1, -1):
        result_rows.append(values[level_index] - ratios[level_index] * result_rows[-1])
    return jnp.stack(result_rows[::-1], axis=-3)


def reference(tracer, east_vel, north_vel, wet_mask, bottom_level, vertical_mix):
    mask_float = wet_mask.astype(jnp.float32)
    east_pad = pad_global(east_vel, -1.0)
    north_pad = pad_global(north_vel, -1.0)
    mask_pad = pad_global(mask_float, 1.0)
    level_ids = lax.broadcasted_iota(jnp.int32, vertical_mix.shape, 0)
    couple = jnp.where(level_ids + 1 < bottom_level[None, :, :], vertical_mix, jnp.float32(0.0))

    def one_tracer(field_now):
        section_one = field_now + flux_sum(pad_global(field_now, 1.0), east_pad, north_pad, mask_pad)
        section_two = 0.5 * ((field_now + section_one) + flux_sum(pad_global(section_one, 1.0), east_pad, north_pad, mask_pad))
        return solve_columns(section_two, couple)

    return lax.map(one_tracer, tracer)
```

```python
import jax
import jax.numpy as jnp
from jax import lax
from jax.experimental import pallas as pl
from jax.experimental.pallas import tpu as pltpu
from jax.sharding import PartitionSpec as P

ROWS = 8
COLS = 128
NT = 6
K = 16
TILES = NT * K
mixing = 0.08
AXES = ("lat", "lon")

FIELDS = NT + 3
PACKS = (FIELDS + 1) // 2
PACK_ROWS = PACKS * ROWS
TPACKS = NT // 2

ROW_T = 0
ROW_P = TILES
ROW_V = 2 * TILES
ROW_M = ROW_V + K
ROW_C = ROW_M + K
PAY_ROWS = ROW_C + ROWS

AUX_F = 0
AUX_Q = TPACKS
AUX_T = 2 * TPACKS
AUX_V = 3 * TPACKS
AUX_M = AUX_V + 1
AUX_A = AUX_M + 1
AUX_B = AUX_A + 1
AUX = AUX_T + ROWS


def roll(x, shift, axis):
    shift %= x.shape[axis]
    return pltpu.roll(x, shift, axis) if shift else x


def lanes(rows=ROWS):
    return lax.broadcasted_iota(jnp.int32, (rows, COLS), 1)


def row_ids():
    return lax.broadcasted_iota(jnp.int32, (ROWS, COLS), 0)


def face(speed, opening):
    return opening * (jnp.maximum(speed, 0.0) + mixing), opening * (jnp.minimum(speed, 0.0) - mixing)


def tile(ref, index):
    return ref[index * ROWS : (index + 1) * ROWS, :]


def edge_kernel(tracer, east, north, mask, pack):
    group = lanes() // 4
    for half_pair in range(PACKS):
        total = jnp.zeros((ROWS, COLS), jnp.float32)
        for half in range(2):
            field = 2 * half_pair + half
            if field >= FIELDS:
                continue
            for k in range(K):
                if field < NT:
                    x = tile(tracer, field * K + k)
                elif field == NT:
                    x = tile(east, k)
                elif field == NT + 1:
                    x = tile(mask, k).astype(jnp.float32)
                else:
                    x = tile(north, k)
                base = 64 * half + 4 * k
                total = jnp.where(group == base // 4, roll(x, base - 126, 1), total)
        pack[half_pair * ROWS : (half_pair + 1) * ROWS, :] = total


def level_faces(east, north, mask, k):
    u, v, m = tile(east, k), tile(north, k), tile(mask, k).astype(jnp.float32)
    inner_x = lanes() < COLS - 1
    inner_y = row_ids() < ROWS - 1
    open_x = jnp.where(inner_x, m * roll(m, -1, 1), 0.0)
    open_y = jnp.where(inner_y, m * roll(m, -1, 0), 0.0)
    ax, bx = face(0.5 * (u + roll(u, -1, 1)), open_x)
    ay, by = face(0.5 * (v + roll(v, -1, 0)), open_y)
    return ax, bx, ay, by


def inner_sum(t, faces):
    ax, bx, ay, by = faces
    fe = ax * t + bx * roll(t, -1, 1)
    gn = ay * t + by * roll(t, -1, 0)
    return (roll(fe, 1, 1) - fe) + (roll(gn, 1, 0) - gn)


def edge_sign():
    lane = lanes()
    return jnp.where(lane == 0, 1.0, jnp.where(lane == COLS - 1, -1.0, 0.0))


def spread(packed, field, k):
    return roll(packed, COLS - 1 - (64 * (field % 2) + 4 * k + 1), 1)


def both_halves(x, half):
    swapped = roll(x, 64, 1)
    low = lanes() < 64
    return jnp.where(low, x, swapped) if half == 0 else jnp.where(low, swapped, x)


def flipped(x):
    lane = lanes(x.shape[0])
    for step in (1, 2, 4, 8, 16, 32, 64):
        x = jnp.where((lane & step) != 0, roll(x, step, 1), roll(x, -step, 1))
    return x


def first_kernel(own, near, far, tracer, east, north, mask, pay_far, pay_near, part, aux):
    lat_odd = lax.rem(lax.axis_index("lat"), 2)
    lon_odd = lax.rem(lax.axis_index("lon"), 2)
    is_top = lax.axis_index("lat") == lax.axis_size("lat") - 1
    at_east = (lanes() & 3) == 1
    even = lon_odd == 0
    offset = pl.multiple_of((1 - lon_odd) * PACK_ROWS, ROWS)
    one, two, here = [], [], []
    for p in range(PACKS):
        a = near[pl.ds(pl.multiple_of(offset + p * ROWS, ROWS), ROWS), :]
        b = tile(far, p)
        e = jnp.where(even, a, b)
        w = jnp.where(even, b, a)
        here.append(tile(own, p))
        one.append(jnp.where(at_east, roll(e, -1, 1), roll(w, 1, 1)))
        two.append(jnp.where(at_east, roll(e, -2, 1), roll(w, 2, 1)))
    u0, m0 = both_halves(here[TPACKS], 0), both_halves(here[TPACKS], 1)
    u1, m1 = both_halves(one[TPACKS], 0), both_halves(one[TPACKS], 1)
    u2, m2 = both_halves(two[TPACKS], 0), both_halves(two[TPACKS], 1)
    v1 = both_halves(one[TPACKS + 1], 0)
    a1, b1 = face(0.5 * (u0 + u1), m0 * m1)
    a2, b2 = face(0.5 * (u1 + u2), m1 * m2)
    inner_y = row_ids() < ROWS - 1
    ay, by = face(0.5 * (v1 + roll(v1, -1, 0)), jnp.where(inner_y, m1 * roll(m1, -1, 0), 0.0))
    flux = []
    for p in range(TPACKS):
        t0, t1, t2 = here[p], one[p], two[p]
        f1 = a1 * jnp.where(at_east, t0, t1) + b1 * jnp.where(at_east, t1, t0)
        f2 = a2 * jnp.where(at_east, t1, t2) + b2 * jnp.where(at_east, t2, t1)
        gn = ay * t1 + by * roll(t1, -1, 0)
        flux.append(f1)
        q = t1 + jnp.where(at_east, -f2, f2) + (roll(gn, 1, 0) - gn)
        aux[(AUX_F + p) * ROWS : (AUX_F + p + 1) * ROWS, :] = f1
        aux[(AUX_Q + p) * ROWS : (AUX_Q + p + 1) * ROWS, :] = q
        aux[(AUX_T + p) * ROWS : (AUX_T + p + 1) * ROWS, :] = t1
    for place, x in ((AUX_V, v1), (AUX_M, m1), (AUX_A, a1), (AUX_B, b1)):
        aux[place * ROWS : (place + 1) * ROWS, :] = x
    for place in range(AUX_B + 1, AUX):
        aux[place * ROWS : (place + 1) * ROWS, :] = jnp.zeros((ROWS, COLS), jnp.float32)
    sign = edge_sign()
    for k in range(K):
        faces = level_faces(east, north, mask, k)
        for f in range(NT):
            t = tile(tracer, f * K + k)
            index = f * K + k
            part[index * ROWS : (index + 1) * ROWS, :] = (
                t + inner_sum(t, faces) + sign * spread(flux[f // 2], f, k)
            )
    for pay, row in ((pay_far, (ROWS - 1) * lat_odd), (pay_near, (ROWS - 1) * (1 - lat_odd))):
        pay[ROW_T : ROW_T + TILES, :] = tracer[pl.ds(row, TILES, stride=ROWS), :]
        pay[ROW_P : ROW_P + TILES, :] = part[pl.ds(row, TILES, stride=ROWS), :]
        pay[ROW_V : ROW_V + K, :] = north[pl.ds(row, K, stride=ROWS), :]
        pay[ROW_M : ROW_M + K, :] = mask[pl.ds(row, K, stride=ROWS), :].astype(jnp.float32)
        pay[ROW_C : ROW_C + ROWS, :] = aux[pl.ds(AUX_T * ROWS + row, ROWS, stride=ROWS), :]

    @pl.when(is_top)
    def _():
        for start in range(0, ROW_C, K):
            x = flipped(pay_far[start : start + K, :])
            pay_far[start : start + K, :] = -x if start == ROW_V else x
        c = pay_far[ROW_C : ROW_C + ROWS, :]
        c = jnp.where(at_east, roll(c, -1, 1), roll(c, 1, 1))
        pay_far[ROW_C : ROW_C + ROWS, :] = jnp.where(row_ids() == TPACKS, -c, c)


def last_kernel(far, near, tracer, east, north, mask, mix, bottom, part, aux, out, face_n, face_s, one):
    lat_odd = lax.rem(lax.axis_index("lat"), 2)
    odd = lat_odd == 1
    offset = pl.multiple_of((1 - lat_odd) * PAY_ROWS, ROWS)
    at_east = (lanes() & 3) == 1
    rows = row_ids()
    at_south, at_north = rows == 0, rows == ROWS - 1

    def both(start, size):
        a = far[start : start + size, :]
        b = near[pl.ds(pl.multiple_of(offset + start, ROWS), size), :]
        return jnp.where(odd, a, b), jnp.where(odd, b, a)

    def edge(ref, start, size, row):
        return ref[pl.ds(start * ROWS + row, size, stride=ROWS), :]

    v_n, v_s = both(ROW_V, K)
    m_n, m_s = both(ROW_M, K)
    c_n, c_s = both(ROW_C, ROWS)
    an, bn = face(
        0.5 * (edge(north, 0, K, ROWS - 1) + v_n), edge(mask, 0, K, ROWS - 1).astype(jnp.float32) * m_n
    )
    as_, bs = face(0.5 * (v_s + edge(north, 0, K, 0)), m_s * edge(mask, 0, K, 0).astype(jnp.float32))
    s_n, s_s = [], []
    for f in range(NT):
        t_n, t_s = both(ROW_T + f * K, K)
        p_n, p_s = both(ROW_P + f * K, K)
        g_n = an * edge(tracer, f * K, K, ROWS - 1) + bn * t_n
        g_s = as_ * t_s + bs * edge(tracer, f * K, K, 0)
        face_n[f * K : (f + 1) * K, :] = g_n
        face_s[f * K : (f + 1) * K, :] = g_s
        s_n.append(p_n + g_n)
        s_s.append(p_s - g_s)

    def outer(index):
        return jnp.where(at_south, face_s[index : index + 1, :], 0.0) - jnp.where(
            at_north, face_n[index : index + 1, :], 0.0
        )

    group = lanes() // 4
    own = []
    for p in range(TPACKS):
        packed = jnp.zeros((ROWS, COLS), jnp.float32)
        for f in (2 * p, 2 * p + 1):
            for k in range(K):
                index = f * K + k
                s = tile(part, index) + outer(index)
                one[index * ROWS : (index + 1) * ROWS, :] = s
                base = 64 * (f % 2) + 4 * k
                packed = jnp.where(group == base // 4, roll(s, base - 126, 1), packed)
        own.append(packed)
    v1, m1, a1, b1 = (tile(aux, x) for x in (AUX_V, AUX_M, AUX_A, AUX_B))
    acn, bcn = face(0.5 * (v1 + c_n[TPACKS : TPACKS + 1]), m1 * c_n[TPACKS + 1 : TPACKS + 2])
    acs, bcs = face(0.5 * (c_s[TPACKS : TPACKS + 1] + v1), c_s[TPACKS + 1 : TPACKS + 2] * m1)
    flux = []
    for p in range(TPACKS):
        f1, q, t1 = tile(aux, AUX_F + p), tile(aux, AUX_Q + p), tile(aux, AUX_T + p)
        gcn = acn * t1 + bcn * c_n[p : p + 1]
        gcs = acs * c_s[p : p + 1] + bcs * t1
        s1 = (
            q
            + jnp.where(at_east, f1, -f1)
            + jnp.where(at_south, gcs, 0.0)
            - jnp.where(at_north, gcn, 0.0)
        )
        flux.append(a1 * jnp.where(at_east, own[p], s1) + b1 * jnp.where(at_east, s1, own[p]))
    for f in range(NT):
        face_n[f * K : (f + 1) * K, :] = an * edge(one, f * K, K, ROWS - 1) + bn * s_n[f]
        face_s[f * K : (f + 1) * K, :] = as_ * s_s[f] + bs * edge(one, f * K, K, 0)

    depth = bottom[...]
    sign = edge_sign()
    values = [None] * NT
    lower = None
    ratios = []
    for k in range(K):
        faces = level_faces(east, north, mask, k)
        upper = jnp.where(k + 1 < depth, tile(mix, k), 0.0) if k + 1 < K else None
        denom = 1.0
        if upper is not None:
            denom = denom + upper
        if k:
            denom = denom + lower + lower * ratios[-1]
        inverse = 1.0 / denom
        if upper is not None:
            ratios.append(-upper * inverse)
        for f in range(NT):
            index = f * K + k
            s = tile(one, index)
            total = inner_sum(s, faces) + sign * spread(flux[f // 2], f, k) + outer(index)
            rhs = 0.5 * ((tile(tracer, index) + s) + total)
            if k:
                rhs = rhs + lower * values[f]
            values[f] = rhs * inverse
            out[index * ROWS : (index + 1) * ROWS, :] = values[f]
        lower = upper
    for k in range(K - 2, -1, -1):
        for f in range(NT):
            index = f * K + k
            values[f] = tile(out, index) - ratios[k] * values[f]
            out[index * ROWS : (index + 1) * ROWS, :] = values[f]


def call(kernel, out_rows, scratch_rows, *operands):
    vmem = pl.BlockSpec(memory_space=pltpu.VMEM)
    shapes = [jax.ShapeDtypeStruct((rows, COLS), jnp.float32) for rows in out_rows]
    return pl.pallas_call(
        kernel,
        out_shape=shapes,
        in_specs=[vmem] * len(operands),
        out_specs=[vmem] * len(shapes),
        scratch_shapes=[pltpu.VMEM((rows, COLS), jnp.float32) for rows in scratch_rows],
        compiler_params=pltpu.CompilerParams(vmem_limit_bytes=24 * 1024 * 1024),
    )(*operands)


def pairs(lat_count, lon_count):
    def at(i, j):
        return i * lon_count + j % lon_count

    lon_near = [(at(i, j), at(i, j + 1)) for i in range(lat_count) for j in range(0, lon_count, 2)]
    lon_far = [(at(i, j), at(i, j + 1)) for i in range(lat_count) for j in range(1, lon_count, 2)]
    lat_near = [(at(i, j), at(i + 1, j)) for i in range(0, lat_count, 2) for j in range(lon_count)]
    lat_far = [(at(i, j), at(i + 1, j)) for i in range(1, lat_count - 1, 2) for j in range(lon_count)]
    top = lat_count - 1
    lat_far += [(at(top, j), at(top, lon_count - 1 - j)) for j in range(lon_count // 2)]
    return lon_near, lon_far, lat_near, lat_far


def swapped(x, groups):
    return lax.ppermute(x, AXES, [(a, b) for a, b in groups] + [(b, a) for a, b in groups])


def gathered(x, groups):
    both = lax.all_gather(x, AXES, axis_index_groups=[list(g) for g in groups])
    return both.reshape(-1, COLS)


def on_device(tracer, east_vel, north_vel, wet_mask, bottom_level, vertical_mix):
    lon_near, lon_far, lat_near, lat_far = pairs(lax.axis_size("lat"), lax.axis_size("lon"))
    flat = lambda x: x.reshape(-1, COLS)
    t, u, v, m, mix = map(flat, (tracer, east_vel, north_vel, wet_mask, vertical_mix))
    (own,) = call(edge_kernel, [PACK_ROWS], [], t, u, v, m)
    far = swapped(own, lon_far)
    near = gathered(own, lon_near)
    pay_far, pay_near, part, aux = call(
        first_kernel,
        [PAY_ROWS, PAY_ROWS, TILES * ROWS, AUX * ROWS],
        [],
        own, near, far, t, u, v, m,
    )
    far_rows = swapped(pay_far, lat_far)
    near_rows = gathered(pay_near, lat_near)
    (out,) = call(
        last_kernel,
        [TILES * ROWS],
        [TILES, TILES, TILES * ROWS],
        far_rows, near_rows, t, u, v, m, mix, bottom_level, part, aux,
    )
    return out.reshape(tracer.shape)


def solution(mesh):
    fields = P(None, "lat", "lon")
    tracers = P(None, None, "lat", "lon")
    return jax.shard_map(
        on_device,
        mesh=mesh,
        in_specs=(tracers, fields, fields, fields, P("lat", "lon"), fields),
        out_specs=tracers,
        check_vma=False,
    )
```

```python
import jax
import jax.numpy as jnp
from jax import lax
from jax.experimental import pallas as pl
from jax.experimental.pallas import tpu as pltpu
from jax.sharding import PartitionSpec as P

ROWS = 8
COLS = 128
NT = 6
K = 16
TILES = NT * K
mixing = 0.08
AXES = ("lat", "lon")

FIELDS = NT + 3
PACKS = (FIELDS + 1) // 2
PACK_ROWS = PACKS * ROWS
TPACKS = NT // 2

ROW_T = 0
ROW_P = TILES
ROW_V = 2 * TILES
ROW_M = ROW_V + K
ROW_C = ROW_M + K
PAY_ROWS = ROW_C + ROWS

AUX_T = 0
AUX_V = TPACKS
AUX_M = AUX_V + 1
AUX_F = AUX_M + 1
AUX_Q = AUX_F + TPACKS
AUX_A = AUX_Q + TPACKS
AUX_B = AUX_A + 1
AUX = AUX_B + 1


def roll(x, shift, axis):
    shift %= x.shape[axis]
    return pltpu.roll(x, shift, axis) if shift else x


def lanes(rows=ROWS):
    return lax.broadcasted_iota(jnp.int32, (rows, COLS), 1)


def row_ids():
    return lax.broadcasted_iota(jnp.int32, (ROWS, COLS), 0)


def face(speed, opening):
    return opening * (jnp.maximum(speed, 0.0) + mixing), opening * (jnp.minimum(speed, 0.0) - mixing)


def tile(ref, index):
    return ref[index * ROWS : (index + 1) * ROWS, :]


def put(ref, index, value):
    ref[index * ROWS : (index + 1) * ROWS, :] = value


def edge(ref, start, size, row):
    return ref[pl.ds(start * ROWS + row, size, stride=ROWS), :]


def lane_base(field, k):
    return 64 * (field % 2) + 4 * (K - 1 - k)


def packed_edges(load, fields):
    group = lanes() // 4
    total = jnp.zeros((ROWS, COLS), jnp.float32)
    for field in fields:
        for k in range(K):
            base = lane_base(field, k)
            total = jnp.where(group == base // 4, roll(load(field, k), base - 126, 1), total)
    return total


def load_kernel(tracer, east, north, mask, pack, t, u, v, m, sems):
    copies = [
        pltpu.make_async_copy(src, dst, sems.at[i])
        for i, (src, dst) in enumerate(((east, u), (north, v), (mask, m), (tracer, t)))
    ]
    for copy in copies:
        copy.start()
    for copy in copies[:3]:
        copy.wait()

    def load(field, k):
        if field < NT:
            return tile(t, field * K + k)
        if field == NT:
            return tile(u, k)
        if field == NT + 1:
            return tile(m, k).astype(jnp.float32)
        return tile(v, k)

    for p in range(TPACKS, PACKS):
        put(pack, p, packed_edges(load, range(2 * p, min(2 * p + 2, FIELDS))))
    copies[3].wait()
    for p in range(TPACKS):
        put(pack, p, packed_edges(load, range(2 * p, 2 * p + 2)))


def level_faces(east, north, mask, k):
    u, v, m = tile(east, k), tile(north, k), tile(mask, k).astype(jnp.float32)
    open_x = jnp.where(lanes() < COLS - 1, m * roll(m, -1, 1), 0.0)
    open_y = jnp.where(row_ids() < ROWS - 1, m * roll(m, -1, 0), 0.0)
    ax, bx = face(0.5 * (u + roll(u, -1, 1)), open_x)
    ay, by = face(0.5 * (v + roll(v, -1, 0)), open_y)
    return ax, bx, ay, by


def inner_sum(t, faces):
    ax, bx, ay, by = faces
    fe = ax * t + bx * roll(t, -1, 1)
    gn = ay * t + by * roll(t, -1, 0)
    return (roll(fe, 1, 1) - fe) + (roll(gn, 1, 0) - gn)


def flipped(x):
    lane = lanes(x.shape[0])
    for step in (1, 2, 4, 8, 16, 32, 64):
        x = jnp.where((lane & step) != 0, roll(x, step, 1), roll(x, -step, 1))
    return x


def inner_kernel(tracer, east, north, mask, part, coeff, pay_far, pay_near):
    lat_odd = lax.rem(lax.axis_index("lat"), 2)
    is_top = lax.axis_index("lat") == lax.axis_size("lat") - 1
    for k in range(K):
        faces = level_faces(east, north, mask, k)
        for i in range(4):
            put(coeff, i * K + k, faces[i])
        for f in range(NT):
            index = f * K + k
            t = tile(tracer, index)
            put(part, index, t + inner_sum(t, faces))
    for pay, row in ((pay_far, (ROWS - 1) * lat_odd), (pay_near, (ROWS - 1) * (1 - lat_odd))):
        pay[ROW_T : ROW_T + TILES, :] = edge(tracer, 0, TILES, row)
        pay[ROW_P : ROW_P + TILES, :] = edge(part, 0, TILES, row)
        pay[ROW_V : ROW_V + K, :] = edge(north, 0, K, row)
        pay[ROW_M : ROW_M + K, :] = edge(mask, 0, K, row).astype(jnp.float32)
        pay[ROW_C : ROW_C + ROWS, :] = jnp.zeros((ROWS, COLS), jnp.float32)

    @pl.when(is_top)
    def _():
        x = flipped(pay_far[:ROW_C, :])
        pay_far[:ROW_V, :] = x[:ROW_V]
        pay_far[ROW_V:ROW_M, :] = -x[ROW_V:ROW_M]
        pay_far[ROW_M:ROW_C, :] = x[ROW_M:]


def both_halves(x, half):
    swapped = roll(x, 64, 1)
    low = lanes() < 64
    return jnp.where(low, x, swapped) if half == 0 else jnp.where(low, swapped, x)


def edge_sign():
    lane = lanes()
    return jnp.where(lane == 0, 1.0, jnp.where(lane == COLS - 1, -1.0, 0.0))


def outward_kernel(own, near, far, pay_far_in, pay_near_in, pay_far, pay_near, aux):
    lat_odd = lax.rem(lax.axis_index("lat"), 2)
    lon_odd = lax.rem(lax.axis_index("lon"), 2)
    is_top = lax.axis_index("lat") == lax.axis_size("lat") - 1
    place = lanes() & 3
    at_east = place == 1
    even = lon_odd == 0
    offset = pl.multiple_of((1 - lon_odd) * PACK_ROWS, ROWS)
    here, one, two = [], [], []
    for p in range(PACKS):
        a = near[pl.ds(pl.multiple_of(offset + p * ROWS, ROWS), ROWS), :]
        b = tile(far, p)
        e = jnp.where(even, a, b)
        w = jnp.where(even, b, a)
        here.append(tile(own, p))
        one.append(jnp.where(at_east, roll(e, -1, 1), roll(w, 1, 1)))
        two.append(jnp.where(at_east, roll(e, -2, 1), roll(w, 2, 1)))
    u0, m0 = both_halves(here[TPACKS], 0), both_halves(here[TPACKS], 1)
    u1, m1 = both_halves(one[TPACKS], 0), both_halves(one[TPACKS], 1)
    u2, m2 = both_halves(two[TPACKS], 0), both_halves(two[TPACKS], 1)
    v0, v1 = both_halves(here[TPACKS + 1], 0), both_halves(one[TPACKS + 1], 0)
    a1, b1 = face(0.5 * (u0 + u1), m0 * m1)
    a2, b2 = face(0.5 * (u1 + u2), m1 * m2)
    inner_y = row_ids() < ROWS - 1
    ay, by = face(0.5 * (v1 + roll(v1, -1, 0)), jnp.where(inner_y, m1 * roll(m1, -1, 0), 0.0))

    def corner(mine, halo):
        return jnp.where(
            place == 0, roll(mine, -1, 1), jnp.where(place == 3, roll(mine, 1, 1), halo)
        )

    for p in range(TPACKS):
        t0, t1, t2 = here[p], one[p], two[p]
        f1 = a1 * jnp.where(at_east, t0, t1) + b1 * jnp.where(at_east, t1, t0)
        f2 = a2 * jnp.where(at_east, t1, t2) + b2 * jnp.where(at_east, t2, t1)
        gn = ay * t1 + by * roll(t1, -1, 0)
        put(aux, AUX_F + p, f1)
        put(aux, AUX_Q + p, t1 + jnp.where(at_east, -f2, f2) + (roll(gn, 1, 0) - gn))
        put(aux, AUX_T + p, corner(t0, t1))
    put(aux, AUX_V, corner(v0, v1))
    put(aux, AUX_M, corner(m0, m1))
    put(aux, AUX_A, a1)
    put(aux, AUX_B, b1)

    lane = lanes()
    sign = edge_sign()
    sign_top = -sign
    rows = row_ids()
    for pay, source, row, top in (
        (pay_far, pay_far_in, (ROWS - 1) * lat_odd, is_top),
        (pay_near, pay_near_in, (ROWS - 1) * (1 - lat_odd), None),
    ):
        pay[:ROW_P, :] = source[:ROW_P, :]
        pay[ROW_V:ROW_C, :] = source[ROW_V:ROW_C, :]
        for p in range(TPACKS):
            line = jnp.broadcast_to(aux[pl.ds((AUX_F + p) * ROWS + row, 1), :], (ROWS, COLS))
            for f in (2 * p, 2 * p + 1):
                for k in (0, ROWS):
                    shift = COLS - 1 - (lane_base(f, k) + 1)
                    x = sign * pltpu.roll(line, shift, 1, stride=4, stride_axis=0)
                    if top is not None:
                        turned = jnp.where(lane == 0, roll(x, 1, 1), roll(x, -1, 1))
                        x = jnp.where(top, jnp.where(sign != 0.0, turned, 0.0), x)
                    start = ROW_P + f * K + k
                    pay[start : start + ROWS, :] = source[start : start + ROWS, :] + x
        c = aux[pl.ds(AUX_T * ROWS + row, ROWS, stride=ROWS), :]
        if top is not None:
            turned = jnp.where(
                place == 0,
                roll(c, -3, 1),
                jnp.where(place == 1, roll(c, -1, 1), jnp.where(place == 2, roll(c, 1, 1), roll(c, 3, 1))),
            )
            c = jnp.where(top, jnp.where(rows == AUX_V, -turned, turned), c)
        pay[ROW_C : ROW_C + ROWS, :] = c


def column_kernel(tracer, part, aux, own, mix, bottom, full, both, rows_0, rows_7, packs, solve, spread):
    sign = edge_sign()
    for f in range(NT):
        packed = tile(aux, AUX_F + f // 2)
        for k in range(K):
            put(spread, f * K + k, sign * roll(packed, COLS - 1 - (lane_base(f, k) + 1), 1))
    for index in range(TILES):
        x = tile(part, index) + tile(spread, index)
        put(full, index, x)
        put(both, index, tile(tracer, index) + x)
    rows_0[...] = edge(full, 0, TILES, 0)
    rows_7[...] = edge(full, 0, TILES, ROWS - 1)
    for p in range(TPACKS):
        put(packs, p, packed_edges(lambda f, k: tile(full, f * K + k), (2 * p, 2 * p + 1)))
    depth = bottom[...]
    lower = ratio = None
    for k in range(K):
        denom = 1.0
        upper = None
        if k + 1 < K:
            upper = jnp.where(k + 1 < depth, tile(mix, k), 0.0)
            denom = denom + upper
        if k:
            denom = denom + lower + lower * ratio
        inverse = 1.0 / denom
        put(solve, k, 0.5 * inverse)
        if k:
            put(solve, K + k, lower * inverse)
        else:
            put(solve, K + k, jnp.zeros((ROWS, COLS), jnp.float32))
        ratio = -upper * inverse if upper is not None else jnp.zeros((ROWS, COLS), jnp.float32)
        put(solve, 2 * K + k, ratio)
        lower = upper


def last_kernel(
    far, near, tracer, north, mask, coeff, full, both_sums, rows_0, rows_7, packs, solve, own, aux,
    out, edge_1, edge_2, spread,
):
    lat_odd = lax.rem(lax.axis_index("lat"), 2)
    odd = lat_odd == 1
    offset = pl.multiple_of((1 - lat_odd) * PAY_ROWS, ROWS)
    place = lanes() & 3
    at_east = place == 1
    rows = row_ids()
    at_south, at_north = rows == 0, rows == ROWS - 1

    def both(start, size):
        a = far[start : start + size, :]
        b = near[pl.ds(pl.multiple_of(offset + start, ROWS), size), :]
        return jnp.where(odd, a, b), jnp.where(odd, b, a)

    c_n, c_s = both(ROW_C, ROWS)

    def inner_columns(c):
        return jnp.where(at_east, roll(c, 1, 1), roll(c, -1, 1))

    d_n, d_s = inner_columns(c_n), inner_columns(c_s)
    v0, m0 = both_halves(tile(own, TPACKS + 1), 0), both_halves(tile(own, TPACKS), 1)
    v1, m1 = tile(aux, AUX_V), tile(aux, AUX_M)

    def corner_faces(v, m, north_rows, south_rows):
        v_n, v_s = north_rows[AUX_V : AUX_V + 1], south_rows[AUX_V : AUX_V + 1]
        m_n, m_s = north_rows[AUX_M : AUX_M + 1], south_rows[AUX_M : AUX_M + 1]
        an, bn = face(0.5 * (v + v_n), jnp.where(at_north, m * m_n, 0.0))
        as_, bs = face(0.5 * (v_s + v), jnp.where(at_south, m_s * m, 0.0))
        return lambda t, t_n, t_s: (as_ * t_s + bs * t) - (an * t + bn * t_n)

    halo_sum = corner_faces(v1, m1, c_n, c_s)
    own_sum = corner_faces(v0, m0, d_n, d_s)
    a1, b1 = tile(aux, AUX_A), tile(aux, AUX_B)
    sign = edge_sign()
    for p in range(TPACKS):
        f1 = tile(aux, AUX_F + p)
        s1 = tile(aux, AUX_Q + p) + jnp.where(at_east, f1, -f1)
        s1 = s1 + halo_sum(tile(aux, AUX_T + p), c_n[p : p + 1], c_s[p : p + 1])
        s0 = tile(packs, p) + own_sum(tile(own, p), d_n[p : p + 1], d_s[p : p + 1])
        flux = a1 * jnp.where(at_east, s0, s1) + b1 * jnp.where(at_east, s1, s0)
        for f in (2 * p, 2 * p + 1):
            for k in range(K):
                put(spread, f * K + k, sign * roll(flux, COLS - 1 - (lane_base(f, k) + 1), 1))

    v_n, v_s = both(ROW_V, K)
    m_n, m_s = both(ROW_M, K)
    an, bn = face(
        0.5 * (edge(north, 0, K, ROWS - 1) + v_n), edge(mask, 0, K, ROWS - 1).astype(jnp.float32) * m_n
    )
    as_, bs = face(0.5 * (v_s + edge(north, 0, K, 0)), m_s * edge(mask, 0, K, 0).astype(jnp.float32))
    for f in range(NT):
        t_n, t_s = both(ROW_T + f * K, K)
        p_n, p_s = both(ROW_P + f * K, K)
        g_n = an * edge(tracer, f * K, K, ROWS - 1) + bn * t_n
        g_s = as_ * t_s + bs * edge(tracer, f * K, K, 0)
        h_n = an * (rows_7[f * K : (f + 1) * K, :] - g_n) + bn * (p_n + g_n)
        h_s = as_ * (p_s - g_s) + bs * (rows_0[f * K : (f + 1) * K, :] + g_s)
        edge_1[f * K : (f + 1) * K, :] = g_s
        edge_1[TILES + f * K : TILES + (f + 1) * K, :] = -g_n
        edge_2[f * K : (f + 1) * K, :] = g_s + h_s
        edge_2[TILES + f * K : TILES + (f + 1) * K, :] = -(g_n + h_n)

    def outer(ref, index):
        low = ref[index : index + 1, :]
        high = ref[TILES + index : TILES + index + 1, :]
        return jnp.where(at_south, low, jnp.where(at_north, high, 0.0))

    for f in range(NT):
        value = None
        for k in range(K):
            index = f * K + k
            faces = [tile(coeff, i * K + k) for i in range(4)]
            s = tile(full, index) + outer(edge_1, index)
            rhs = (tile(both_sums, index) + inner_sum(s, faces)) + (tile(spread, index) + outer(edge_2, index))
            value_new = rhs * tile(solve, k)
            if k:
                value_new = value_new + tile(solve, K + k) * value
            value = value_new
            put(out, index, value)
        for k in range(K - 2, -1, -1):
            index = f * K + k
            value = tile(out, index) - tile(solve, 2 * K + k) * value
            put(out, index, value)


def call(kernel, outs, scratch_rows, *operands, hbm=False, scratch=(), cost=None):
    vmem = pl.BlockSpec(memory_space=pltpu.VMEM)
    place = pl.BlockSpec(memory_space=pltpu.HBM) if hbm else vmem
    shapes = [
        x if isinstance(x, jax.ShapeDtypeStruct) else jax.ShapeDtypeStruct((x, COLS), jnp.float32)
        for x in outs
    ]
    return pl.pallas_call(
        kernel,
        out_shape=shapes,
        in_specs=[place] * len(operands),
        out_specs=[vmem] * len(shapes),
        scratch_shapes=[pltpu.VMEM((rows, COLS), jnp.float32) for rows in scratch_rows] + list(scratch),
        compiler_params=pltpu.CompilerParams(vmem_limit_bytes=24 * 1024 * 1024),
        cost_estimate=cost,
    )(*operands)


def pairs(lat_count, lon_count):
    def at(i, j):
        return i * lon_count + j % lon_count

    lon_near = [(at(i, j), at(i, j + 1)) for i in range(lat_count) for j in range(0, lon_count, 2)]
    lon_far = [(at(i, j), at(i, j + 1)) for i in range(lat_count) for j in range(1, lon_count, 2)]
    lat_near = [(at(i, j), at(i + 1, j)) for i in range(0, lat_count, 2) for j in range(lon_count)]
    lat_far = [(at(i, j), at(i + 1, j)) for i in range(1, lat_count - 1, 2) for j in range(lon_count)]
    top = lat_count - 1
    lat_far += [(at(top, j), at(top, lon_count - 1 - j)) for j in range(lon_count // 2)]
    return lon_near, lon_far, lat_near, lat_far


def swapped(x, groups):
    return lax.ppermute(x, AXES, [(a, b) for a, b in groups] + [(b, a) for a, b in groups])


def gathered(x, groups):
    both = lax.all_gather(x, AXES, axis_index_groups=[list(g) for g in groups])
    return both.reshape(-1, COLS)


def on_device(tracer, east_vel, north_vel, wet_mask, bottom_level, vertical_mix):
    lon_near, lon_far, lat_near, lat_far = pairs(lax.axis_size("lat"), lax.axis_size("lon"))
    flat = lambda x: x.reshape(-1, COLS)
    fields = [
        pltpu.with_memory_space_constraint(flat(x), pltpu.HBM)
        for x in (tracer, east_vel, north_vel, wet_mask)
    ]
    own, t, u, v, m = call(
        load_kernel,
        [PACK_ROWS] + [jax.ShapeDtypeStruct(x.shape, x.dtype) for x in fields],
        [],
        *fields,
        hbm=True,
        scratch=[pltpu.SemaphoreType.DMA((4,))],
    )
    far = swapped(own, lon_far)
    near = gathered(own, lon_near)
    part, coeff, pay_far, pay_near = call(
        inner_kernel, [TILES * ROWS, 4 * K * ROWS, PAY_ROWS, PAY_ROWS], [], t, u, v, m
    )
    pay_far, pay_near, aux = call(
        outward_kernel, [PAY_ROWS, PAY_ROWS, AUX * ROWS], [], own, near, far, pay_far, pay_near
    )
    far_rows = swapped(pay_far, lat_far)
    near_rows = gathered(pay_near, lat_near)
    full, both, rows_0, rows_7, packs, solve = call(
        column_kernel,
        [TILES * ROWS, TILES * ROWS, TILES, TILES, TPACKS * ROWS, 3 * K * ROWS],
        [TILES * ROWS],
        t, part, aux, own, flat(vertical_mix), bottom_level,
    )
    (out,) = call(
        last_kernel,
        [TILES * ROWS],
        [2 * TILES, 2 * TILES, TILES * ROWS],
        far_rows, near_rows, t, v, m, coeff, full, both, rows_0, rows_7, packs, solve, own, aux,
    )
    return out.reshape(tracer.shape)


def solution(mesh):
    fields = P(None, "lat", "lon")
    tracers = P(None, None, "lat", "lon")
    return jax.shard_map(
        on_device,
        mesh=mesh,
        in_specs=(tracers, fields, fields, fields, P("lat", "lon"), fields),
        out_specs=tracers,
        check_vma=False,
    )
```

```python
import jax
import jax.numpy as jnp
from jax import lax
from jax.experimental import pallas as pl
from jax.experimental.pallas import tpu as pltpu
from jax.sharding import PartitionSpec as P

ROWS = 8
COLS = 128
NT = 6
K = 16
TILES = NT * K
mixing = 0.08
AXES = ("lat", "lon")

FIELDS = NT + 3
PACKS = (FIELDS + 1) // 2
PACK_ROWS = PACKS * ROWS
TPACKS = NT // 2

ROW_T = 0
ROW_P = TILES
ROW_V = 2 * TILES
ROW_M = ROW_V + K
ROW_C = ROW_M + K
PAY_ROWS = ROW_C + ROWS

AUX_T = 0
AUX_V = TPACKS
AUX_M = AUX_V + 1
AUX_F = AUX_M + 1
AUX_Q = AUX_F + TPACKS
AUX_A = AUX_Q + TPACKS
AUX_B = AUX_A + 1
AUX = AUX_B + 1


def roll(x, shift, axis):
    shift %= x.shape[axis]
    return pltpu.roll(x, shift, axis) if shift else x


def lanes(rows=ROWS):
    return lax.broadcasted_iota(jnp.int32, (rows, COLS), 1)


def row_ids():
    return lax.broadcasted_iota(jnp.int32, (ROWS, COLS), 0)


def face(speed, opening):
    return opening * (jnp.maximum(speed, 0.0) + mixing), opening * (jnp.minimum(speed, 0.0) - mixing)


def tile(ref, index):
    return ref[index * ROWS : (index + 1) * ROWS, :]


def put(ref, index, value):
    ref[index * ROWS : (index + 1) * ROWS, :] = value


def edge(ref, start, size, row):
    return ref[pl.ds(start * ROWS + row, size, stride=ROWS), :]


def lane_base(field, k):
    return 64 * (field % 2) + 4 * (K - 1 - k)


def packed_edges(load, fields):
    group = lanes() // 4
    total = jnp.zeros((ROWS, COLS), jnp.float32)
    for field in fields:
        for k in range(K):
            base = lane_base(field, k)
            total = jnp.where(group == base // 4, roll(load(field, k), base - 126, 1), total)
    return total


def row_part(tracer, east, north, mask, row, inward):
    u, m = edge(east, 0, K, row), edge(mask, 0, K, row).astype(jnp.float32)
    v, v_in = edge(north, 0, K, row), edge(north, 0, K, inward)
    m_in = edge(mask, 0, K, inward).astype(jnp.float32)
    ax, bx = face(0.5 * (u + roll(u, -1, 1)), jnp.where(lanes(K) < COLS - 1, m * roll(m, -1, 1), 0.0))
    ay, by = face(0.5 * (v + v_in), m * m_in)
    ts, sums = [], []
    for f in range(NT):
        t, t_in = edge(tracer, f * K, K, row), edge(tracer, f * K, K, inward)
        fe = ax * t + bx * roll(t, -1, 1)
        g = -(ay * t + by * t_in) if inward > row else ay * t_in + by * t
        ts.append(t)
        sums.append(t + ((roll(fe, 1, 1) - fe) + g))
    return ts + sums + [v, m]


def load_kernel(tracer, east, north, mask, pack, t, u, v, m, sems):
    copies = [
        pltpu.make_async_copy(src, dst, sems.at[i])
        for i, (src, dst) in enumerate(((tracer, t), (east, u), (north, v), (mask, m)))
    ]
    for copy in copies:
        copy.start()

    def load(field, k):
        if field < NT:
            return tile(t, field * K + k)
        if field == NT:
            return tile(u, k)
        if field == NT + 1:
            return tile(m, k).astype(jnp.float32)
        return tile(v, k)

    for copy in copies[1:]:
        copy.wait()
    for p in range(TPACKS, PACKS):
        put(pack, p, packed_edges(load, range(2 * p, min(2 * p + 2, FIELDS))))
    copies[0].wait()
    for p in range(TPACKS):
        put(pack, p, packed_edges(load, range(2 * p, 2 * p + 2)))


def rows_kernel(t, u, v, m, pay_far, pay_near):
    odd = lax.rem(lax.axis_index("lat"), 2) == 1
    upper = row_part(t, u, v, m, ROWS - 1, ROWS - 2)
    lower = row_part(t, u, v, m, 0, 1)
    for i, (x, y) in enumerate(zip(upper, lower)):
        pay_far[i * K : (i + 1) * K, :] = jnp.where(odd, x, y)
        pay_near[i * K : (i + 1) * K, :] = jnp.where(odd, y, x)
    for pay in (pay_far, pay_near):
        pay[ROW_C:, :] = jnp.zeros((ROWS, COLS), jnp.float32)

    @pl.when(lax.axis_index("lat") == lax.axis_size("lat") - 1)
    def _():
        x = flipped(pay_far[:ROW_C, :])
        pay_far[:ROW_V, :] = x[:ROW_V]
        pay_far[ROW_V:ROW_M, :] = -x[ROW_V:ROW_M]
        pay_far[ROW_M:ROW_C, :] = x[ROW_M:]


def level_faces(east, north, mask, k):
    u, v, m = tile(east, k), tile(north, k), tile(mask, k).astype(jnp.float32)
    open_x = jnp.where(lanes() < COLS - 1, m * roll(m, -1, 1), 0.0)
    open_y = jnp.where(row_ids() < ROWS - 1, m * roll(m, -1, 0), 0.0)
    ax, bx = face(0.5 * (u + roll(u, -1, 1)), open_x)
    ay, by = face(0.5 * (v + roll(v, -1, 0)), open_y)
    return ax, bx, ay, by


def inner_sum(t, faces):
    ax, bx, ay, by = faces
    fe = ax * t + bx * roll(t, -1, 1)
    gn = ay * t + by * roll(t, -1, 0)
    return (roll(fe, 1, 1) - fe) + (roll(gn, 1, 0) - gn)


def flipped(x):
    lane = lanes(x.shape[0])
    for step in (1, 2, 4, 8, 16, 32, 64):
        x = jnp.where((lane & step) != 0, roll(x, step, 1), roll(x, -step, 1))
    return x


def inner_kernel(tracer, east, north, mask, ahead, part, coeff):
    del ahead
    for k in range(K):
        faces = level_faces(east, north, mask, k)
        for i in range(4):
            put(coeff, i * K + k, faces[i])
        for f in range(NT):
            index = f * K + k
            t = tile(tracer, index)
            put(part, index, t + inner_sum(t, faces))


def both_halves(x, half):
    swapped = roll(x, 64, 1)
    low = lanes() < 64
    return jnp.where(low, x, swapped) if half == 0 else jnp.where(low, swapped, x)


def edge_sign():
    lane = lanes()
    return jnp.where(lane == 0, 1.0, jnp.where(lane == COLS - 1, -1.0, 0.0))


def outward_kernel(own, near, far, far_in, near_in, pay_far, pay_near, aux):
    lat_odd = lax.rem(lax.axis_index("lat"), 2)
    lon_odd = lax.rem(lax.axis_index("lon"), 2)
    is_top = lax.axis_index("lat") == lax.axis_size("lat") - 1
    place = lanes() & 3
    at_east = place == 1
    even = lon_odd == 0
    offset = pl.multiple_of((1 - lon_odd) * PACK_ROWS, ROWS)
    here, one, two = [], [], []
    for p in range(PACKS):
        a = near[pl.ds(pl.multiple_of(offset + p * ROWS, ROWS), ROWS), :]
        b = tile(far, p)
        e = jnp.where(even, a, b)
        w = jnp.where(even, b, a)
        here.append(tile(own, p))
        one.append(jnp.where(at_east, roll(e, -1, 1), roll(w, 1, 1)))
        two.append(jnp.where(at_east, roll(e, -2, 1), roll(w, 2, 1)))
    u0, m0 = both_halves(here[TPACKS], 0), both_halves(here[TPACKS], 1)
    u1, m1 = both_halves(one[TPACKS], 0), both_halves(one[TPACKS], 1)
    u2, m2 = both_halves(two[TPACKS], 0), both_halves(two[TPACKS], 1)
    v0, v1 = both_halves(here[TPACKS + 1], 0), both_halves(one[TPACKS + 1], 0)
    a1, b1 = face(0.5 * (u0 + u1), m0 * m1)
    a2, b2 = face(0.5 * (u1 + u2), m1 * m2)
    inner_y = row_ids() < ROWS - 1
    ay, by = face(0.5 * (v1 + roll(v1, -1, 0)), jnp.where(inner_y, m1 * roll(m1, -1, 0), 0.0))

    def corner(mine, halo):
        return jnp.where(
            place == 0, roll(mine, -1, 1), jnp.where(place == 3, roll(mine, 1, 1), halo)
        )

    for p in range(TPACKS):
        t0, t1, t2 = here[p], one[p], two[p]
        f1 = a1 * jnp.where(at_east, t0, t1) + b1 * jnp.where(at_east, t1, t0)
        f2 = a2 * jnp.where(at_east, t1, t2) + b2 * jnp.where(at_east, t2, t1)
        gn = ay * t1 + by * roll(t1, -1, 0)
        put(aux, AUX_F + p, f1)
        put(aux, AUX_Q + p, t1 + jnp.where(at_east, -f2, f2) + (roll(gn, 1, 0) - gn))
        put(aux, AUX_T + p, corner(t0, t1))
    put(aux, AUX_V, corner(v0, v1))
    put(aux, AUX_M, corner(m0, m1))
    put(aux, AUX_A, a1)
    put(aux, AUX_B, b1)

    del far_in, near_in
    pay_near[ROW_C:, :] = aux[pl.ds(AUX_T * ROWS + (ROWS - 1) * (1 - lat_odd), ROWS, stride=ROWS), :]
    c = aux[pl.ds(AUX_T * ROWS + (ROWS - 1) * lat_odd, ROWS, stride=ROWS), :]
    turned = jnp.where(
        place == 0,
        roll(c, -3, 1),
        jnp.where(place == 1, roll(c, -1, 1), jnp.where(place == 2, roll(c, 1, 1), roll(c, 3, 1))),
    )
    rows = row_ids()
    turned = jnp.where((rows == AUX_V) | (rows >= AUX_F), -turned, turned)
    pay_far[ROW_C:, :] = jnp.where(is_top, turned, c)


def column_kernel(tracer, part, aux, own, mix, bottom, full, both, rows_0, rows_7, packs, solve, spread):
    sign = edge_sign()
    for f in range(NT):
        packed = tile(aux, AUX_F + f // 2)
        for k in range(K):
            put(spread, f * K + k, sign * roll(packed, COLS - 1 - (lane_base(f, k) + 1), 1))
    for index in range(TILES):
        x = tile(part, index) + tile(spread, index)
        put(full, index, x)
        put(both, index, tile(tracer, index) + x)
    rows_0[...] = edge(full, 0, TILES, 0)
    rows_7[...] = edge(full, 0, TILES, ROWS - 1)
    for p in range(TPACKS):
        put(packs, p, packed_edges(lambda f, k: tile(full, f * K + k), (2 * p, 2 * p + 1)))
    depth = bottom[...]
    lower = ratio = None
    for k in range(K):
        denom = 1.0
        upper = None
        if k + 1 < K:
            upper = jnp.where(k + 1 < depth, tile(mix, k), 0.0)
            denom = denom + upper
        if k:
            denom = denom + lower + lower * ratio
        inverse = 1.0 / denom
        put(solve, k, 0.5 * inverse)
        if k:
            put(solve, K + k, lower * inverse)
        else:
            put(solve, K + k, jnp.zeros((ROWS, COLS), jnp.float32))
        ratio = -upper * inverse if upper is not None else jnp.zeros((ROWS, COLS), jnp.float32)
        put(solve, 2 * K + k, ratio)
        lower = upper


def last_kernel(
    far, near, tracer, north, mask, coeff, full, both_sums, rows_0, rows_7, packs, solve, own, aux,
    out, edge_1, edge_2, spread,
):
    lat_odd = lax.rem(lax.axis_index("lat"), 2)
    odd = lat_odd == 1
    offset = pl.multiple_of((1 - lat_odd) * PAY_ROWS, ROWS)
    place = lanes() & 3
    at_east = place == 1
    rows = row_ids()
    at_south, at_north = rows == 0, rows == ROWS - 1

    def both(start, size):
        a = far[start : start + size, :]
        b = near[pl.ds(pl.multiple_of(offset + start, ROWS), size), :]
        return jnp.where(odd, a, b), jnp.where(odd, b, a)

    c_n, c_s = both(ROW_C, ROWS)

    def inner_columns(c):
        return jnp.where(at_east, roll(c, 1, 1), roll(c, -1, 1))

    d_n, d_s = inner_columns(c_n), inner_columns(c_s)
    v0, m0 = both_halves(tile(own, TPACKS + 1), 0), both_halves(tile(own, TPACKS), 1)
    v1, m1 = tile(aux, AUX_V), tile(aux, AUX_M)

    def corner_faces(v, m, north_rows, south_rows):
        v_n, v_s = north_rows[AUX_V : AUX_V + 1], south_rows[AUX_V : AUX_V + 1]
        m_n, m_s = north_rows[AUX_M : AUX_M + 1], south_rows[AUX_M : AUX_M + 1]
        an, bn = face(0.5 * (v + v_n), jnp.where(at_north, m * m_n, 0.0))
        as_, bs = face(0.5 * (v_s + v), jnp.where(at_south, m_s * m, 0.0))
        return lambda t, t_n, t_s: (as_ * t_s + bs * t) - (an * t + bn * t_n)

    halo_sum = corner_faces(v1, m1, c_n, c_s)
    own_sum = corner_faces(v0, m0, d_n, d_s)
    a1, b1 = tile(aux, AUX_A), tile(aux, AUX_B)
    sign = edge_sign()
    for p in range(TPACKS):
        f1 = tile(aux, AUX_F + p)
        s1 = tile(aux, AUX_Q + p) + jnp.where(at_east, f1, -f1)
        s1 = s1 + halo_sum(tile(aux, AUX_T + p), c_n[p : p + 1], c_s[p : p + 1])
        s0 = tile(packs, p) + own_sum(tile(own, p), d_n[p : p + 1], d_s[p : p + 1])
        flux = a1 * jnp.where(at_east, s0, s1) + b1 * jnp.where(at_east, s1, s0)
        for f in (2 * p, 2 * p + 1):
            for k in range(K):
                put(spread, f * K + k, sign * roll(flux, COLS - 1 - (lane_base(f, k) + 1), 1))

    v_n, v_s = both(ROW_V, K)
    m_n, m_s = both(ROW_M, K)
    an, bn = face(
        0.5 * (edge(north, 0, K, ROWS - 1) + v_n), edge(mask, 0, K, ROWS - 1).astype(jnp.float32) * m_n
    )
    as_, bs = face(0.5 * (v_s + edge(north, 0, K, 0)), m_s * edge(mask, 0, K, 0).astype(jnp.float32))

    def edge_flux(c, f):
        line = jnp.broadcast_to(c[AUX_F + f // 2 : AUX_F + f // 2 + 1], (ROWS, COLS))
        return jnp.concatenate(
            [
                sign * pltpu.roll(line, COLS - 1 - (lane_base(f, k) + 1), 1, stride=4, stride_axis=0)
                for k in (0, ROWS)
            ],
            axis=0,
        )

    for f in range(NT):
        t_n, t_s = both(ROW_T + f * K, K)
        p_n, p_s = both(ROW_P + f * K, K)
        p_n, p_s = p_n + edge_flux(c_n, f), p_s + edge_flux(c_s, f)
        g_n = an * edge(tracer, f * K, K, ROWS - 1) + bn * t_n
        g_s = as_ * t_s + bs * edge(tracer, f * K, K, 0)
        h_n = an * (rows_7[f * K : (f + 1) * K, :] - g_n) + bn * (p_n + g_n)
        h_s = as_ * (p_s - g_s) + bs * (rows_0[f * K : (f + 1) * K, :] + g_s)
        edge_1[f * K : (f + 1) * K, :] = g_s
        edge_1[TILES + f * K : TILES + (f + 1) * K, :] = -g_n
        edge_2[f * K : (f + 1) * K, :] = g_s + h_s
        edge_2[TILES + f * K : TILES + (f + 1) * K, :] = -(g_n + h_n)

    def outer(ref, index):
        low = ref[index : index + 1, :]
        high = ref[TILES + index : TILES + index + 1, :]
        return jnp.where(at_south, low, jnp.where(at_north, high, 0.0))

    for f in range(NT):
        value = None
        for k in range(K):
            index = f * K + k
            faces = [tile(coeff, i * K + k) for i in range(4)]
            s = tile(full, index) + outer(edge_1, index)
            rhs = (tile(both_sums, index) + inner_sum(s, faces)) + (tile(spread, index) + outer(edge_2, index))
            value_new = rhs * tile(solve, k)
            if k:
                value_new = value_new + tile(solve, K + k) * value
            value = value_new
            put(out, index, value)
        for k in range(K - 2, -1, -1):
            index = f * K + k
            value = tile(out, index) - tile(solve, 2 * K + k) * value
            put(out, index, value)


def call(kernel, outs, scratch_rows, *operands, hbm=False, scratch=(), alias=None):
    vmem = pl.BlockSpec(memory_space=pltpu.VMEM)
    place = pl.BlockSpec(memory_space=pltpu.HBM) if hbm else vmem
    shapes = [
        x if isinstance(x, jax.ShapeDtypeStruct) else jax.ShapeDtypeStruct((x, COLS), jnp.float32)
        for x in outs
    ]
    return pl.pallas_call(
        kernel,
        out_shape=shapes,
        in_specs=[place] * len(operands),
        out_specs=[vmem] * len(shapes),
        scratch_shapes=[pltpu.VMEM((rows, COLS), jnp.float32) for rows in scratch_rows] + list(scratch),
        compiler_params=pltpu.CompilerParams(vmem_limit_bytes=24 * 1024 * 1024),
        input_output_aliases=alias or {},
    )(*operands)


def pairs(lat_count, lon_count):
    def at(i, j):
        return i * lon_count + j % lon_count

    lon_near = [(at(i, j), at(i, j + 1)) for i in range(lat_count) for j in range(0, lon_count, 2)]
    lon_far = [(at(i, j), at(i, j + 1)) for i in range(lat_count) for j in range(1, lon_count, 2)]
    lat_near = [(at(i, j), at(i + 1, j)) for i in range(0, lat_count, 2) for j in range(lon_count)]
    lat_far = [(at(i, j), at(i + 1, j)) for i in range(1, lat_count - 1, 2) for j in range(lon_count)]
    top = lat_count - 1
    lat_far += [(at(top, j), at(top, lon_count - 1 - j)) for j in range(lon_count // 2)]
    return lon_near, lon_far, lat_near, lat_far


def swapped(x, groups):
    return lax.ppermute(x, AXES, [(a, b) for a, b in groups] + [(b, a) for a, b in groups])


def gathered(x, groups):
    both = lax.all_gather(x, AXES, axis_index_groups=[list(g) for g in groups])
    return both.reshape(-1, COLS)


def on_device(tracer, east_vel, north_vel, wet_mask, bottom_level, vertical_mix):
    lon_near, lon_far, lat_near, lat_far = pairs(lax.axis_size("lat"), lax.axis_size("lon"))
    flat = lambda x: x.reshape(-1, COLS)
    fields = [
        pltpu.with_memory_space_constraint(flat(x), pltpu.HBM)
        for x in (tracer, east_vel, north_vel, wet_mask)
    ]
    own, t, u, v, m = call(
        load_kernel,
        [PACK_ROWS] + [jax.ShapeDtypeStruct(x.shape, x.dtype) for x in fields],
        [],
        *fields,
        hbm=True,
        scratch=[pltpu.SemaphoreType.DMA((4,))],
    )
    far = swapped(own, lon_far)
    pay_far, pay_near = call(rows_kernel, [PAY_ROWS, PAY_ROWS], [], t, u, v, m)
    near = gathered(own, lon_near)
    pay_far, pay_near, aux = call(
        outward_kernel,
        [PAY_ROWS, PAY_ROWS, AUX * ROWS],
        [],
        own, near, far, pay_far, pay_near,
        alias={3: 0, 4: 1},
    )
    far_rows = swapped(pay_far, lat_far)
    part, coeff = call(inner_kernel, [TILES * ROWS, 4 * K * ROWS], [], t, u, v, m, aux)
    near_rows = gathered(pay_near, lat_near)
    full, both, rows_0, rows_7, packs, solve = call(
        column_kernel,
        [TILES * ROWS, TILES * ROWS, TILES, TILES, TPACKS * ROWS, 3 * K * ROWS],
        [TILES * ROWS],
        t, part, aux, own, flat(vertical_mix), bottom_level,
    )
    (out,) = call(
        last_kernel,
        [TILES * ROWS],
        [2 * TILES, 2 * TILES, TILES * ROWS],
        far_rows, near_rows, t, v, m, coeff, full, both, rows_0, rows_7, packs, solve, own, aux,
    )
    return out.reshape(tracer.shape)


def solution(mesh):
    fields = P(None, "lat", "lon")
    tracers = P(None, None, "lat", "lon")
    return jax.shard_map(
        on_device,
        mesh=mesh,
        in_specs=(tracers, fields, fields, fields, P("lat", "lon"), fields),
        out_specs=tracers,
        check_vma=False,
    )
```

```python
import jax
import jax.numpy as jnp
from jax import lax
from jax.experimental import pallas as pl
from jax.experimental.pallas import tpu as pltpu
from jax.sharding import PartitionSpec as P

ROWS = 8
COLS = 128
NT = 6
K = 16
TILES = NT * K
mixing = 0.08
AXES = ("lat", "lon")

FIELDS = NT + 3
PACKS = (FIELDS + 1) // 2
PACK_ROWS = PACKS * ROWS
TPACKS = NT // 2

ROW_T = 0
ROW_P = TILES
ROW_V = 2 * TILES
ROW_M = ROW_V + K
ROW_C = ROW_M + K
PAY_ROWS = ROW_C + ROWS
EARLY_ROWS = PAY_ROWS + ROWS

AUX_T = 0
AUX_V = TPACKS
AUX_M = AUX_V + 1
AUX_F = AUX_M + 1
AUX_Q = AUX_F + TPACKS
AUX_A = AUX_Q + TPACKS
AUX_B = AUX_A + 1
AUX = AUX_B + 1


def roll(x, shift, axis):
    shift %= x.shape[axis]
    return pltpu.roll(x, shift, axis) if shift else x


def lanes(rows=ROWS):
    return lax.broadcasted_iota(jnp.int32, (rows, COLS), 1)


def row_ids():
    return lax.broadcasted_iota(jnp.int32, (ROWS, COLS), 0)


def face(speed, opening):
    return opening * (jnp.maximum(speed, 0.0) + mixing), opening * (jnp.minimum(speed, 0.0) - mixing)


def rows_at(start, size):
    return pl.ds(start if isinstance(start, int) else pl.multiple_of(start, ROWS), size)


def tile(ref, index):
    return ref[rows_at(index * ROWS, ROWS), :]


def put(ref, index, value):
    ref[rows_at(index * ROWS, ROWS), :] = value


def edge(ref, start, size, row):
    return ref[pl.ds(start * ROWS + row, size, stride=ROWS), :]


def repeat(count, body, unroll=1):
    def step(i, carry):
        body(i)
        return carry

    lax.fori_loop(0, count, step, 0, unroll=unroll)


def lane_base(field, k):
    return 64 * (field % 2) + 4 * (K - 1 - k)


def packed_edges(load, fields):
    group = lanes() // 4
    total = jnp.zeros((ROWS, COLS), jnp.float32)
    for field in fields:
        for k in range(K):
            base = lane_base(field, k)
            total = jnp.where(group == base // 4, roll(load(field, k), base - 126, 1), total)
    return total


def row_part(tracer, east, north, mask, row, inward):
    u, m = edge(east, 0, K, row), edge(mask, 0, K, row).astype(jnp.float32)
    v, v_in = edge(north, 0, K, row), edge(north, 0, K, inward)
    m_in = edge(mask, 0, K, inward).astype(jnp.float32)
    ax, bx = face(0.5 * (u + roll(u, -1, 1)), jnp.where(lanes(K) < COLS - 1, m * roll(m, -1, 1), 0.0))
    ay, by = face(0.5 * (v + v_in), m * m_in)
    ts, sums = [], []
    for f in range(NT):
        t, t_in = edge(tracer, f * K, K, row), edge(tracer, f * K, K, inward)
        fe = ax * t + bx * roll(t, -1, 1)
        g = -(ay * t + by * t_in) if inward > row else ay * t_in + by * t
        ts.append(t)
        sums.append(t + ((roll(fe, 1, 1) - fe) + g))
    return ts + sums + [v, m]


def load_kernel(tracer, east, north, mask, pack, t, u, v, m, sems):
    copies = [
        pltpu.make_async_copy(src, dst, sems.at[i])
        for i, (src, dst) in enumerate(((tracer, t), (east, u), (north, v), (mask, m)))
    ]
    for copy in copies:
        copy.start()

    def load(field, k):
        if field < NT:
            return tile(t, field * K + k)
        if field == NT:
            return tile(u, k)
        if field == NT + 1:
            return tile(m, k).astype(jnp.float32)
        return tile(v, k)

    for copy in copies[1:]:
        copy.wait()
    for p in range(TPACKS, PACKS):
        put(pack, p, packed_edges(load, range(2 * p, min(2 * p + 2, FIELDS))))
    copies[0].wait()
    for p in range(TPACKS):
        put(pack, p, packed_edges(load, range(2 * p, 2 * p + 2)))


def rows_kernel(t, u, v, m, pay_far, pay_near):
    odd = lax.rem(lax.axis_index("lat"), 2) == 1
    upper = row_part(t, u, v, m, ROWS - 1, ROWS - 2)
    lower = row_part(t, u, v, m, 0, 1)
    for i, (x, y) in enumerate(zip(upper, lower)):
        pay_far[i * K : (i + 1) * K, :] = jnp.where(odd, x, y)
        pay_near[i * K : (i + 1) * K, :] = jnp.where(odd, y, x)
    for pay in (pay_far, pay_near):
        pay[ROW_C:, :] = jnp.zeros((ROWS, COLS), jnp.float32)

    @pl.when(lax.axis_index("lat") == lax.axis_size("lat") - 1)
    def _():
        x = flipped(pay_far[:ROW_C, :])
        pay_far[:ROW_V, :] = x[:ROW_V]
        pay_far[ROW_V:ROW_M, :] = -x[ROW_V:ROW_M]
        pay_far[ROW_M:ROW_C, :] = x[ROW_M:]


def early_kernel(pay_far, own, early, own_out):
    own_out[...] = own[...]
    early[:ROW_C, :] = pay_far[:ROW_C, :]
    early[ROW_C:, :] = jnp.zeros((EARLY_ROWS - ROW_C, COLS), jnp.float32)


def level_faces(east, north, mask, k):
    u, v, m = tile(east, k), tile(north, k), tile(mask, k).astype(jnp.float32)
    open_x = jnp.where(lanes() < COLS - 1, m * roll(m, -1, 1), 0.0)
    open_y = jnp.where(row_ids() < ROWS - 1, m * roll(m, -1, 0), 0.0)
    ax, bx = face(0.5 * (u + roll(u, -1, 1)), open_x)
    ay, by = face(0.5 * (v + roll(v, -1, 0)), open_y)
    middle = (roll(bx, 1, 1) - ax) + (roll(by, 1, 0) - ay)
    return middle, roll(ax, 1, 1), -bx, roll(ay, 1, 0), -by


def inner_sum(t, faces):
    middle, west, east, south, north = faces
    sides = (west * roll(t, 1, 1) + east * roll(t, -1, 1)) + (south * roll(t, 1, 0) + north * roll(t, -1, 0))
    return middle * t + sides


def flipped(x):
    lane = lanes(x.shape[0])
    for step in (1, 2, 4, 8, 16, 32, 64):
        x = jnp.where((lane & step) != 0, roll(x, step, 1), roll(x, -step, 1))
    return x


def both_halves(x, half):
    swapped = roll(x, 64, 1)
    low = lanes() < 64
    return jnp.where(low, x, swapped) if half == 0 else jnp.where(low, swapped, x)


def edge_sign():
    lane = lanes()
    return jnp.where(lane == 0, 1.0, jnp.where(lane == COLS - 1, -1.0, 0.0))


def outward_kernel(
    own, near, far, far_in, near_in, tracer, east, north, mask, mix, bottom,
    pay_far, pay_near, aux, corner_far, *refs,
):
    lat_odd = lax.rem(lax.axis_index("lat"), 2)
    lon_odd = lax.rem(lax.axis_index("lon"), 2)
    is_top = lax.axis_index("lat") == lax.axis_size("lat") - 1
    place = lanes() & 3
    at_east = place == 1
    even = lon_odd == 0
    offset = pl.multiple_of((1 - lon_odd) * PACK_ROWS, ROWS)
    here, one, two = [], [], []
    for p in range(PACKS):
        a = near[pl.ds(pl.multiple_of(offset + p * ROWS, ROWS), ROWS), :]
        b = tile(far, p)
        e = jnp.where(even, a, b)
        w = jnp.where(even, b, a)
        here.append(tile(own, p))
        one.append(jnp.where(at_east, roll(e, -1, 1), roll(w, 1, 1)))
        two.append(jnp.where(at_east, roll(e, -2, 1), roll(w, 2, 1)))
    u0, m0 = both_halves(here[TPACKS], 0), both_halves(here[TPACKS], 1)
    u1, m1 = both_halves(one[TPACKS], 0), both_halves(one[TPACKS], 1)
    u2, m2 = both_halves(two[TPACKS], 0), both_halves(two[TPACKS], 1)
    v0, v1 = both_halves(here[TPACKS + 1], 0), both_halves(one[TPACKS + 1], 0)
    a1, b1 = face(0.5 * (u0 + u1), m0 * m1)
    a2, b2 = face(0.5 * (u1 + u2), m1 * m2)
    inner_y = row_ids() < ROWS - 1
    ay, by = face(0.5 * (v1 + roll(v1, -1, 0)), jnp.where(inner_y, m1 * roll(m1, -1, 0), 0.0))

    def corner(mine, halo):
        return jnp.where(
            place == 0, roll(mine, -1, 1), jnp.where(place == 3, roll(mine, 1, 1), halo)
        )

    for p in range(TPACKS):
        t0, t1, t2 = here[p], one[p], two[p]
        f1 = a1 * jnp.where(at_east, t0, t1) + b1 * jnp.where(at_east, t1, t0)
        f2 = a2 * jnp.where(at_east, t1, t2) + b2 * jnp.where(at_east, t2, t1)
        gn = ay * t1 + by * roll(t1, -1, 0)
        put(aux, AUX_F + p, f1)
        put(aux, AUX_Q + p, t1 + jnp.where(at_east, -f2, f2) + (roll(gn, 1, 0) - gn))
        put(aux, AUX_T + p, corner(t0, t1))
    put(aux, AUX_V, corner(v0, v1))
    put(aux, AUX_M, corner(m0, m1))
    put(aux, AUX_A, a1)
    put(aux, AUX_B, b1)

    del far_in, near_in
    pay_near[ROW_C:, :] = aux[pl.ds(AUX_T * ROWS + (ROWS - 1) * (1 - lat_odd), ROWS, stride=ROWS), :]
    c = aux[pl.ds(AUX_T * ROWS + (ROWS - 1) * lat_odd, ROWS, stride=ROWS), :]
    turned = jnp.where(
        place == 0,
        roll(c, -3, 1),
        jnp.where(place == 1, roll(c, -1, 1), jnp.where(place == 2, roll(c, 1, 1), roll(c, 3, 1))),
    )
    rows = row_ids()
    turned = jnp.where((rows == AUX_V) | (rows >= AUX_F), -turned, turned)
    c = jnp.where(is_top, turned, c)
    pay_far[ROW_C:, :] = c
    corner_far[...] = c

    @pl.when(ahead_of_partner())
    def _():
        columns(tracer, east, north, mask, mix, bottom, aux, *refs)


def spread_out(spread, packed, sign):
    def pair(p):
        x = packed(p)
        for f in (0, 1):
            for k in range(K):
                put(spread, (2 * p + f) * K + k, sign * roll(x, COLS - 1 - (lane_base(f, k) + 1), 1))

    for p in range(TPACKS):
        pair(p)


def columns(tracer, east, north, mask, mix, bottom, aux, full, both, rows_0, rows_7, packs, solve, coeff, spread):
    sign = edge_sign()
    spread_out(spread, lambda p: tile(aux, AUX_F + p), sign)

    def level(k):
        faces = level_faces(east, north, mask, k)
        for i in range(5):
            put(coeff, i * K + k, faces[i])
        for f in range(NT):
            index = f * K + k
            t = tile(tracer, index)
            x = t + (inner_sum(t, faces) + tile(spread, index))
            put(full, index, x)
            put(both, index, t + x)

    repeat(K, level, unroll=8)
    rows_0[...] = edge(full, 0, TILES, 0)
    rows_7[...] = edge(full, 0, TILES, ROWS - 1)
    for p in range(TPACKS):
        put(packs, p, packed_edges(lambda f, k: tile(full, f * K + k), (2 * p, 2 * p + 1)))
    depth = bottom[...]
    lower = ratio = None
    for k in range(K):
        denom = 1.0
        upper = None
        if k + 1 < K:
            upper = jnp.where(k + 1 < depth, tile(mix, k), 0.0)
            denom = denom + upper
        if k:
            denom = denom + lower + lower * ratio
        inverse = 1.0 / denom
        put(solve, k, 0.5 * inverse)
        if k:
            put(solve, K + k, lower * inverse)
        else:
            put(solve, K + k, jnp.zeros((ROWS, COLS), jnp.float32))
        ratio = -upper * inverse if upper is not None else jnp.zeros((ROWS, COLS), jnp.float32)
        put(solve, 2 * K + k, ratio)
        lower = upper


COLUMN_ROWS = [TILES * ROWS, TILES * ROWS, TILES, TILES, TPACKS * ROWS, 3 * K * ROWS, 5 * K * ROWS]


def ahead_of_partner():
    lat, count = lax.axis_index("lat"), lax.axis_size("lat")
    place = lax.rem(lat, 4)
    waits = ((place >= 2) & (lat < count // 2)) | ((place < 2) & (lat >= count // 2))
    return waits & (lax.rem(lax.axis_index("lon"), 8) < 2)


def column_kernel(tracer, east, north, mask, mix, bottom, aux, *refs):
    count = len(COLUMN_ROWS)

    @pl.when(jnp.logical_not(ahead_of_partner()))
    def _():
        columns(tracer, east, north, mask, mix, bottom, aux, *refs[count:])


def last_kernel(
    early, corner, far, near, tracer, north, mask, coeff, full, both_sums, rows_0, rows_7, packs, solve, own, aux,
    result, edge_1, edge_2, spread, out, line_1, line_2, line_3, line_4, sems,
):
    lines_refs = (line_1, line_2, line_3, line_4)
    lat_odd = lax.rem(lax.axis_index("lat"), 2)
    odd = lat_odd == 1
    offset = pl.multiple_of((1 - lat_odd) * PAY_ROWS, ROWS)
    place = lanes() & 3
    at_east = place == 1
    rows = row_ids()
    at_south, at_north = rows == 0, rows == ROWS - 1

    is_early = early_lon(lax.axis_index("lon"))

    def both(start, size, step=0):
        place = rows_at(start + step, size)
        first = early[place, :] if start < ROW_C else corner[...]
        a = jnp.where(is_early, first, far[place, :])
        b = near[rows_at(offset + start + step, size), :]
        return jnp.where(odd, a, b), jnp.where(odd, b, a)

    c_n, c_s = both(ROW_C, ROWS)

    def inner_columns(c):
        return jnp.where(at_east, roll(c, 1, 1), roll(c, -1, 1))

    d_n, d_s = inner_columns(c_n), inner_columns(c_s)
    v0, m0 = both_halves(tile(own, TPACKS + 1), 0), both_halves(tile(own, TPACKS), 1)
    v1, m1 = tile(aux, AUX_V), tile(aux, AUX_M)

    def corner_faces(v, m, north_rows, south_rows):
        v_n, v_s = north_rows[AUX_V : AUX_V + 1], south_rows[AUX_V : AUX_V + 1]
        m_n, m_s = north_rows[AUX_M : AUX_M + 1], south_rows[AUX_M : AUX_M + 1]
        an, bn = face(0.5 * (v + v_n), jnp.where(at_north, m * m_n, 0.0))
        as_, bs = face(0.5 * (v_s + v), jnp.where(at_south, m_s * m, 0.0))
        return lambda t, t_n, t_s: (as_ * t_s + bs * t) - (an * t + bn * t_n)

    halo_sum = corner_faces(v1, m1, c_n, c_s)
    own_sum = corner_faces(v0, m0, d_n, d_s)
    a1, b1 = tile(aux, AUX_A), tile(aux, AUX_B)
    sign = edge_sign()

    def corner_row(c, ref, p):
        del c
        return ref[pl.ds(p, 1), :]

    for c, ref in zip((c_n, c_s, d_n, d_s), lines_refs):
        ref[...] = c

    def flux_of(p):
        lines = [corner_row(c, ref, p) for c, ref in zip((c_n, c_s, d_n, d_s), lines_refs)]
        f1 = tile(aux, AUX_F + p)
        s1 = tile(aux, AUX_Q + p) + jnp.where(at_east, f1, -f1)
        s1 = s1 + halo_sum(tile(aux, AUX_T + p), lines[0], lines[1])
        s0 = tile(packs, p) + own_sum(tile(own, p), lines[2], lines[3])
        return a1 * jnp.where(at_east, s0, s1) + b1 * jnp.where(at_east, s1, s0)

    spread_out(spread, flux_of, sign)

    v_n, v_s = both(ROW_V, K)
    m_n, m_s = both(ROW_M, K)
    an, bn = face(
        0.5 * (edge(north, 0, K, ROWS - 1) + v_n), edge(mask, 0, K, ROWS - 1).astype(jnp.float32) * m_n
    )
    as_, bs = face(0.5 * (v_s + edge(north, 0, K, 0)), m_s * edge(mask, 0, K, 0).astype(jnp.float32))

    def edge_flux(ref, p, f):
        line = jnp.broadcast_to(ref[pl.ds(AUX_F + p, 1), :], (ROWS, COLS))
        return jnp.concatenate(
            [
                sign * pltpu.roll(line, COLS - 1 - (lane_base(f, k) + 1), 1, stride=4, stride_axis=0)
                for k in (0, ROWS)
            ],
            axis=0,
        )

    def edge_pair(p):
        for half in (0, 1):
            f = 2 * p + half
            t_n, t_s = both(ROW_T, K, f * K)
            p_n, p_s = both(ROW_P, K, f * K)
            p_n = p_n + edge_flux(lines_refs[0], p, half)
            p_s = p_s + edge_flux(lines_refs[1], p, half)
            g_n = an * edge(tracer, f * K, K, ROWS - 1) + bn * t_n
            g_s = as_ * t_s + bs * edge(tracer, f * K, K, 0)
            here = rows_at(f * K, K)
            there = rows_at(TILES + f * K, K)
            h_n = an * (rows_7[here, :] - g_n) + bn * (p_n + g_n)
            h_s = as_ * (p_s - g_s) + bs * (rows_0[here, :] + g_s)
            edge_1[here, :] = g_s
            edge_1[there, :] = -g_n
            edge_2[here, :] = g_s + h_s
            edge_2[there, :] = -(g_n + h_n)

    for p in range(TPACKS):
        edge_pair(p)

    def outer(ref, index):
        low = ref[pl.ds(index, 1), :]
        high = ref[pl.ds(TILES + index, 1), :]
        return jnp.where(at_south, low, jnp.where(at_north, high, 0.0))


    def copy_of(f):
        place = rows_at(f * K * ROWS, K * ROWS)
        return pltpu.make_async_copy(out.at[place, :], result.at[place, :], sems.at[f])

    def tracer_columns(f):
        value = None
        for k in range(K):
            index = f * K + k
            faces = [tile(coeff, i * K + k) for i in range(5)]
            s = tile(full, index) + outer(edge_1, index)
            rhs = (tile(both_sums, index) + inner_sum(s, faces)) + (tile(spread, index) + outer(edge_2, index))
            value_new = rhs * tile(solve, k)
            if k:
                value_new = value_new + tile(solve, K + k) * value
            value = value_new
            put(out, index, value)
        for k in range(K - 2, -1, -1):
            index = f * K + k
            value = tile(out, index) - tile(solve, 2 * K + k) * value
            put(out, index, value)
        copy_of(f).start()

    for f in range(NT):
        tracer_columns(f)
    for f in range(NT):
        copy_of(f).wait()


def early_lon(lon):
    place = lax.rem(lon, 8) if not isinstance(lon, int) else lon % 8
    return (place >= 2) & (place < 6)


def call(kernel, outs, scratch_rows, *operands, hbm=False, hbm_out=False, scratch=(), alias=None):
    vmem = pl.BlockSpec(memory_space=pltpu.VMEM)
    in_hbm = pl.BlockSpec(memory_space=pltpu.HBM)
    shapes = [
        x if isinstance(x, jax.ShapeDtypeStruct) else jax.ShapeDtypeStruct((x, COLS), jnp.float32)
        for x in outs
    ]
    return pl.pallas_call(
        kernel,
        out_shape=shapes,
        in_specs=[in_hbm if hbm else vmem] * len(operands),
        out_specs=[in_hbm if hbm_out else vmem] * len(shapes),
        scratch_shapes=[pltpu.VMEM((rows, COLS), jnp.float32) for rows in scratch_rows] + list(scratch),
        compiler_params=pltpu.CompilerParams(vmem_limit_bytes=24 * 1024 * 1024),
        input_output_aliases=alias or {},
    )(*operands)


def pairs(lat_count, lon_count):
    def at(i, j):
        return i * lon_count + j % lon_count

    lon_near = [(at(i, j), at(i, j + 1)) for i in range(lat_count) for j in range(0, lon_count, 2)]
    lon_far = [(at(i, j), at(i, j + 1)) for i in range(lat_count) for j in range(1, lon_count, 2)]
    lat_near = [(at(i, j), at(i + 1, j)) for i in range(0, lat_count, 2) for j in range(lon_count)]
    lat_far = [(at(i, j), at(i + 1, j)) for i in range(1, lat_count - 1, 2) for j in range(lon_count)]
    top = lat_count - 1
    lat_far += [(at(top, j), at(top, lon_count - 1 - j)) for j in range(lon_count // 2)]
    return lon_near, lon_far, lat_near, lat_far


def swapped(x, groups):
    return lax.ppermute(x, AXES, [(a, b) for a, b in groups] + [(b, a) for a, b in groups])


def gathered(x, groups):
    both = lax.all_gather(x, AXES, axis_index_groups=[list(g) for g in groups])
    return both.reshape(-1, COLS)


def on_device(tracer, east_vel, north_vel, wet_mask, bottom_level, vertical_mix):
    lon_near, lon_far, lat_near, lat_far = pairs(lax.axis_size("lat"), lax.axis_size("lon"))
    flat = lambda x: x.reshape(-1, COLS)
    fields = [
        pltpu.with_memory_space_constraint(flat(x), pltpu.HBM)
        for x in (tracer, east_vel, north_vel, wet_mask)
    ]
    own, t, u, v, m = call(
        load_kernel,
        [PACK_ROWS] + [jax.ShapeDtypeStruct(x.shape, x.dtype) for x in fields],
        [],
        *fields,
        hbm=True,
        scratch=[pltpu.SemaphoreType.DMA((4,))],
    )
    far = swapped(own, lon_far)
    pay_far, pay_near = call(rows_kernel, [PAY_ROWS, PAY_ROWS], [], t, u, v, m)
    lon_count = lax.axis_size("lon")
    lat_early = [(a, b) for a, b in lat_far if early_lon(a % lon_count)]
    lat_late = [(a, b) for a, b in lat_far if not early_lon(a % lon_count)]
    early, own_again = call(early_kernel, [EARLY_ROWS, PACK_ROWS], [], pay_far, own)
    early_rows = swapped(early, lat_early)
    near = gathered(own_again, lon_near)
    vertical = flat(vertical_mix)
    pay_far, pay_near, aux, corner, *ready = call(
        outward_kernel,
        [PAY_ROWS, PAY_ROWS, AUX * ROWS, ROWS] + COLUMN_ROWS,
        [TILES * ROWS],
        own, near, far, pay_far, pay_near, t, u, v, m, vertical, bottom_level,
        alias={3: 0, 4: 1},
    )
    far_rows = swapped(pay_far, lat_late)
    corner_rows = swapped(corner, lat_early)
    near_rows = gathered(pay_near, lat_near)
    full, both, rows_0, rows_7, packs, solve, coeff = call(
        column_kernel,
        COLUMN_ROWS,
        [TILES * ROWS],
        t, u, v, m, vertical, bottom_level, aux, *ready,
        alias={7 + i: i for i in range(len(COLUMN_ROWS))},
    )
    (out,) = call(
        last_kernel,
        [TILES * ROWS],
        [2 * TILES, 2 * TILES, TILES * ROWS, TILES * ROWS] + [ROWS] * 4,
        early_rows, corner_rows, far_rows, near_rows, t, v, m, coeff, full, both, rows_0, rows_7, packs, solve, own, aux,
        scratch=[pltpu.SemaphoreType.DMA((NT,))],
        hbm_out=True,
    )
    return out.reshape(tracer.shape)


def solution(mesh):
    fields = P(None, "lat", "lon")
    tracers = P(None, None, "lat", "lon")
    return jax.shard_map(
        on_device,
        mesh=mesh,
        in_specs=(tracers, fields, fields, fields, P("lat", "lon"), fields),
        out_specs=tracers,
        check_vma=False,
    )
```

```python
import jax
import jax.numpy as jnp
from jax import lax
from jax.experimental import pallas as pl
from jax.experimental.pallas import tpu as pltpu
from jax.sharding import PartitionSpec as P

ROWS = 8
COLS = 128
NT = 6
K = 16
TILES = NT * K
mixing = 0.08
AXES = ("lat", "lon")

FIELDS = NT + 3
PACKS = (FIELDS + 1) // 2
PACK_ROWS = PACKS * ROWS
TPACKS = NT // 2

ROW_T = 0
ROW_P = TILES
ROW_V = 2 * TILES
ROW_M = ROW_V + K
ROW_C = ROW_M + K
PAY_ROWS = ROW_C + ROWS
EARLY_ROWS = PAY_ROWS + ROWS

AUX_T = 0
AUX_V = TPACKS
AUX_M = AUX_V + 1
AUX_F = AUX_M + 1
AUX_Q = AUX_F + TPACKS
AUX_A = AUX_Q + TPACKS
AUX_B = AUX_A + 1
AUX = AUX_B + 1


def roll(x, shift, axis):
    shift %= x.shape[axis]
    return pltpu.roll(x, shift, axis) if shift else x


def lanes(rows=ROWS):
    return lax.broadcasted_iota(jnp.int32, (rows, COLS), 1)


def row_ids():
    return lax.broadcasted_iota(jnp.int32, (ROWS, COLS), 0)


def face(speed, opening):
    return opening * (jnp.maximum(speed, 0.0) + mixing), opening * (jnp.minimum(speed, 0.0) - mixing)


def rows_at(start, size):
    return pl.ds(start if isinstance(start, int) else pl.multiple_of(start, ROWS), size)


def tile(ref, index):
    return ref[rows_at(index * ROWS, ROWS), :]


def put(ref, index, value):
    ref[rows_at(index * ROWS, ROWS), :] = value


def edge(ref, start, size, row):
    return ref[pl.ds(start * ROWS + row, size, stride=ROWS), :]


def repeat(count, body, unroll=1):
    def step(i, carry):
        body(i)
        return carry

    lax.fori_loop(0, count, step, 0, unroll=unroll)


def lane_base(field, k):
    return 64 * (field % 2) + 4 * (K - 1 - k)


def packed_edges(load, fields):
    group = lanes() // 4
    total = jnp.zeros((ROWS, COLS), jnp.float32)
    for field in fields:
        for k in range(K):
            base = lane_base(field, k)
            total = jnp.where(group == base // 4, roll(load(field, k), base - 126, 1), total)
    return total


def row_part(tracer, east, north, mask, row, inward):
    u, m = edge(east, 0, K, row), edge(mask, 0, K, row).astype(jnp.float32)
    v, v_in = edge(north, 0, K, row), edge(north, 0, K, inward)
    m_in = edge(mask, 0, K, inward).astype(jnp.float32)
    ax, bx = face(0.5 * (u + roll(u, -1, 1)), jnp.where(lanes(K) < COLS - 1, m * roll(m, -1, 1), 0.0))
    ay, by = face(0.5 * (v + v_in), m * m_in)
    ts, sums = [], []
    for f in range(NT):
        t, t_in = edge(tracer, f * K, K, row), edge(tracer, f * K, K, inward)
        fe = ax * t + bx * roll(t, -1, 1)
        g = -(ay * t + by * t_in) if inward > row else ay * t_in + by * t
        ts.append(t)
        sums.append(t + ((roll(fe, 1, 1) - fe) + g))
    return ts + sums + [v, m]


def load_kernel(tracer, east, north, mask, mix, bottom, pack, t, u, v, m, vertical, depth, sems):
    copies = [
        pltpu.make_async_copy(src, dst, sems.at[i])
        for i, (src, dst) in enumerate(
            ((tracer, t), (east, u), (north, v), (mask, m), (mix, vertical), (bottom, depth))
        )
    ]
    for copy in copies:
        copy.start()

    def load(field, k):
        if field < NT:
            return tile(t, field * K + k)
        if field == NT:
            return tile(u, k)
        if field == NT + 1:
            return tile(m, k).astype(jnp.float32)
        return tile(v, k)

    for copy in copies[1:4]:
        copy.wait()
    for p in range(TPACKS, PACKS):
        put(pack, p, packed_edges(load, range(2 * p, min(2 * p + 2, FIELDS))))
    copies[0].wait()
    for p in range(TPACKS):
        put(pack, p, packed_edges(load, range(2 * p, 2 * p + 2)))
    for copy in copies[4:]:
        copy.wait()


def rows_kernel(t, u, v, m, own, pay_far, pay_near, early, own_out):
    odd = lax.rem(lax.axis_index("lat"), 2) == 1
    upper = row_part(t, u, v, m, ROWS - 1, ROWS - 2)
    lower = row_part(t, u, v, m, 0, 1)
    for i, (x, y) in enumerate(zip(upper, lower)):
        pay_far[i * K : (i + 1) * K, :] = jnp.where(odd, x, y)
        pay_near[i * K : (i + 1) * K, :] = jnp.where(odd, y, x)
    for pay in (pay_far, pay_near):
        pay[ROW_C:, :] = jnp.zeros((ROWS, COLS), jnp.float32)

    @pl.when(lax.axis_index("lat") == lax.axis_size("lat") - 1)
    def _():
        x = flipped(pay_far[:ROW_C, :])
        pay_far[:ROW_V, :] = x[:ROW_V]
        pay_far[ROW_V:ROW_M, :] = -x[ROW_V:ROW_M]
        pay_far[ROW_M:ROW_C, :] = x[ROW_M:]

    early[:ROW_C, :] = pay_far[:ROW_C, :]
    early[ROW_C:, :] = jnp.zeros((EARLY_ROWS - ROW_C, COLS), jnp.float32)
    own_out[...] = own[...]


def level_faces(east, north, mask, k):
    u, v, m = tile(east, k), tile(north, k), tile(mask, k).astype(jnp.float32)
    open_x = jnp.where(lanes() < COLS - 1, m * roll(m, -1, 1), 0.0)
    open_y = jnp.where(row_ids() < ROWS - 1, m * roll(m, -1, 0), 0.0)
    ax, bx = face(0.5 * (u + roll(u, -1, 1)), open_x)
    ay, by = face(0.5 * (v + roll(v, -1, 0)), open_y)
    middle = (roll(bx, 1, 1) - ax) + (roll(by, 1, 0) - ay)
    return middle, roll(ax, 1, 1), -bx, roll(ay, 1, 0), -by


def inner_sum(t, faces):
    middle, west, east, south, north = faces
    sides = (west * roll(t, 1, 1) + east * roll(t, -1, 1)) + (south * roll(t, 1, 0) + north * roll(t, -1, 0))
    return middle * t + sides


def flipped(x):
    lane = lanes(x.shape[0])
    for step in (1, 2, 4, 8, 16, 32, 64):
        x = jnp.where((lane & step) != 0, roll(x, step, 1), roll(x, -step, 1))
    return x


def both_halves(x, half):
    swapped = roll(x, 64, 1)
    low = lanes() < 64
    return jnp.where(low, x, swapped) if half == 0 else jnp.where(low, swapped, x)


def edge_sign():
    lane = lanes()
    return jnp.where(lane == 0, 1.0, jnp.where(lane == COLS - 1, -1.0, 0.0))


def outward_kernel(
    own, near, far, far_in, near_in, tracer, east, north, mask, mix, bottom,
    pay_far, pay_near, aux, corner_far, *refs,
):
    lat_odd = lax.rem(lax.axis_index("lat"), 2)
    lon_odd = lax.rem(lax.axis_index("lon"), 2)
    is_top = lax.axis_index("lat") == lax.axis_size("lat") - 1
    place = lanes() & 3
    at_east = place == 1
    even = lon_odd == 0
    offset = pl.multiple_of((1 - lon_odd) * PACK_ROWS, ROWS)
    here, one, two = [], [], []
    for p in range(PACKS):
        a = near[pl.ds(pl.multiple_of(offset + p * ROWS, ROWS), ROWS), :]
        b = tile(far, p)
        e = jnp.where(even, a, b)
        w = jnp.where(even, b, a)
        here.append(tile(own, p))
        one.append(jnp.where(at_east, roll(e, -1, 1), roll(w, 1, 1)))
        two.append(jnp.where(at_east, roll(e, -2, 1), roll(w, 2, 1)))
    u0, m0 = both_halves(here[TPACKS], 0), both_halves(here[TPACKS], 1)
    u1, m1 = both_halves(one[TPACKS], 0), both_halves(one[TPACKS], 1)
    u2, m2 = both_halves(two[TPACKS], 0), both_halves(two[TPACKS], 1)
    v0, v1 = both_halves(here[TPACKS + 1], 0), both_halves(one[TPACKS + 1], 0)
    a1, b1 = face(0.5 * (u0 + u1), m0 * m1)
    a2, b2 = face(0.5 * (u1 + u2), m1 * m2)
    inner_y = row_ids() < ROWS - 1
    ay, by = face(0.5 * (v1 + roll(v1, -1, 0)), jnp.where(inner_y, m1 * roll(m1, -1, 0), 0.0))

    def corner(mine, halo):
        return jnp.where(
            place == 0, roll(mine, -1, 1), jnp.where(place == 3, roll(mine, 1, 1), halo)
        )

    for p in range(TPACKS):
        t0, t1, t2 = here[p], one[p], two[p]
        f1 = a1 * jnp.where(at_east, t0, t1) + b1 * jnp.where(at_east, t1, t0)
        f2 = a2 * jnp.where(at_east, t1, t2) + b2 * jnp.where(at_east, t2, t1)
        gn = ay * t1 + by * roll(t1, -1, 0)
        put(aux, AUX_F + p, f1)
        put(aux, AUX_Q + p, t1 + jnp.where(at_east, -f2, f2) + (roll(gn, 1, 0) - gn))
        put(aux, AUX_T + p, corner(t0, t1))
    put(aux, AUX_V, corner(v0, v1))
    put(aux, AUX_M, corner(m0, m1))
    put(aux, AUX_A, a1)
    put(aux, AUX_B, b1)

    del far_in, near_in
    pay_near[ROW_C:, :] = aux[pl.ds(AUX_T * ROWS + (ROWS - 1) * (1 - lat_odd), ROWS, stride=ROWS), :]
    c = aux[pl.ds(AUX_T * ROWS + (ROWS - 1) * lat_odd, ROWS, stride=ROWS), :]
    turned = jnp.where(
        place == 0,
        roll(c, -3, 1),
        jnp.where(place == 1, roll(c, -1, 1), jnp.where(place == 2, roll(c, 1, 1), roll(c, 3, 1))),
    )
    rows = row_ids()
    turned = jnp.where((rows == AUX_V) | (rows >= AUX_F), -turned, turned)
    c = jnp.where(is_top, turned, c)
    pay_far[ROW_C:, :] = c
    corner_far[...] = c

    @pl.when(ahead_of_partner())
    def _():
        columns(tracer, east, north, mask, mix, bottom, aux, *refs)


def spread_out(spread, packed, sign):
    def pair(p):
        x = packed(p)
        for f in (0, 1):
            for k in range(K):
                put(spread, (2 * p + f) * K + k, sign * roll(x, COLS - 1 - (lane_base(f, k) + 1), 1))

    for p in range(TPACKS):
        pair(p)


def columns(tracer, east, north, mask, mix, bottom, aux, full, both, packs, solve, coeff, spread):
    sign = edge_sign()
    spread_out(spread, lambda p: tile(aux, AUX_F + p), sign)

    def level(k):
        faces = level_faces(east, north, mask, k)
        for i in range(5):
            put(coeff, i * K + k, faces[i])
        for f in range(NT):
            index = f * K + k
            t = tile(tracer, index)
            x = t + (inner_sum(t, faces) + tile(spread, index))
            put(full, index, x)
            put(both, index, t + x)

    repeat(K, level, unroll=8)
    for p in range(TPACKS):
        put(packs, p, packed_edges(lambda f, k: tile(full, f * K + k), (2 * p, 2 * p + 1)))
    depth = bottom[...]
    lower = ratio = None
    for k in range(K):
        denom = 1.0
        upper = None
        if k + 1 < K:
            upper = jnp.where(k + 1 < depth, tile(mix, k), 0.0)
            denom = denom + upper
        if k:
            denom = denom + lower + lower * ratio
        inverse = 1.0 / denom
        put(solve, k, 0.5 * inverse)
        if k:
            put(solve, K + k, lower * inverse)
        else:
            put(solve, K + k, jnp.zeros((ROWS, COLS), jnp.float32))
        ratio = -upper * inverse if upper is not None else jnp.zeros((ROWS, COLS), jnp.float32)
        put(solve, 2 * K + k, ratio)
        lower = upper


COLUMN_ROWS = [TILES * ROWS, TILES * ROWS, TPACKS * ROWS, 3 * K * ROWS, 5 * K * ROWS]


def ahead_of_partner():
    lat, count = lax.axis_index("lat"), lax.axis_size("lat")
    place = lax.rem(lat, 4)
    waits = ((place >= 2) & (lat < count // 2)) | ((place < 2) & (lat >= count // 2))
    return waits & (lax.rem(lax.axis_index("lon"), 8) < 2)


def column_kernel(tracer, east, north, mask, mix, bottom, aux, *refs):
    count = len(COLUMN_ROWS)

    @pl.when(jnp.logical_not(ahead_of_partner()))
    def _():
        columns(tracer, east, north, mask, mix, bottom, aux, *refs[count:])


def last_kernel(
    early, corner, far, near, tracer, north, mask, coeff, full_in, sums_in, packs, solve, own, aux,
    result, full, sums, spread, out, line_1, line_2, line_3, line_4, sems,
):
    del full_in, sums_in
    lines_refs = (line_1, line_2, line_3, line_4)
    lat_odd = lax.rem(lax.axis_index("lat"), 2)
    odd = lat_odd == 1
    offset = pl.multiple_of((1 - lat_odd) * PAY_ROWS, ROWS)
    place = lanes() & 3
    at_east = place == 1
    rows = row_ids()
    at_south, at_north = rows == 0, rows == ROWS - 1

    is_early = early_far(lax.axis_index("lat"), lax.axis_index("lon"), lax.axis_size("lat"), lax.axis_size("lon"))

    def both(start, size, step=0):
        place = rows_at(start + step, size)
        first = early[place, :] if start < ROW_C else corner[...]
        a = jnp.where(is_early, first, far[place, :])
        b = near[rows_at(offset + start + step, size), :]
        return jnp.where(odd, a, b), jnp.where(odd, b, a)

    c_n, c_s = both(ROW_C, ROWS)

    def inner_columns(c):
        return jnp.where(at_east, roll(c, 1, 1), roll(c, -1, 1))

    d_n, d_s = inner_columns(c_n), inner_columns(c_s)
    v0, m0 = both_halves(tile(own, TPACKS + 1), 0), both_halves(tile(own, TPACKS), 1)
    v1, m1 = tile(aux, AUX_V), tile(aux, AUX_M)

    def corner_faces(v, m, north_rows, south_rows):
        v_n, v_s = north_rows[AUX_V : AUX_V + 1], south_rows[AUX_V : AUX_V + 1]
        m_n, m_s = north_rows[AUX_M : AUX_M + 1], south_rows[AUX_M : AUX_M + 1]
        an, bn = face(0.5 * (v + v_n), jnp.where(at_north, m * m_n, 0.0))
        as_, bs = face(0.5 * (v_s + v), jnp.where(at_south, m_s * m, 0.0))
        return lambda t, t_n, t_s: (as_ * t_s + bs * t) - (an * t + bn * t_n)

    halo_sum = corner_faces(v1, m1, c_n, c_s)
    own_sum = corner_faces(v0, m0, d_n, d_s)
    a1, b1 = tile(aux, AUX_A), tile(aux, AUX_B)
    sign = edge_sign()

    def corner_row(c, ref, p):
        del c
        return ref[pl.ds(p, 1), :]

    for c, ref in zip((c_n, c_s, d_n, d_s), lines_refs):
        ref[...] = c

    def flux_of(p):
        lines = [corner_row(c, ref, p) for c, ref in zip((c_n, c_s, d_n, d_s), lines_refs)]
        f1 = tile(aux, AUX_F + p)
        s1 = tile(aux, AUX_Q + p) + jnp.where(at_east, f1, -f1)
        s1 = s1 + halo_sum(tile(aux, AUX_T + p), lines[0], lines[1])
        s0 = tile(packs, p) + own_sum(tile(own, p), lines[2], lines[3])
        return a1 * jnp.where(at_east, s0, s1) + b1 * jnp.where(at_east, s1, s0)

    spread_out(spread, flux_of, sign)

    v_n, v_s = both(ROW_V, K)
    m_n, m_s = both(ROW_M, K)
    an, bn = face(
        0.5 * (edge(north, 0, K, ROWS - 1) + v_n), edge(mask, 0, K, ROWS - 1).astype(jnp.float32) * m_n
    )
    as_, bs = face(0.5 * (v_s + edge(north, 0, K, 0)), m_s * edge(mask, 0, K, 0).astype(jnp.float32))

    def edge_flux(ref, p, f):
        line = jnp.broadcast_to(ref[pl.ds(AUX_F + p, 1), :], (ROWS, COLS))
        return jnp.concatenate(
            [
                sign * pltpu.roll(line, COLS - 1 - (lane_base(f, k) + 1), 1, stride=4, stride_axis=0)
                for k in (0, ROWS)
            ],
            axis=0,
        )

    def edge_pair(p):
        for half in (0, 1):
            f = 2 * p + half
            t_n, t_s = both(ROW_T, K, f * K)
            p_n, p_s = both(ROW_P, K, f * K)
            p_n = p_n + edge_flux(lines_refs[0], p, half)
            p_s = p_s + edge_flux(lines_refs[1], p, half)
            g_n = an * edge(tracer, f * K, K, ROWS - 1) + bn * t_n
            g_s = as_ * t_s + bs * edge(tracer, f * K, K, 0)
            low = pl.ds(f * K * ROWS, K, stride=ROWS)
            high = pl.ds(f * K * ROWS + ROWS - 1, K, stride=ROWS)
            s_low, s_high = full[low, :] + g_s, full[high, :] - g_n
            full[low, :] = s_low
            full[high, :] = s_high
            sums[low, :] = sums[low, :] + (g_s + (as_ * (p_s - g_s) + bs * s_low))
            sums[high, :] = sums[high, :] - (g_n + (an * s_high + bn * (p_n + g_n)))

    for p in range(TPACKS):
        edge_pair(p)

    def copy_of(f):
        place = rows_at(f * K * ROWS, K * ROWS)
        return pltpu.make_async_copy(out.at[place, :], result.at[place, :], sems.at[f])

    def tracer_columns(f):
        value = None
        for k in range(K):
            index = f * K + k
            faces = [tile(coeff, i * K + k) for i in range(5)]
            rhs = (tile(sums, index) + tile(spread, index)) + inner_sum(tile(full, index), faces)
            value_new = rhs * tile(solve, k)
            if k:
                value_new = value_new + tile(solve, K + k) * value
            value = value_new
            put(out, index, value)
        for k in range(K - 2, -1, -1):
            index = f * K + k
            value = tile(out, index) - tile(solve, 2 * K + k) * value
            put(out, index, value)
        copy_of(f).start()

    for f in range(NT):
        tracer_columns(f)
    for f in range(NT):
        copy_of(f).wait()


def early_far(lat, lon, lat_count, lon_count):
    mirrored = lon_count - 1 - lon
    return (lon % 8 >= 2) & ((lat < lat_count - 1) | (mirrored % 8 >= 2))


def call(kernel, outs, scratch_rows, *operands, hbm=False, hbm_out=0, scratch=(), alias=None):
    vmem = pl.BlockSpec(memory_space=pltpu.VMEM)
    in_hbm = pl.BlockSpec(memory_space=pltpu.HBM)
    shapes = [
        x if isinstance(x, jax.ShapeDtypeStruct) else jax.ShapeDtypeStruct((x, COLS), jnp.float32)
        for x in outs
    ]
    return pl.pallas_call(
        kernel,
        out_shape=shapes,
        in_specs=[in_hbm if hbm else vmem] * len(operands),
        out_specs=[in_hbm] * hbm_out + [vmem] * (len(shapes) - hbm_out),
        scratch_shapes=[pltpu.VMEM((rows, COLS), jnp.float32) for rows in scratch_rows] + list(scratch),
        compiler_params=pltpu.CompilerParams(vmem_limit_bytes=24 * 1024 * 1024),
        input_output_aliases=alias or {},
    )(*operands)


def pairs(lat_count, lon_count):
    def at(i, j):
        return i * lon_count + j % lon_count

    lon_near = [(at(i, j), at(i, j + 1)) for i in range(lat_count) for j in range(0, lon_count, 2)]
    lon_far = [(at(i, j), at(i, j + 1)) for i in range(lat_count) for j in range(1, lon_count, 2)]
    lat_near = [(at(i, j), at(i + 1, j)) for i in range(0, lat_count, 2) for j in range(lon_count)]
    lat_far = [(at(i, j), at(i + 1, j)) for i in range(1, lat_count - 1, 2) for j in range(lon_count)]
    top = lat_count - 1
    lat_far += [(at(top, j), at(top, lon_count - 1 - j)) for j in range(lon_count // 2)]
    return lon_near, lon_far, lat_near, lat_far


def swapped(x, groups):
    return lax.ppermute(x, AXES, [(a, b) for a, b in groups] + [(b, a) for a, b in groups])


def gathered(x, groups):
    both = lax.all_gather(x, AXES, axis_index_groups=[list(g) for g in groups])
    return both.reshape(-1, COLS)


def on_device(tracer, east_vel, north_vel, wet_mask, bottom_level, vertical_mix):
    lon_near, lon_far, lat_near, lat_far = pairs(lax.axis_size("lat"), lax.axis_size("lon"))
    flat = lambda x: x.reshape(-1, COLS)
    fields = [
        pltpu.with_memory_space_constraint(flat(x), pltpu.HBM)
        for x in (tracer, east_vel, north_vel, wet_mask, vertical_mix, bottom_level)
    ]
    own, t, u, v, m, vertical, depth = call(
        load_kernel,
        [PACK_ROWS] + [jax.ShapeDtypeStruct(x.shape, x.dtype) for x in fields],
        [],
        *fields,
        hbm=True,
        scratch=[pltpu.SemaphoreType.DMA((6,))],
    )
    far = swapped(own, lon_far)
    pay_far, pay_near, early, own_again = call(
        rows_kernel, [PAY_ROWS, PAY_ROWS, EARLY_ROWS, PACK_ROWS], [], t, u, v, m, own
    )
    counts = lax.axis_size("lat"), lax.axis_size("lon")
    lat_early = [(a, b) for a, b in lat_far if early_far(*divmod(b, counts[1]), *counts)]
    lat_late = [pair for pair in lat_far if pair not in lat_early]
    early_rows = swapped(early, lat_early)
    near = gathered(own_again, lon_near)
    pay_far, pay_near, aux, corner, *ready = call(
        outward_kernel,
        [PAY_ROWS, PAY_ROWS, AUX * ROWS, ROWS] + COLUMN_ROWS,
        [TILES * ROWS],
        own, near, far, pay_far, pay_near, t, u, v, m, vertical, depth,
        alias={3: 0, 4: 1},
    )
    far_rows = swapped(pay_far, lat_late)
    corner_rows = swapped(corner, lat_early)
    near_rows = gathered(pay_near, lat_near)
    full, both, packs, solve, coeff = call(
        column_kernel,
        COLUMN_ROWS,
        [TILES * ROWS],
        t, u, v, m, vertical, depth, aux, *ready,
        alias={7 + i: i for i in range(len(COLUMN_ROWS))},
    )
    out, _, _ = call(
        last_kernel,
        [TILES * ROWS] * 3,
        [TILES * ROWS, TILES * ROWS] + [ROWS] * 4,
        early_rows, corner_rows, far_rows, near_rows, t, v, m, coeff, full, both, packs, solve, own, aux,
        alias={8: 1, 9: 2},
        scratch=[pltpu.SemaphoreType.DMA((NT,))],
        hbm_out=1,
    )
    return out.reshape(tracer.shape)


def solution(mesh):
    fields = P(None, "lat", "lon")
    tracers = P(None, None, "lat", "lon")
    return jax.shard_map(
        on_device,
        mesh=mesh,
        in_specs=(tracers, fields, fields, fields, P("lat", "lon"), fields),
        out_specs=tracers,
        check_vma=False,
    )
```

```python
import jax
import jax.numpy as jnp
from jax import lax
from jax.experimental import pallas as pl
from jax.experimental.pallas import tpu as pltpu
from jax.sharding import PartitionSpec as P

ROWS = 8
COLS = 128
NT = 6
K = 16
TILES = NT * K
mixing = 0.08
AXES = ("lat", "lon")

FIELDS = NT + 3
PACKS = (FIELDS + 1) // 2
PACK_ROWS = PACKS * ROWS
TPACKS = NT // 2

ROW_T = 0
ROW_P = TILES
ROW_V = 2 * TILES
ROW_M = ROW_V + K
ROW_C = ROW_M + K
PAY_ROWS = ROW_C + ROWS
EARLY_ROWS = PAY_ROWS + ROWS

AUX_T = 0
AUX_V = TPACKS
AUX_M = AUX_V + 1
AUX_F = AUX_M + 1
AUX_Q = AUX_F + TPACKS
AUX_A = AUX_Q + TPACKS
AUX_B = AUX_A + 1
AUX = AUX_B + 1


def roll(x, shift, axis):
    shift %= x.shape[axis]
    return pltpu.roll(x, shift, axis) if shift else x


def lanes(rows=ROWS):
    return lax.broadcasted_iota(jnp.int32, (rows, COLS), 1)


def row_ids():
    return lax.broadcasted_iota(jnp.int32, (ROWS, COLS), 0)


def face(speed, opening):
    return opening * (jnp.maximum(speed, 0.0) + mixing), opening * (jnp.minimum(speed, 0.0) - mixing)


def rows_at(start, size):
    return pl.ds(start if isinstance(start, int) else pl.multiple_of(start, ROWS), size)


def tile(ref, index):
    return ref[rows_at(index * ROWS, ROWS), :]


def put(ref, index, value):
    ref[rows_at(index * ROWS, ROWS), :] = value


def edge(ref, start, size, row):
    return ref[pl.ds(start * ROWS + row, size, stride=ROWS), :]


def repeat(count, body, unroll=1):
    def step(i, carry):
        body(i)
        return carry

    lax.fori_loop(0, count, step, 0, unroll=unroll)


def lane_base(field, k):
    return 64 * (field % 2) + 4 * (K - 1 - k)


def packed_edges(load, fields):
    group = lanes() // 4
    total = jnp.zeros((ROWS, COLS), jnp.float32)
    for field in fields:
        for k in range(K):
            base = lane_base(field, k)
            total = jnp.where(group == base // 4, roll(load(field, k), base - 126, 1), total)
    return total


def row_part(tracer, east, north, mask, row, inward):
    u, m = edge(east, 0, K, row), edge(mask, 0, K, row).astype(jnp.float32)
    v, v_in = edge(north, 0, K, row), edge(north, 0, K, inward)
    m_in = edge(mask, 0, K, inward).astype(jnp.float32)
    ax, bx = face(0.5 * (u + roll(u, -1, 1)), jnp.where(lanes(K) < COLS - 1, m * roll(m, -1, 1), 0.0))
    ay, by = face(0.5 * (v + v_in), m * m_in)
    ts, sums = [], []
    for f in range(NT):
        t, t_in = edge(tracer, f * K, K, row), edge(tracer, f * K, K, inward)
        fe = ax * t + bx * roll(t, -1, 1)
        g = -(ay * t + by * t_in) if inward > row else ay * t_in + by * t
        ts.append(t)
        sums.append(t + ((roll(fe, 1, 1) - fe) + g))
    return ts + sums + [v, m]


def load_kernel(tracer, east, north, mask, mix, bottom, pack, t, u, v, m, vertical, depth, sems):
    copies = [
        pltpu.make_async_copy(src, dst, sems.at[i])
        for i, (src, dst) in enumerate(
            ((tracer, t), (east, u), (north, v), (mask, m), (mix, vertical), (bottom, depth))
        )
    ]
    for copy in copies:
        copy.start()

    def load(field, k):
        if field < NT:
            return tile(t, field * K + k)
        if field == NT:
            return tile(u, k)
        if field == NT + 1:
            return tile(m, k).astype(jnp.float32)
        return tile(v, k)

    for copy in copies[1:4]:
        copy.wait()
    for p in range(TPACKS, PACKS):
        put(pack, p, packed_edges(load, range(2 * p, min(2 * p + 2, FIELDS))))
    copies[0].wait()
    for p in range(TPACKS):
        put(pack, p, packed_edges(load, range(2 * p, 2 * p + 2)))
    for copy in copies[4:]:
        copy.wait()


def rows_kernel(t, u, v, m, own, pay_far, pay_near, early, own_out):
    odd = lax.rem(lax.axis_index("lat"), 2) == 1
    upper = row_part(t, u, v, m, ROWS - 1, ROWS - 2)
    lower = row_part(t, u, v, m, 0, 1)
    for i, (x, y) in enumerate(zip(upper, lower)):
        pay_far[i * K : (i + 1) * K, :] = jnp.where(odd, x, y)
        pay_near[i * K : (i + 1) * K, :] = jnp.where(odd, y, x)
    for pay in (pay_far, pay_near):
        pay[ROW_C:, :] = jnp.zeros((ROWS, COLS), jnp.float32)

    @pl.when(lax.axis_index("lat") == lax.axis_size("lat") - 1)
    def _():
        x = flipped(pay_far[:ROW_C, :])
        pay_far[:ROW_V, :] = x[:ROW_V]
        pay_far[ROW_V:ROW_M, :] = -x[ROW_V:ROW_M]
        pay_far[ROW_M:ROW_C, :] = x[ROW_M:]

    early[:ROW_C, :] = pay_far[:ROW_C, :]
    early[ROW_C:, :] = jnp.zeros((EARLY_ROWS - ROW_C, COLS), jnp.float32)
    own_out[...] = own[...]


def level_faces(east, north, mask, k):
    u, v, m = tile(east, k), tile(north, k), tile(mask, k).astype(jnp.float32)
    open_x = jnp.where(lanes() < COLS - 1, m * roll(m, -1, 1), 0.0)
    open_y = jnp.where(row_ids() < ROWS - 1, m * roll(m, -1, 0), 0.0)
    ax, bx = face(0.5 * (u + roll(u, -1, 1)), open_x)
    ay, by = face(0.5 * (v + roll(v, -1, 0)), open_y)
    middle = (roll(bx, 1, 1) - ax) + (roll(by, 1, 0) - ay)
    return middle, roll(ax, 1, 1), -bx, roll(ay, 1, 0), -by


def inner_sum(t, faces):
    middle, west, east, south, north = faces
    sides = (west * roll(t, 1, 1) + east * roll(t, -1, 1)) + (south * roll(t, 1, 0) + north * roll(t, -1, 0))
    return middle * t + sides


def flipped(x):
    lane = lanes(x.shape[0])
    for step in (1, 2, 4, 8, 16, 32, 64):
        x = jnp.where((lane & step) != 0, roll(x, step, 1), roll(x, -step, 1))
    return x


def both_halves(x, half):
    swapped = roll(x, 64, 1)
    low = lanes() < 64
    return jnp.where(low, x, swapped) if half == 0 else jnp.where(low, swapped, x)


def edge_sign():
    lane = lanes()
    return jnp.where(lane == 0, 1.0, jnp.where(lane == COLS - 1, -1.0, 0.0))


def outward_kernel(
    own, near, far, far_in, near_in, tracer, east, north, mask, mix, bottom,
    pay_far, pay_near, aux, corner_far, *refs,
):
    lat_odd = lax.rem(lax.axis_index("lat"), 2)
    lon_odd = lax.rem(lax.axis_index("lon"), 2)
    is_top = lax.axis_index("lat") == lax.axis_size("lat") - 1
    place = lanes() & 3
    at_east = place == 1
    even = lon_odd == 0
    offset = pl.multiple_of((1 - lon_odd) * PACK_ROWS, ROWS)
    here, one, two = [], [], []
    for p in range(PACKS):
        a = near[pl.ds(pl.multiple_of(offset + p * ROWS, ROWS), ROWS), :]
        b = tile(far, p)
        e = jnp.where(even, a, b)
        w = jnp.where(even, b, a)
        here.append(tile(own, p))
        one.append(jnp.where(at_east, roll(e, -1, 1), roll(w, 1, 1)))
        two.append(jnp.where(at_east, roll(e, -2, 1), roll(w, 2, 1)))
    u0, m0 = both_halves(here[TPACKS], 0), both_halves(here[TPACKS], 1)
    u1, m1 = both_halves(one[TPACKS], 0), both_halves(one[TPACKS], 1)
    u2, m2 = both_halves(two[TPACKS], 0), both_halves(two[TPACKS], 1)
    v0, v1 = both_halves(here[TPACKS + 1], 0), both_halves(one[TPACKS + 1], 0)
    a1, b1 = face(0.5 * (u0 + u1), m0 * m1)
    a2, b2 = face(0.5 * (u1 + u2), m1 * m2)
    inner_y = row_ids() < ROWS - 1
    ay, by = face(0.5 * (v1 + roll(v1, -1, 0)), jnp.where(inner_y, m1 * roll(m1, -1, 0), 0.0))

    def corner(mine, halo):
        return jnp.where(
            place == 0, roll(mine, -1, 1), jnp.where(place == 3, roll(mine, 1, 1), halo)
        )

    for p in range(TPACKS):
        t0, t1, t2 = here[p], one[p], two[p]
        f1 = a1 * jnp.where(at_east, t0, t1) + b1 * jnp.where(at_east, t1, t0)
        f2 = a2 * jnp.where(at_east, t1, t2) + b2 * jnp.where(at_east, t2, t1)
        gn = ay * t1 + by * roll(t1, -1, 0)
        put(aux, AUX_F + p, f1)
        put(aux, AUX_Q + p, t1 + jnp.where(at_east, -f2, f2) + (roll(gn, 1, 0) - gn))
        put(aux, AUX_T + p, corner(t0, t1))
    put(aux, AUX_V, corner(v0, v1))
    put(aux, AUX_M, corner(m0, m1))
    put(aux, AUX_A, a1)
    put(aux, AUX_B, b1)

    del far_in, near_in
    pay_near[ROW_C:, :] = aux[pl.ds(AUX_T * ROWS + (ROWS - 1) * (1 - lat_odd), ROWS, stride=ROWS), :]
    c = aux[pl.ds(AUX_T * ROWS + (ROWS - 1) * lat_odd, ROWS, stride=ROWS), :]
    turned = jnp.where(
        place == 0,
        roll(c, -3, 1),
        jnp.where(place == 1, roll(c, -1, 1), jnp.where(place == 2, roll(c, 1, 1), roll(c, 3, 1))),
    )
    rows = row_ids()
    turned = jnp.where((rows == AUX_V) | (rows >= AUX_F), -turned, turned)
    c = jnp.where(is_top, turned, c)
    pay_far[ROW_C:, :] = c
    corner_far[...] = c

    @pl.when(ahead_of_partner())
    def _():
        columns(tracer, east, north, mask, mix, bottom, aux, *refs)


def spread_out(spread, packed, sign):
    def pair(p):
        x = packed(p)
        for f in (0, 1):
            for k in range(K):
                put(spread, (2 * p + f) * K + k, sign * roll(x, COLS - 1 - (lane_base(f, k) + 1), 1))

    for p in range(TPACKS):
        pair(p)


def columns(tracer, east, north, mask, mix, bottom, aux, full, both, packs, solve, coeff, spread):
    sign = edge_sign()
    spread_out(spread, lambda p: tile(aux, AUX_F + p), sign)

    def level(k):
        faces = level_faces(east, north, mask, k)
        for i in range(5):
            put(coeff, i * K + k, faces[i])
        for f in range(NT):
            index = f * K + k
            t = tile(tracer, index)
            x = t + (inner_sum(t, faces) + tile(spread, index))
            put(full, index, x)
            put(both, index, t + x)

    repeat(K, level, unroll=8)
    for p in range(TPACKS):
        put(packs, p, packed_edges(lambda f, k: tile(full, f * K + k), (2 * p, 2 * p + 1)))
    depth = bottom[...]
    lower = ratio = None
    for k in range(K):
        denom = 1.0
        upper = None
        if k + 1 < K:
            upper = jnp.where(k + 1 < depth, tile(mix, k), 0.0)
            denom = denom + upper
        if k:
            denom = denom + lower + lower * ratio
        inverse = 1.0 / denom
        put(solve, k, 0.5 * inverse)
        if k:
            put(solve, K + k, lower * inverse)
        else:
            put(solve, K + k, jnp.zeros((ROWS, COLS), jnp.float32))
        ratio = -upper * inverse if upper is not None else jnp.zeros((ROWS, COLS), jnp.float32)
        put(solve, 2 * K + k, ratio)
        lower = upper


COLUMN_ROWS = [TILES * ROWS, TILES * ROWS, TPACKS * ROWS, 3 * K * ROWS, 5 * K * ROWS]


def ahead_of_partner():
    lat = lax.axis_index("lat")
    return (lat >= 2) & (lat < 4) & (lax.axis_index("lon") < 2)


class Edge:
    def __init__(self, is_north, tracer, north, mask, other):
        self.is_north, self.tracer, self.other = is_north, tracer, other
        self.row = jnp.where(is_north, ROWS - 1, 0)
        first, second = face(
            0.5 * (edge(north, 0, K, self.row) + other(ROW_V, K)),
            edge(mask, 0, K, self.row).astype(jnp.float32) * other(ROW_M, K),
        )
        self.mine = jnp.where(is_north, -first, second)
        self.theirs = jnp.where(is_north, -second, first)

    def place(self, f):
        return pl.ds(f * K * ROWS + self.row, K, stride=ROWS)

    def fluxes(self, f, flux_row, before):
        line = jnp.broadcast_to(flux_row, (ROWS, COLS))
        sign = edge_sign()
        added = [
            sign * pltpu.roll(line, COLS - 1 - (lane_base(f, k) + 1), 1, stride=4, stride_axis=0) for k in (0, ROWS)
        ]
        beyond = self.other(ROW_P + f * K, K) + jnp.concatenate(added, axis=0)
        g = self.mine * edge(self.tracer, f * K, K, self.row) + self.theirs * self.other(ROW_T + f * K, K)
        s = before + g
        return g, s, self.mine * s + self.theirs * (beyond - g)


def column_kernel(tracer, east, north, mask, mix, bottom, aux, near, *refs):
    count = len(COLUMN_ROWS)

    @pl.when(jnp.logical_not(ahead_of_partner()))
    def _():
        columns(tracer, east, north, mask, mix, bottom, aux, *refs[count:])

    full, sums, _, _, coeff = refs[count : 2 * count]
    lat_odd = lax.rem(lax.axis_index("lat"), 2)
    offset = pl.multiple_of((1 - lat_odd) * PAY_ROWS, ROWS)
    side = Edge(lat_odd == 0, tracer, north, mask, lambda start, size: near[rows_at(offset + start, size), :])
    for f in range(NT):
        place = side.place(f)
        g, s, h = side.fluxes(f, near[pl.ds(offset + ROW_C + AUX_F + f // 2, 1), :], full[place, :])
        full[place, :] = s
        sums[place, :] = sums[place, :] + (g + h)

    def level(k):
        faces = [tile(coeff, i * K + k) for i in range(5)]
        for f in range(NT):
            index = f * K + k
            put(sums, index, tile(sums, index) + inner_sum(tile(full, index), faces))

    repeat(K, level, unroll=8)


def last_kernel(
    early, corner, far, near, tracer, north, mask, coeff, full, sums_in, packs, solve, own, aux,
    result, sums, spread, out, line_1, line_2, line_3, line_4, line_5, sems,
):
    del sums_in
    lines_refs = (line_1, line_2, line_3, line_4)
    lat_odd = lax.rem(lax.axis_index("lat"), 2)
    odd = lat_odd == 1
    offset = pl.multiple_of((1 - lat_odd) * PAY_ROWS, ROWS)
    place = lanes() & 3
    at_east = place == 1
    rows = row_ids()
    at_south, at_north = rows == 0, rows == ROWS - 1

    is_early = early_far(lax.axis_index("lat"), lax.axis_index("lon"), lax.axis_size("lat"), lax.axis_size("lon"))

    def beyond(start, size):
        return jnp.where(is_early, early[start : start + size, :], far[start : start + size, :])

    c_far = jnp.where(is_early, corner[...], far[ROW_C:, :])
    c_near = near[rows_at(offset + ROW_C, ROWS), :]
    c_n, c_s = jnp.where(odd, c_far, c_near), jnp.where(odd, c_near, c_far)
    line_5[...] = c_far

    def inner_columns(c):
        return jnp.where(at_east, roll(c, 1, 1), roll(c, -1, 1))

    d_n, d_s = inner_columns(c_n), inner_columns(c_s)
    v0, m0 = both_halves(tile(own, TPACKS + 1), 0), both_halves(tile(own, TPACKS), 1)
    v1, m1 = tile(aux, AUX_V), tile(aux, AUX_M)

    def corner_faces(v, m, north_rows, south_rows):
        v_n, v_s = north_rows[AUX_V : AUX_V + 1], south_rows[AUX_V : AUX_V + 1]
        m_n, m_s = north_rows[AUX_M : AUX_M + 1], south_rows[AUX_M : AUX_M + 1]
        an, bn = face(0.5 * (v + v_n), jnp.where(at_north, m * m_n, 0.0))
        as_, bs = face(0.5 * (v_s + v), jnp.where(at_south, m_s * m, 0.0))
        return lambda t, t_n, t_s: (as_ * t_s + bs * t) - (an * t + bn * t_n)

    halo_sum = corner_faces(v1, m1, c_n, c_s)
    own_sum = corner_faces(v0, m0, d_n, d_s)
    a1, b1 = tile(aux, AUX_A), tile(aux, AUX_B)
    sign = edge_sign()

    def corner_row(c, ref, p):
        del c
        return ref[pl.ds(p, 1), :]

    for c, ref in zip((c_n, c_s, d_n, d_s), lines_refs):
        ref[...] = c

    def flux_of(p):
        lines = [corner_row(c, ref, p) for c, ref in zip((c_n, c_s, d_n, d_s), lines_refs)]
        f1 = tile(aux, AUX_F + p)
        s1 = tile(aux, AUX_Q + p) + jnp.where(at_east, f1, -f1)
        s1 = s1 + halo_sum(tile(aux, AUX_T + p), lines[0], lines[1])
        s0 = tile(packs, p) + own_sum(tile(own, p), lines[2], lines[3])
        return a1 * jnp.where(at_east, s0, s1) + b1 * jnp.where(at_east, s1, s0)

    spread_out(spread, flux_of, sign)

    side = Edge(odd, tracer, north, mask, beyond)
    inward = jnp.where(odd, ROWS - 2, 1)
    middle, west, east = (edge(coeff, i * K, K, side.row) for i in range(3))
    beside = jnp.where(odd, edge(coeff, 4 * K, K, ROWS - 2), edge(coeff, 3 * K, K, 1))
    for f in range(NT):
        place = side.place(f)
        g, _, h = side.fluxes(f, line_5[AUX_F + f // 2 : AUX_F + f // 2 + 1, :], full[place, :])
        sums[place, :] = sums[place, :] + (g + h + (middle * g + (west * roll(g, 1, 1) + east * roll(g, -1, 1))))
        place = pl.ds(f * K * ROWS + inward, K, stride=ROWS)
        sums[place, :] = sums[place, :] + beside * g

    def copy_of(f):
        place = rows_at(f * K * ROWS, K * ROWS)
        return pltpu.make_async_copy(out.at[place, :], result.at[place, :], sems.at[f])

    def tracer_columns(f):
        value = None
        for k in range(K):
            index = f * K + k
            value_new = (tile(sums, index) + tile(spread, index)) * tile(solve, k)
            if k:
                value_new = value_new + tile(solve, K + k) * value
            value = value_new
            put(out, index, value)
        for k in range(K - 2, -1, -1):
            index = f * K + k
            value = tile(out, index) - tile(solve, 2 * K + k) * value
            put(out, index, value)
        copy_of(f).start()

    for f in range(NT):
        tracer_columns(f)
    for f in range(NT):
        copy_of(f).wait()


def early_far(lat, lon, lat_count, lon_count):
    mirrored = lon_count - 1 - lon
    return (lon % 8 >= 4) & ((lat < lat_count - 1) | (mirrored % 8 >= 4))


def call(kernel, outs, scratch_rows, *operands, hbm=False, hbm_out=0, scratch=(), alias=None):
    vmem = pl.BlockSpec(memory_space=pltpu.VMEM)
    in_hbm = pl.BlockSpec(memory_space=pltpu.HBM)
    shapes = [
        x if isinstance(x, jax.ShapeDtypeStruct) else jax.ShapeDtypeStruct((x, COLS), jnp.float32)
        for x in outs
    ]
    return pl.pallas_call(
        kernel,
        out_shape=shapes,
        in_specs=[in_hbm if hbm else vmem] * len(operands),
        out_specs=[in_hbm] * hbm_out + [vmem] * (len(shapes) - hbm_out),
        scratch_shapes=[pltpu.VMEM((rows, COLS), jnp.float32) for rows in scratch_rows] + list(scratch),
        compiler_params=pltpu.CompilerParams(vmem_limit_bytes=24 * 1024 * 1024),
        input_output_aliases=alias or {},
    )(*operands)


def pairs(lat_count, lon_count):
    def at(i, j):
        return i * lon_count + j % lon_count

    lon_near = [(at(i, j), at(i, j + 1)) for i in range(lat_count) for j in range(0, lon_count, 2)]
    lon_far = [(at(i, j), at(i, j + 1)) for i in range(lat_count) for j in range(1, lon_count, 2)]
    lat_near = [(at(i, j), at(i + 1, j)) for i in range(0, lat_count, 2) for j in range(lon_count)]
    lat_far = [(at(i, j), at(i + 1, j)) for i in range(1, lat_count - 1, 2) for j in range(lon_count)]
    top = lat_count - 1
    lat_far += [(at(top, j), at(top, lon_count - 1 - j)) for j in range(lon_count // 2)]
    return lon_near, lon_far, lat_near, lat_far


def swapped(x, groups):
    return lax.ppermute(x, AXES, [(a, b) for a, b in groups] + [(b, a) for a, b in groups])


def gathered(x, groups):
    both = lax.all_gather(x, AXES, axis_index_groups=[list(g) for g in groups])
    return both.reshape(-1, COLS)


def on_device(tracer, east_vel, north_vel, wet_mask, bottom_level, vertical_mix):
    lon_near, lon_far, lat_near, lat_far = pairs(lax.axis_size("lat"), lax.axis_size("lon"))
    flat = lambda x: x.reshape(-1, COLS)
    fields = [
        pltpu.with_memory_space_constraint(flat(x), pltpu.HBM)
        for x in (tracer, east_vel, north_vel, wet_mask, vertical_mix, bottom_level)
    ]
    own, t, u, v, m, vertical, depth = call(
        load_kernel,
        [PACK_ROWS] + [jax.ShapeDtypeStruct(x.shape, x.dtype) for x in fields],
        [],
        *fields,
        hbm=True,
        scratch=[pltpu.SemaphoreType.DMA((6,))],
    )
    far = swapped(own, lon_far)
    pay_far, pay_near, early, own_again = call(
        rows_kernel, [PAY_ROWS, PAY_ROWS, EARLY_ROWS, PACK_ROWS], [], t, u, v, m, own
    )
    counts = lax.axis_size("lat"), lax.axis_size("lon")
    lat_early = [(a, b) for a, b in lat_far if early_far(*divmod(b, counts[1]), *counts)]
    lat_late = [pair for pair in lat_far if pair not in lat_early]
    early_rows = swapped(early, lat_early)
    near = gathered(own_again, lon_near)
    pay_far, pay_near, aux, corner, *ready = call(
        outward_kernel,
        [PAY_ROWS, PAY_ROWS, AUX * ROWS, ROWS] + COLUMN_ROWS,
        [TILES * ROWS],
        own, near, far, pay_far, pay_near, t, u, v, m, vertical, depth,
        alias={3: 0, 4: 1},
    )
    far_rows = swapped(pay_far, lat_late)
    corner_rows = swapped(corner, lat_early)
    near_rows = gathered(pay_near, lat_near)
    full, both, packs, solve, coeff = call(
        column_kernel,
        COLUMN_ROWS,
        [TILES * ROWS],
        t, u, v, m, vertical, depth, aux, near_rows, *ready,
        alias={8 + i: i for i in range(len(COLUMN_ROWS))},
    )
    out, _ = call(
        last_kernel,
        [TILES * ROWS] * 2,
        [TILES * ROWS, TILES * ROWS] + [ROWS] * 5,
        early_rows, corner_rows, far_rows, near_rows, t, v, m, coeff, full, both, packs, solve, own, aux,
        alias={9: 1},
        scratch=[pltpu.SemaphoreType.DMA((NT,))],
        hbm_out=1,
    )
    return out.reshape(tracer.shape)


def solution(mesh):
    fields = P(None, "lat", "lon")
    tracers = P(None, None, "lat", "lon")
    return jax.shard_map(
        on_device,
        mesh=mesh,
        in_specs=(tracers, fields, fields, fields, P("lat", "lon"), fields),
        out_specs=tracers,
        check_vma=False,
    )
```

```python
import jax
import jax.numpy as jnp
from jax import lax
from jax.experimental import pallas as pl
from jax.experimental.pallas import tpu as pltpu
from jax.sharding import PartitionSpec as P

ROWS = 8
COLS = 128
NT = 6
K = 16
TILES = NT * K
mixing = 0.08
AXES = ("lat", "lon")

FIELDS = NT + 3
PACKS = (FIELDS + 1) // 2
PACK_ROWS = PACKS * ROWS
TPACKS = NT // 2

ROW_T = 0
ROW_P = TILES
ROW_V = 2 * TILES
ROW_M = ROW_V + K
ROW_C = ROW_M + K
PAY_ROWS = ROW_C + ROWS
EARLY_ROWS = PAY_ROWS + ROWS

AUX_T = 0
AUX_V = TPACKS
AUX_M = AUX_V + 1
AUX_F = AUX_M + 1
AUX_Q = AUX_F + TPACKS
AUX_A = AUX_Q + TPACKS
AUX_B = AUX_A + 1
AUX = AUX_B + 1


def roll(x, shift, axis):
    shift %= x.shape[axis]
    return pltpu.roll(x, shift, axis) if shift else x


def lanes(rows=ROWS):
    return lax.broadcasted_iota(jnp.int32, (rows, COLS), 1)


def row_ids():
    return lax.broadcasted_iota(jnp.int32, (ROWS, COLS), 0)


def face(speed, opening):
    return opening * (jnp.maximum(speed, 0.0) + mixing), opening * (jnp.minimum(speed, 0.0) - mixing)


def rows_at(start, size):
    return pl.ds(start if isinstance(start, int) else pl.multiple_of(start, ROWS), size)


def tile(ref, index):
    return ref[rows_at(index * ROWS, ROWS), :]


def put(ref, index, value):
    ref[rows_at(index * ROWS, ROWS), :] = value


def edge(ref, start, size, row):
    return ref[pl.ds(start * ROWS + row, size, stride=ROWS), :]


def repeat(count, body, unroll=1):
    def step(i, carry):
        body(i)
        return carry

    lax.fori_loop(0, count, step, 0, unroll=unroll)


def lane_base(field, k):
    return 64 * (field % 2) + 4 * (K - 1 - k)


def packed_edges(load, fields):
    group = lanes() // 4
    total = jnp.zeros((ROWS, COLS), jnp.float32)
    for field in fields:
        for k in range(K):
            base = lane_base(field, k)
            total = jnp.where(group == base // 4, roll(load(field, k), base - 126, 1), total)
    return total


def row_part(tracer, east, north, mask, row, inward):
    u, m = edge(east, 0, K, row), edge(mask, 0, K, row).astype(jnp.float32)
    v, v_in = edge(north, 0, K, row), edge(north, 0, K, inward)
    m_in = edge(mask, 0, K, inward).astype(jnp.float32)
    ax, bx = face(0.5 * (u + roll(u, -1, 1)), jnp.where(lanes(K) < COLS - 1, m * roll(m, -1, 1), 0.0))
    ay, by = face(0.5 * (v + v_in), m * m_in)
    ts, sums = [], []
    for f in range(NT):
        t, t_in = edge(tracer, f * K, K, row), edge(tracer, f * K, K, inward)
        fe = ax * t + bx * roll(t, -1, 1)
        g = -(ay * t + by * t_in) if inward > row else ay * t_in + by * t
        ts.append(t)
        sums.append(t + ((roll(fe, 1, 1) - fe) + g))
    return ts + sums + [v, m]


def load_kernel(tracer, east, north, mask, mix, bottom, pack, t, u, v, m, vertical, depth, sems):
    copies = [
        pltpu.make_async_copy(src, dst, sems.at[i])
        for i, (src, dst) in enumerate(
            ((tracer, t), (east, u), (north, v), (mask, m), (mix, vertical), (bottom, depth))
        )
    ]
    for copy in copies:
        copy.start()

    def load(field, k):
        if field < NT:
            return tile(t, field * K + k)
        if field == NT:
            return tile(u, k)
        if field == NT + 1:
            return tile(m, k).astype(jnp.float32)
        return tile(v, k)

    for copy in copies[1:4]:
        copy.wait()
    for p in range(TPACKS, PACKS):
        put(pack, p, packed_edges(load, range(2 * p, min(2 * p + 2, FIELDS))))
    copies[0].wait()
    for p in range(TPACKS):
        put(pack, p, packed_edges(load, range(2 * p, 2 * p + 2)))
    for copy in copies[4:]:
        copy.wait()


def rows_kernel(t, u, v, m, own, pay_far, pay_near, early, own_out):
    odd = lax.rem(lax.axis_index("lat"), 2) == 1
    upper = row_part(t, u, v, m, ROWS - 1, ROWS - 2)
    lower = row_part(t, u, v, m, 0, 1)
    for i, (x, y) in enumerate(zip(upper, lower)):
        pay_far[i * K : (i + 1) * K, :] = jnp.where(odd, x, y)
        pay_near[i * K : (i + 1) * K, :] = jnp.where(odd, y, x)
    for pay in (pay_far, pay_near):
        pay[ROW_C:, :] = jnp.zeros((ROWS, COLS), jnp.float32)

    @pl.when(lax.axis_index("lat") == lax.axis_size("lat") - 1)
    def _():
        x = flipped(pay_far[:ROW_C, :])
        pay_far[:ROW_V, :] = x[:ROW_V]
        pay_far[ROW_V:ROW_M, :] = -x[ROW_V:ROW_M]
        pay_far[ROW_M:ROW_C, :] = x[ROW_M:]

    early[:ROW_C, :] = pay_far[:ROW_C, :]
    early[ROW_C:, :] = jnp.zeros((EARLY_ROWS - ROW_C, COLS), jnp.float32)
    own_out[...] = own[...]


def level_faces(east, north, mask, k):
    u, v, m = tile(east, k), tile(north, k), tile(mask, k).astype(jnp.float32)
    open_x = jnp.where(lanes() < COLS - 1, m * roll(m, -1, 1), 0.0)
    open_y = jnp.where(row_ids() < ROWS - 1, m * roll(m, -1, 0), 0.0)
    ax, bx = face(0.5 * (u + roll(u, -1, 1)), open_x)
    ay, by = face(0.5 * (v + roll(v, -1, 0)), open_y)
    middle = (roll(bx, 1, 1) - ax) + (roll(by, 1, 0) - ay)
    return middle, roll(ax, 1, 1), -bx, roll(ay, 1, 0), -by


def inner_sum(t, faces):
    middle, west, east, south, north = faces
    sides = (west * roll(t, 1, 1) + east * roll(t, -1, 1)) + (south * roll(t, 1, 0) + north * roll(t, -1, 0))
    return middle * t + sides


def flipped(x):
    lane = lanes(x.shape[0])
    for step in (1, 2, 4, 8, 16, 32, 64):
        x = jnp.where((lane & step) != 0, roll(x, step, 1), roll(x, -step, 1))
    return x


def both_halves(x, half):
    swapped = roll(x, 64, 1)
    low = lanes() < 64
    return jnp.where(low, x, swapped) if half == 0 else jnp.where(low, swapped, x)


def edge_sign():
    lane = lanes()
    return jnp.where(lane == 0, 1.0, jnp.where(lane == COLS - 1, -1.0, 0.0))


def outward_kernel(
    own, near, far, far_in, near_in, tracer, east, north, mask, mix, bottom,
    pay_far, pay_near, aux, corner_far, *refs,
):
    lat_odd = lax.rem(lax.axis_index("lat"), 2)
    lon_odd = lax.rem(lax.axis_index("lon"), 2)
    is_top = lax.axis_index("lat") == lax.axis_size("lat") - 1
    place = lanes() & 3
    at_east = place == 1
    even = lon_odd == 0
    offset = pl.multiple_of((1 - lon_odd) * PACK_ROWS, ROWS)
    here, one, two = [], [], []
    for p in range(PACKS):
        a = near[pl.ds(pl.multiple_of(offset + p * ROWS, ROWS), ROWS), :]
        b = tile(far, p)
        e = jnp.where(even, a, b)
        w = jnp.where(even, b, a)
        here.append(tile(own, p))
        one.append(jnp.where(at_east, roll(e, -1, 1), roll(w, 1, 1)))
        two.append(jnp.where(at_east, roll(e, -2, 1), roll(w, 2, 1)))
    u0, m0 = both_halves(here[TPACKS], 0), both_halves(here[TPACKS], 1)
    u1, m1 = both_halves(one[TPACKS], 0), both_halves(one[TPACKS], 1)
    u2, m2 = both_halves(two[TPACKS], 0), both_halves(two[TPACKS], 1)
    v0, v1 = both_halves(here[TPACKS + 1], 0), both_halves(one[TPACKS + 1], 0)
    a1, b1 = face(0.5 * (u0 + u1), m0 * m1)
    a2, b2 = face(0.5 * (u1 + u2), m1 * m2)
    inner_y = row_ids() < ROWS - 1
    ay, by = face(0.5 * (v1 + roll(v1, -1, 0)), jnp.where(inner_y, m1 * roll(m1, -1, 0), 0.0))

    def corner(mine, halo):
        return jnp.where(
            place == 0, roll(mine, -1, 1), jnp.where(place == 3, roll(mine, 1, 1), halo)
        )

    for p in range(TPACKS):
        t0, t1, t2 = here[p], one[p], two[p]
        f1 = a1 * jnp.where(at_east, t0, t1) + b1 * jnp.where(at_east, t1, t0)
        f2 = a2 * jnp.where(at_east, t1, t2) + b2 * jnp.where(at_east, t2, t1)
        gn = ay * t1 + by * roll(t1, -1, 0)
        put(aux, AUX_F + p, f1)
        put(aux, AUX_Q + p, t1 + jnp.where(at_east, -f2, f2) + (roll(gn, 1, 0) - gn))
        put(aux, AUX_T + p, corner(t0, t1))
    put(aux, AUX_V, corner(v0, v1))
    put(aux, AUX_M, corner(m0, m1))
    put(aux, AUX_A, a1)
    put(aux, AUX_B, b1)

    del far_in, near_in
    pay_near[ROW_C:, :] = aux[pl.ds(AUX_T * ROWS + (ROWS - 1) * (1 - lat_odd), ROWS, stride=ROWS), :]
    c = aux[pl.ds(AUX_T * ROWS + (ROWS - 1) * lat_odd, ROWS, stride=ROWS), :]
    turned = jnp.where(
        place == 0,
        roll(c, -3, 1),
        jnp.where(place == 1, roll(c, -1, 1), jnp.where(place == 2, roll(c, 1, 1), roll(c, 3, 1))),
    )
    rows = row_ids()
    turned = jnp.where((rows == AUX_V) | (rows >= AUX_F), -turned, turned)
    c = jnp.where(is_top, turned, c)
    pay_far[ROW_C:, :] = c
    corner_far[...] = c

    @pl.when(ahead_of_partner())
    def _():
        columns(tracer, east, north, mask, mix, bottom, aux, *refs)


def spread_out(spread, packed, sign):
    def pair(p):
        x = packed(p)
        for f in (0, 1):
            for k in range(K):
                put(spread, (2 * p + f) * K + k, sign * roll(x, COLS - 1 - (lane_base(f, k) + 1), 1))

    for p in range(TPACKS):
        pair(p)


def columns(tracer, east, north, mask, mix, bottom, aux, full, both, packs, solve, coeff, spread):
    sign = edge_sign()
    spread_out(spread, lambda p: tile(aux, AUX_F + p), sign)

    def level(k):
        faces = level_faces(east, north, mask, k)
        for i in range(5):
            put(coeff, i * K + k, faces[i])
        for f in range(NT):
            index = f * K + k
            t = tile(tracer, index)
            x = t + (inner_sum(t, faces) + tile(spread, index))
            put(full, index, x)
            put(both, index, t + x)

    repeat(K, level, unroll=8)
    for p in range(TPACKS):
        put(packs, p, packed_edges(lambda f, k: tile(full, f * K + k), (2 * p, 2 * p + 1)))
    depth = bottom[...]
    lower = ratio = None
    for k in range(K):
        denom = 1.0
        upper = None
        if k + 1 < K:
            upper = jnp.where(k + 1 < depth, tile(mix, k), 0.0)
            denom = denom + upper
        if k:
            denom = denom + lower + lower * ratio
        inverse = 1.0 / denom
        put(solve, k, 0.5 * inverse)
        if k:
            put(solve, K + k, lower * inverse)
        else:
            put(solve, K + k, jnp.zeros((ROWS, COLS), jnp.float32))
        ratio = -upper * inverse if upper is not None else jnp.zeros((ROWS, COLS), jnp.float32)
        put(solve, 2 * K + k, ratio)
        lower = upper


COLUMN_ROWS = [TILES * ROWS, TILES * ROWS, TPACKS * ROWS, 3 * K * ROWS, 5 * K * ROWS]


def ahead_of_partner():
    lat = lax.axis_index("lat")
    return (lat >= 2) & (lat < 4) & (lax.axis_index("lon") < 2)


class Edge:
    def __init__(self, is_north, tracer, north, mask, other):
        self.is_north, self.tracer, self.other = is_north, tracer, other
        self.row = jnp.where(is_north, ROWS - 1, 0)
        first, second = face(
            0.5 * (edge(north, 0, K, self.row) + other(ROW_V, K)),
            edge(mask, 0, K, self.row).astype(jnp.float32) * other(ROW_M, K),
        )
        self.mine = jnp.where(is_north, -first, second)
        self.theirs = jnp.where(is_north, -second, first)

    def place(self, f):
        return pl.ds(f * K * ROWS + self.row, K, stride=ROWS)

    def fluxes(self, f, flux_row, before):
        line = jnp.broadcast_to(flux_row, (ROWS, COLS))
        sign = edge_sign()
        added = [
            sign * pltpu.roll(line, COLS - 1 - (lane_base(f, k) + 1), 1, stride=4, stride_axis=0) for k in (0, ROWS)
        ]
        beyond = self.other(ROW_P + f * K, K) + jnp.concatenate(added, axis=0)
        g = self.mine * edge(self.tracer, f * K, K, self.row) + self.theirs * self.other(ROW_T + f * K, K)
        s = before + g
        return g, s, self.mine * s + self.theirs * (beyond - g)


def column_kernel(tracer, east, north, mask, mix, bottom, aux, near, *refs):
    count = len(COLUMN_ROWS)

    @pl.when(jnp.logical_not(ahead_of_partner()))
    def _():
        columns(tracer, east, north, mask, mix, bottom, aux, *refs[count:])

    full, sums, _, _, coeff = refs[count : 2 * count]
    lat_odd = lax.rem(lax.axis_index("lat"), 2)
    offset = pl.multiple_of((1 - lat_odd) * PAY_ROWS, ROWS)
    side = Edge(lat_odd == 0, tracer, north, mask, lambda start, size: near[rows_at(offset + start, size), :])
    for f in range(NT):
        place = side.place(f)
        g, s, h = side.fluxes(f, near[pl.ds(offset + ROW_C + AUX_F + f // 2, 1), :], full[place, :])
        full[place, :] = s
        sums[place, :] = sums[place, :] + (g + h)

    def level(k):
        faces = [tile(coeff, i * K + k) for i in range(5)]
        for f in range(NT):
            index = f * K + k
            put(sums, index, tile(sums, index) + inner_sum(tile(full, index), faces))

    repeat(K, level, unroll=8)


def last_kernel(
    early, corner, far, near, tracer, north, mask, coeff, full, sums_in, packs, solve, own, aux,
    result, sums, spread, out, line_1, line_2, line_3, line_4, line_5, sems,
):
    del sums_in
    lines_refs = (line_1, line_2, line_3, line_4)
    lat_odd = lax.rem(lax.axis_index("lat"), 2)
    odd = lat_odd == 1
    offset = pl.multiple_of((1 - lat_odd) * PAY_ROWS, ROWS)
    place = lanes() & 3
    at_east = place == 1
    rows = row_ids()
    at_south, at_north = rows == 0, rows == ROWS - 1

    is_early = early_far(lax.axis_index("lat"), lax.axis_index("lon"), lax.axis_size("lat"), lax.axis_size("lon"))

    def beyond(start, size):
        return jnp.where(is_early, early[start : start + size, :], far[start : start + size, :])

    c_far = jnp.where(is_early, corner[...], far[ROW_C:, :])
    c_near = near[rows_at(offset + ROW_C, ROWS), :]
    c_n, c_s = jnp.where(odd, c_far, c_near), jnp.where(odd, c_near, c_far)
    line_5[...] = c_far

    def inner_columns(c):
        return jnp.where(at_east, roll(c, 1, 1), roll(c, -1, 1))

    d_n, d_s = inner_columns(c_n), inner_columns(c_s)
    v0, m0 = both_halves(tile(own, TPACKS + 1), 0), both_halves(tile(own, TPACKS), 1)
    v1, m1 = tile(aux, AUX_V), tile(aux, AUX_M)

    def corner_faces(v, m, north_rows, south_rows):
        v_n, v_s = north_rows[AUX_V : AUX_V + 1], south_rows[AUX_V : AUX_V + 1]
        m_n, m_s = north_rows[AUX_M : AUX_M + 1], south_rows[AUX_M : AUX_M + 1]
        an, bn = face(0.5 * (v + v_n), jnp.where(at_north, m * m_n, 0.0))
        as_, bs = face(0.5 * (v_s + v), jnp.where(at_south, m_s * m, 0.0))
        return lambda t, t_n, t_s: (as_ * t_s + bs * t) - (an * t + bn * t_n)

    halo_sum = corner_faces(v1, m1, c_n, c_s)
    own_sum = corner_faces(v0, m0, d_n, d_s)
    a1, b1 = tile(aux, AUX_A), tile(aux, AUX_B)
    sign = edge_sign()

    def corner_row(c, ref, p):
        del c
        return ref[pl.ds(p, 1), :]

    for c, ref in zip((c_n, c_s, d_n, d_s), lines_refs):
        ref[...] = c

    def flux_of(p):
        lines = [corner_row(c, ref, p) for c, ref in zip((c_n, c_s, d_n, d_s), lines_refs)]
        f1 = tile(aux, AUX_F + p)
        s1 = tile(aux, AUX_Q + p) + jnp.where(at_east, f1, -f1)
        s1 = s1 + halo_sum(tile(aux, AUX_T + p), lines[0], lines[1])
        s0 = tile(packs, p) + own_sum(tile(own, p), lines[2], lines[3])
        return a1 * jnp.where(at_east, s0, s1) + b1 * jnp.where(at_east, s1, s0)

    spread_out(spread, flux_of, sign)

    side = Edge(odd, tracer, north, mask, beyond)
    inward = jnp.where(odd, ROWS - 2, 1)
    middle, west, east = (edge(coeff, i * K, K, side.row) for i in range(3))
    beside = jnp.where(odd, edge(coeff, 4 * K, K, ROWS - 2), edge(coeff, 3 * K, K, 1))
    for f in range(NT):
        place = side.place(f)
        g, _, h = side.fluxes(f, line_5[AUX_F + f // 2 : AUX_F + f // 2 + 1, :], full[place, :])
        sums[place, :] = sums[place, :] + (g + h + (middle * g + (west * roll(g, 1, 1) + east * roll(g, -1, 1))))
        place = pl.ds(f * K * ROWS + inward, K, stride=ROWS)
        sums[place, :] = sums[place, :] + beside * g

    def copy_of(f):
        place = rows_at(f * K * ROWS, K * ROWS)
        return pltpu.make_async_copy(out.at[place, :], result.at[place, :], sems.at[f])

    def tracer_columns(fields):
        values = {}
        for k in range(K):
            for f in fields:
                index = f * K + k
                value = (tile(sums, index) + tile(spread, index)) * tile(solve, k)
                if k:
                    value = value + tile(solve, K + k) * values[f]
                values[f] = value
                put(out, index, value)
        for k in range(K - 2, -1, -1):
            for f in fields:
                index = f * K + k
                values[f] = tile(out, index) - tile(solve, 2 * K + k) * values[f]
                put(out, index, values[f])
        for f in fields:
            copy_of(f).start()

    for start in range(0, NT, 3):
        tracer_columns(range(start, start + 3))
    for f in range(NT):
        copy_of(f).wait()


def early_far(lat, lon, lat_count, lon_count):
    mirrored = lon_count - 1 - lon
    return (lon % 8 >= 4) & ((lat < lat_count - 1) | (mirrored % 8 >= 4))


def call(kernel, outs, scratch_rows, *operands, hbm=False, hbm_out=0, scratch=(), alias=None):
    vmem = pl.BlockSpec(memory_space=pltpu.VMEM)
    in_hbm = pl.BlockSpec(memory_space=pltpu.HBM)
    shapes = [
        x if isinstance(x, jax.ShapeDtypeStruct) else jax.ShapeDtypeStruct((x, COLS), jnp.float32)
        for x in outs
    ]
    return pl.pallas_call(
        kernel,
        out_shape=shapes,
        in_specs=[in_hbm if hbm else vmem] * len(operands),
        out_specs=[in_hbm] * hbm_out + [vmem] * (len(shapes) - hbm_out),
        scratch_shapes=[pltpu.VMEM((rows, COLS), jnp.float32) for rows in scratch_rows] + list(scratch),
        compiler_params=pltpu.CompilerParams(vmem_limit_bytes=24 * 1024 * 1024),
        input_output_aliases=alias or {},
    )(*operands)


def pairs(lat_count, lon_count):
    def at(i, j):
        return i * lon_count + j % lon_count

    lon_near = [(at(i, j), at(i, j + 1)) for i in range(lat_count) for j in range(0, lon_count, 2)]
    lon_far = [(at(i, j), at(i, j + 1)) for i in range(lat_count) for j in range(1, lon_count, 2)]
    lat_near = [(at(i, j), at(i + 1, j)) for i in range(0, lat_count, 2) for j in range(lon_count)]
    lat_far = [(at(i, j), at(i + 1, j)) for i in range(1, lat_count - 1, 2) for j in range(lon_count)]
    top = lat_count - 1
    lat_far += [(at(top, j), at(top, lon_count - 1 - j)) for j in range(lon_count // 2)]
    return lon_near, lon_far, lat_near, lat_far


def swapped(x, groups):
    return lax.ppermute(x, AXES, [(a, b) for a, b in groups] + [(b, a) for a, b in groups])


def gathered(x, groups):
    both = lax.all_gather(x, AXES, axis_index_groups=[list(g) for g in groups])
    return both.reshape(-1, COLS)


def on_device(tracer, east_vel, north_vel, wet_mask, bottom_level, vertical_mix):
    lon_near, lon_far, lat_near, lat_far = pairs(lax.axis_size("lat"), lax.axis_size("lon"))
    flat = lambda x: x.reshape(-1, COLS)
    fields = [
        pltpu.with_memory_space_constraint(flat(x), pltpu.HBM)
        for x in (tracer, east_vel, north_vel, wet_mask, vertical_mix, bottom_level)
    ]
    own, t, u, v, m, vertical, depth = call(
        load_kernel,
        [PACK_ROWS] + [jax.ShapeDtypeStruct(x.shape, x.dtype) for x in fields],
        [],
        *fields,
        hbm=True,
        scratch=[pltpu.SemaphoreType.DMA((6,))],
    )
    far = swapped(own, lon_far)
    pay_far, pay_near, early, own_again = call(
        rows_kernel, [PAY_ROWS, PAY_ROWS, EARLY_ROWS, PACK_ROWS], [], t, u, v, m, own
    )
    counts = lax.axis_size("lat"), lax.axis_size("lon")
    lat_early = [(a, b) for a, b in lat_far if early_far(*divmod(b, counts[1]), *counts)]
    lat_late = [pair for pair in lat_far if pair not in lat_early]
    early_rows = swapped(early, lat_early)
    near = gathered(own_again, lon_near)
    pay_far, pay_near, aux, corner, *ready = call(
        outward_kernel,
        [PAY_ROWS, PAY_ROWS, AUX * ROWS, ROWS] + COLUMN_ROWS,
        [TILES * ROWS],
        own, near, far, pay_far, pay_near, t, u, v, m, vertical, depth,
        alias={3: 0, 4: 1},
    )
    far_rows = swapped(pay_far, lat_late)
    corner_rows = swapped(corner, lat_early)
    near_rows = gathered(pay_near, lat_near)
    full, both, packs, solve, coeff = call(
        column_kernel,
        COLUMN_ROWS,
        [TILES * ROWS],
        t, u, v, m, vertical, depth, aux, near_rows, *ready,
        alias={8 + i: i for i in range(len(COLUMN_ROWS))},
    )
    out, _ = call(
        last_kernel,
        [TILES * ROWS] * 2,
        [TILES * ROWS, TILES * ROWS] + [ROWS] * 5,
        early_rows, corner_rows, far_rows, near_rows, t, v, m, coeff, full, both, packs, solve, own, aux,
        alias={9: 1},
        scratch=[pltpu.SemaphoreType.DMA((NT,))],
        hbm_out=1,
    )
    return out.reshape(tracer.shape)


def solution(mesh):
    fields = P(None, "lat", "lon")
    tracers = P(None, None, "lat", "lon")
    return jax.shard_map(
        on_device,
        mesh=mesh,
        in_specs=(tracers, fields, fields, fields, P("lat", "lon"), fields),
        out_specs=tracers,
        check_vma=False,
    )
```

```python
import jax
import jax.numpy as jnp
from jax import lax
from jax.experimental import pallas as pl
from jax.experimental.pallas import tpu as pltpu
from jax.sharding import PartitionSpec as P

ROWS = 8
COLS = 128
NT = 6
K = 16
TILES = NT * K
mixing = 0.08
AXES = ("lat", "lon")

FIELDS = NT + 3
PACKS = (FIELDS + 1) // 2
PACK_ROWS = PACKS * ROWS
TPACKS = NT // 2

ROW_T = 0
ROW_P = TILES
ROW_V = 2 * TILES
ROW_M = ROW_V + K
ROW_C = ROW_M + K
PAY_ROWS = ROW_C + ROWS
EARLY_ROWS = PAY_ROWS + ROWS

AUX_T = 0
AUX_V = TPACKS
AUX_M = AUX_V + 1
AUX_F = AUX_M + 1
AUX_Q = AUX_F + TPACKS
AUX_A = AUX_Q + TPACKS
AUX_B = AUX_A + 1
AUX = AUX_B + 1


def roll(x, shift, axis):
    shift %= x.shape[axis]
    return pltpu.roll(x, shift, axis) if shift else x


def lanes(rows=ROWS):
    return lax.broadcasted_iota(jnp.int32, (rows, COLS), 1)


def row_ids():
    return lax.broadcasted_iota(jnp.int32, (ROWS, COLS), 0)


def face(speed, opening):
    return opening * (jnp.maximum(speed, 0.0) + mixing), opening * (jnp.minimum(speed, 0.0) - mixing)


def rows_at(start, size):
    return pl.ds(start if isinstance(start, int) else pl.multiple_of(start, ROWS), size)


def tile(ref, index):
    return ref[rows_at(index * ROWS, ROWS), :]


def put(ref, index, value):
    ref[rows_at(index * ROWS, ROWS), :] = value


def edge(ref, start, size, row):
    return ref[pl.ds(start * ROWS + row, size, stride=ROWS), :]


def repeat(count, body, unroll=1):
    def step(i, carry):
        body(i)
        return carry

    lax.fori_loop(0, count, step, 0, unroll=unroll)


def lane_base(field, k):
    return 64 * (field % 2) + 4 * (K - 1 - k)


def packed_edges(load, fields):
    group = lanes() // 4
    total = jnp.zeros((ROWS, COLS), jnp.float32)
    for field in fields:
        for k in range(K):
            base = lane_base(field, k)
            total = jnp.where(group == base // 4, roll(load(field, k), base - 126, 1), total)
    return total


def row_part(tracer, east, north, mask, row, inward):
    u, m = edge(east, 0, K, row), edge(mask, 0, K, row).astype(jnp.float32)
    v, v_in = edge(north, 0, K, row), edge(north, 0, K, inward)
    m_in = edge(mask, 0, K, inward).astype(jnp.float32)
    ax, bx = face(0.5 * (u + roll(u, -1, 1)), jnp.where(lanes(K) < COLS - 1, m * roll(m, -1, 1), 0.0))
    ay, by = face(0.5 * (v + v_in), m * m_in)
    ts, sums = [], []
    for f in range(NT):
        t, t_in = edge(tracer, f * K, K, row), edge(tracer, f * K, K, inward)
        fe = ax * t + bx * roll(t, -1, 1)
        g = -(ay * t + by * t_in) if inward > row else ay * t_in + by * t
        ts.append(t)
        sums.append(t + ((roll(fe, 1, 1) - fe) + g))
    return ts + sums + [v, m]


def load_kernel(tracer, east, north, mask, mix, bottom, pack, t, u, v, m, vertical, depth, sems):
    copies = [
        pltpu.make_async_copy(src, dst, sems.at[i])
        for i, (src, dst) in enumerate(
            ((tracer, t), (east, u), (north, v), (mask, m), (mix, vertical), (bottom, depth))
        )
    ]
    for copy in copies:
        copy.start()

    def load(field, k):
        if field < NT:
            return tile(t, field * K + k)
        if field == NT:
            return tile(u, k)
        if field == NT + 1:
            return tile(m, k).astype(jnp.float32)
        return tile(v, k)

    for copy in copies[1:4]:
        copy.wait()
    for p in range(TPACKS, PACKS):
        put(pack, p, packed_edges(load, range(2 * p, min(2 * p + 2, FIELDS))))
    copies[0].wait()
    for p in range(TPACKS):
        put(pack, p, packed_edges(load, range(2 * p, 2 * p + 2)))
    for copy in copies[4:]:
        copy.wait()


def rows_kernel(t, u, v, m, own, pay_far, pay_near, early, own_out):
    odd = lax.rem(lax.axis_index("lat"), 2) == 1
    upper = row_part(t, u, v, m, ROWS - 1, ROWS - 2)
    lower = row_part(t, u, v, m, 0, 1)
    for i, (x, y) in enumerate(zip(upper, lower)):
        pay_far[i * K : (i + 1) * K, :] = jnp.where(odd, x, y)
        pay_near[i * K : (i + 1) * K, :] = jnp.where(odd, y, x)
    for pay in (pay_far, pay_near):
        pay[ROW_C:, :] = jnp.zeros((ROWS, COLS), jnp.float32)

    @pl.when(lax.axis_index("lat") == lax.axis_size("lat") - 1)
    def _():
        x = flipped(pay_far[:ROW_C, :])
        pay_far[:ROW_V, :] = x[:ROW_V]
        pay_far[ROW_V:ROW_M, :] = -x[ROW_V:ROW_M]
        pay_far[ROW_M:ROW_C, :] = x[ROW_M:]

    early[:ROW_C, :] = pay_far[:ROW_C, :]
    early[ROW_C:, :] = jnp.zeros((EARLY_ROWS - ROW_C, COLS), jnp.float32)
    own_out[...] = own[...]


def level_faces(east, north, mask, k):
    u, v, m = tile(east, k), tile(north, k), tile(mask, k).astype(jnp.float32)
    open_x = jnp.where(lanes() < COLS - 1, m * roll(m, -1, 1), 0.0)
    open_y = jnp.where(row_ids() < ROWS - 1, m * roll(m, -1, 0), 0.0)
    ax, bx = face(0.5 * (u + roll(u, -1, 1)), open_x)
    ay, by = face(0.5 * (v + roll(v, -1, 0)), open_y)
    middle = (roll(bx, 1, 1) - ax) + (roll(by, 1, 0) - ay)
    return middle, roll(ax, 1, 1), -bx, roll(ay, 1, 0), -by


def inner_sum(t, faces):
    middle, west, east, south, north = faces
    sides = (west * roll(t, 1, 1) + east * roll(t, -1, 1)) + (south * roll(t, 1, 0) + north * roll(t, -1, 0))
    return middle * t + sides


def flipped(x):
    lane = lanes(x.shape[0])
    for step in (1, 2, 4, 8, 16, 32, 64):
        x = jnp.where((lane & step) != 0, roll(x, step, 1), roll(x, -step, 1))
    return x


def both_halves(x, half):
    swapped = roll(x, 64, 1)
    low = lanes() < 64
    return jnp.where(low, x, swapped) if half == 0 else jnp.where(low, swapped, x)


def edge_sign():
    lane = lanes()
    return jnp.where(lane == 0, 1.0, jnp.where(lane == COLS - 1, -1.0, 0.0))


def outward_kernel(
    own, near, far, far_in, near_in, tracer, east, north, mask, mix, bottom,
    pay_far, pay_near, aux, corner_far, *refs,
):
    lat_odd = lax.rem(lax.axis_index("lat"), 2)
    lon_odd = lax.rem(lax.axis_index("lon"), 2)
    is_top = lax.axis_index("lat") == lax.axis_size("lat") - 1
    place = lanes() & 3
    at_east = place == 1
    even = lon_odd == 0
    offset = pl.multiple_of((1 - lon_odd) * PACK_ROWS, ROWS)
    here, one, two = [], [], []
    for p in range(PACKS):
        a = near[pl.ds(pl.multiple_of(offset + p * ROWS, ROWS), ROWS), :]
        b = tile(far, p)
        e = jnp.where(even, a, b)
        w = jnp.where(even, b, a)
        here.append(tile(own, p))
        one.append(jnp.where(at_east, roll(e, -1, 1), roll(w, 1, 1)))
        two.append(jnp.where(at_east, roll(e, -2, 1), roll(w, 2, 1)))
    u0, m0 = both_halves(here[TPACKS], 0), both_halves(here[TPACKS], 1)
    u1, m1 = both_halves(one[TPACKS], 0), both_halves(one[TPACKS], 1)
    u2, m2 = both_halves(two[TPACKS], 0), both_halves(two[TPACKS], 1)
    v0, v1 = both_halves(here[TPACKS + 1], 0), both_halves(one[TPACKS + 1], 0)
    a1, b1 = face(0.5 * (u0 + u1), m0 * m1)
    a2, b2 = face(0.5 * (u1 + u2), m1 * m2)
    inner_y = row_ids() < ROWS - 1
    ay, by = face(0.5 * (v1 + roll(v1, -1, 0)), jnp.where(inner_y, m1 * roll(m1, -1, 0), 0.0))

    def corner(mine, halo):
        return jnp.where(
            place == 0, roll(mine, -1, 1), jnp.where(place == 3, roll(mine, 1, 1), halo)
        )

    for p in range(TPACKS):
        t0, t1, t2 = here[p], one[p], two[p]
        f1 = a1 * jnp.where(at_east, t0, t1) + b1 * jnp.where(at_east, t1, t0)
        f2 = a2 * jnp.where(at_east, t1, t2) + b2 * jnp.where(at_east, t2, t1)
        gn = ay * t1 + by * roll(t1, -1, 0)
        put(aux, AUX_F + p, f1)
        put(aux, AUX_Q + p, t1 + jnp.where(at_east, -f2, f2) + (roll(gn, 1, 0) - gn))
        put(aux, AUX_T + p, corner(t0, t1))
    put(aux, AUX_V, corner(v0, v1))
    put(aux, AUX_M, corner(m0, m1))
    put(aux, AUX_A, a1)
    put(aux, AUX_B, b1)

    del far_in, near_in
    pay_near[ROW_C:, :] = aux[pl.ds(AUX_T * ROWS + (ROWS - 1) * (1 - lat_odd), ROWS, stride=ROWS), :]
    c = aux[pl.ds(AUX_T * ROWS + (ROWS - 1) * lat_odd, ROWS, stride=ROWS), :]
    turned = jnp.where(
        place == 0,
        roll(c, -3, 1),
        jnp.where(place == 1, roll(c, -1, 1), jnp.where(place == 2, roll(c, 1, 1), roll(c, 3, 1))),
    )
    rows = row_ids()
    turned = jnp.where((rows == AUX_V) | (rows >= AUX_F), -turned, turned)
    c = jnp.where(is_top, turned, c)
    pay_far[ROW_C:, :] = c
    corner_far[...] = c

    @pl.when(ahead_of_partner())
    def _():
        columns(tracer, east, north, mask, mix, bottom, aux, *refs)


def spread_out(spread, packed, sign):
    def pair(p):
        x = packed(p)
        for f in (0, 1):
            for k in range(K):
                put(spread, (2 * p + f) * K + k, sign * roll(x, COLS - 1 - (lane_base(f, k) + 1), 1))

    for p in range(TPACKS):
        pair(p)


def columns(tracer, east, north, mask, mix, bottom, aux, full, both, packs, solve, coeff, spread):
    sign = edge_sign()
    spread_out(spread, lambda p: tile(aux, AUX_F + p), sign)

    def level(k):
        faces = level_faces(east, north, mask, k)
        for i in range(5):
            put(coeff, i * K + k, faces[i])
        for f in range(NT):
            index = f * K + k
            t = tile(tracer, index)
            x = t + (inner_sum(t, faces) + tile(spread, index))
            put(full, index, x)
            put(both, index, t + x)

    repeat(K, level, unroll=8)
    for p in range(TPACKS):
        put(packs, p, packed_edges(lambda f, k: tile(full, f * K + k), (2 * p, 2 * p + 1)))
    depth = bottom[...]
    lower = ratio = None
    for k in range(K):
        denom = 1.0
        upper = None
        if k + 1 < K:
            upper = jnp.where(k + 1 < depth, tile(mix, k), 0.0)
            denom = denom + upper
        if k:
            denom = denom + lower + lower * ratio
        inverse = 1.0 / denom
        put(solve, k, 0.5 * inverse)
        if k:
            put(solve, K + k, lower * inverse)
        else:
            put(solve, K + k, jnp.zeros((ROWS, COLS), jnp.float32))
        ratio = -upper * inverse if upper is not None else jnp.zeros((ROWS, COLS), jnp.float32)
        put(solve, 2 * K + k, ratio)
        lower = upper


COLUMN_ROWS = [TILES * ROWS, TILES * ROWS, TPACKS * ROWS, 3 * K * ROWS, 5 * K * ROWS]


def ahead_of_partner():
    lat = lax.axis_index("lat")
    return (lat >= 2) & (lat < 4) & (lax.axis_index("lon") < 2)


class Edge:
    def __init__(self, is_north, tracer, north, mask, other):
        self.is_north, self.tracer, self.other = is_north, tracer, other
        self.row = jnp.where(is_north, ROWS - 1, 0)
        first, second = face(
            0.5 * (edge(north, 0, K, self.row) + other(ROW_V, K)),
            edge(mask, 0, K, self.row).astype(jnp.float32) * other(ROW_M, K),
        )
        self.mine = jnp.where(is_north, -first, second)
        self.theirs = jnp.where(is_north, -second, first)

    def place(self, f):
        return pl.ds(f * K * ROWS + self.row, K, stride=ROWS)

    def fluxes(self, f, flux_row, before):
        line = jnp.broadcast_to(flux_row, (ROWS, COLS))
        sign = edge_sign()
        added = [
            sign * pltpu.roll(line, COLS - 1 - (lane_base(f, k) + 1), 1, stride=4, stride_axis=0) for k in (0, ROWS)
        ]
        beyond = self.other(ROW_P + f * K, K) + jnp.concatenate(added, axis=0)
        g = self.mine * edge(self.tracer, f * K, K, self.row) + self.theirs * self.other(ROW_T + f * K, K)
        s = before + g
        return g, s, self.mine * s + self.theirs * (beyond - g)


def column_kernel(tracer, east, north, mask, mix, bottom, aux, near, *refs):
    count = len(COLUMN_ROWS)

    @pl.when(jnp.logical_not(ahead_of_partner()))
    def _():
        columns(tracer, east, north, mask, mix, bottom, aux, *refs[count:])

    full, sums, _, _, coeff = refs[count : 2 * count]
    lat_odd = lax.rem(lax.axis_index("lat"), 2)
    offset = pl.multiple_of((1 - lat_odd) * PAY_ROWS, ROWS)
    side = Edge(lat_odd == 0, tracer, north, mask, lambda start, size: near[rows_at(offset + start, size), :])
    for f in range(NT):
        place = side.place(f)
        g, s, h = side.fluxes(f, near[pl.ds(offset + ROW_C + AUX_F + f // 2, 1), :], full[place, :])
        full[place, :] = s
        sums[place, :] = sums[place, :] + (g + h)

    def level(k):
        faces = [tile(coeff, i * K + k) for i in range(5)]
        for f in range(NT):
            index = f * K + k
            put(sums, index, tile(sums, index) + inner_sum(tile(full, index), faces))

    repeat(K, level, unroll=8)


def last_kernel(
    early, corner, far, near, tracer, north, mask, coeff, full, sums_in, packs, solve, own, aux,
    result, sums, spread, out, line_1, line_2, line_3, line_4, line_5, sems,
):
    del sums_in
    lines_refs = (line_1, line_2, line_3, line_4)
    lat_odd = lax.rem(lax.axis_index("lat"), 2)
    odd = lat_odd == 1
    offset = pl.multiple_of((1 - lat_odd) * PAY_ROWS, ROWS)
    place = lanes() & 3
    at_east = place == 1
    rows = row_ids()
    at_south, at_north = rows == 0, rows == ROWS - 1

    is_early = early_far(lax.axis_index("lat"), lax.axis_index("lon"), lax.axis_size("lat"), lax.axis_size("lon"))

    def beyond(start, size):
        return jnp.where(is_early, early[start : start + size, :], far[start : start + size, :])

    c_far = jnp.where(is_early, corner[...], far[ROW_C:, :])
    c_near = near[rows_at(offset + ROW_C, ROWS), :]
    c_n, c_s = jnp.where(odd, c_far, c_near), jnp.where(odd, c_near, c_far)
    line_5[...] = c_far

    def inner_columns(c):
        return jnp.where(at_east, roll(c, 1, 1), roll(c, -1, 1))

    d_n, d_s = inner_columns(c_n), inner_columns(c_s)
    v0, m0 = both_halves(tile(own, TPACKS + 1), 0), both_halves(tile(own, TPACKS), 1)
    v1, m1 = tile(aux, AUX_V), tile(aux, AUX_M)

    def corner_faces(v, m, north_rows, south_rows):
        v_n, v_s = north_rows[AUX_V : AUX_V + 1], south_rows[AUX_V : AUX_V + 1]
        m_n, m_s = north_rows[AUX_M : AUX_M + 1], south_rows[AUX_M : AUX_M + 1]
        an, bn = face(0.5 * (v + v_n), jnp.where(at_north, m * m_n, 0.0))
        as_, bs = face(0.5 * (v_s + v), jnp.where(at_south, m_s * m, 0.0))
        return lambda t, t_n, t_s: (as_ * t_s + bs * t) - (an * t + bn * t_n)

    halo_sum = corner_faces(v1, m1, c_n, c_s)
    own_sum = corner_faces(v0, m0, d_n, d_s)
    a1, b1 = tile(aux, AUX_A), tile(aux, AUX_B)
    sign = edge_sign()

    def corner_row(c, ref, p):
        del c
        return ref[pl.ds(p, 1), :]

    for c, ref in zip((c_n, c_s, d_n, d_s), lines_refs):
        ref[...] = c

    def flux_of(p):
        lines = [corner_row(c, ref, p) for c, ref in zip((c_n, c_s, d_n, d_s), lines_refs)]
        f1 = tile(aux, AUX_F + p)
        s1 = tile(aux, AUX_Q + p) + jnp.where(at_east, f1, -f1)
        s1 = s1 + halo_sum(tile(aux, AUX_T + p), lines[0], lines[1])
        s0 = tile(packs, p) + own_sum(tile(own, p), lines[2], lines[3])
        return a1 * jnp.where(at_east, s0, s1) + b1 * jnp.where(at_east, s1, s0)

    spread_out(spread, flux_of, sign)

    side = Edge(odd, tracer, north, mask, beyond)
    inward = jnp.where(odd, ROWS - 2, 1)
    middle, west, east = (edge(coeff, i * K, K, side.row) for i in range(3))
    beside = jnp.where(odd, edge(coeff, 4 * K, K, ROWS - 2), edge(coeff, 3 * K, K, 1))
    for f in range(NT):
        place = side.place(f)
        g, _, h = side.fluxes(f, line_5[AUX_F + f // 2 : AUX_F + f // 2 + 1, :], full[place, :])
        sums[place, :] = sums[place, :] + (g + h + (middle * g + (west * roll(g, 1, 1) + east * roll(g, -1, 1))))
        place = pl.ds(f * K * ROWS + inward, K, stride=ROWS)
        sums[place, :] = sums[place, :] + beside * g

    def copy_of(f):
        place = rows_at(f * K * ROWS, K * ROWS)
        return pltpu.make_async_copy(out.at[place, :], result.at[place, :], sems.at[f])

    def tracer_columns(fields):
        values = {}
        for k in range(K):
            for f in fields:
                index = f * K + k
                value = (tile(sums, index) + tile(spread, index)) * tile(solve, k)
                if k:
                    value = value + tile(solve, K + k) * values[f]
                values[f] = value
                put(out, index, value)
        for k in range(K - 2, -1, -1):
            for f in fields:
                index = f * K + k
                values[f] = tile(out, index) - tile(solve, 2 * K + k) * values[f]
                put(out, index, values[f])
        for f in fields:
            copy_of(f).start()

    for start in range(0, NT, 3):
        tracer_columns(range(start, start + 3))
    for f in range(NT):
        copy_of(f).wait()


def early_far(lat, lon, lat_count, lon_count):
    mirrored = lon_count - 1 - lon
    return (lon % 4 >= 2) & ((lat < lat_count - 1) | (mirrored % 4 >= 2))


def call(kernel, outs, scratch_rows, *operands, hbm=False, hbm_out=0, scratch=(), alias=None):
    vmem = pl.BlockSpec(memory_space=pltpu.VMEM)
    in_hbm = pl.BlockSpec(memory_space=pltpu.HBM)
    shapes = [
        x if isinstance(x, jax.ShapeDtypeStruct) else jax.ShapeDtypeStruct((x, COLS), jnp.float32)
        for x in outs
    ]
    return pl.pallas_call(
        kernel,
        out_shape=shapes,
        in_specs=[in_hbm if hbm else vmem] * len(operands),
        out_specs=[in_hbm] * hbm_out + [vmem] * (len(shapes) - hbm_out),
        scratch_shapes=[pltpu.VMEM((rows, COLS), jnp.float32) for rows in scratch_rows] + list(scratch),
        compiler_params=pltpu.CompilerParams(vmem_limit_bytes=24 * 1024 * 1024),
        input_output_aliases=alias or {},
    )(*operands)


def pairs(lat_count, lon_count):
    def at(i, j):
        return i * lon_count + j % lon_count

    lon_near = [(at(i, j), at(i, j + 1)) for i in range(lat_count) for j in range(0, lon_count, 2)]
    lon_far = [(at(i, j), at(i, j + 1)) for i in range(lat_count) for j in range(1, lon_count, 2)]
    lat_near = [(at(i, j), at(i + 1, j)) for i in range(0, lat_count, 2) for j in range(lon_count)]
    lat_far = [(at(i, j), at(i + 1, j)) for i in range(1, lat_count - 1, 2) for j in range(lon_count)]
    top = lat_count - 1
    lat_far += [(at(top, j), at(top, lon_count - 1 - j)) for j in range(lon_count // 2)]
    return lon_near, lon_far, lat_near, lat_far


def swapped(x, groups):
    return lax.ppermute(x, AXES, [(a, b) for a, b in groups] + [(b, a) for a, b in groups])


def gathered(x, groups):
    both = lax.all_gather(x, AXES, axis_index_groups=[list(g) for g in groups])
    return both.reshape(-1, COLS)


def on_device(tracer, east_vel, north_vel, wet_mask, bottom_level, vertical_mix):
    lon_near, lon_far, lat_near, lat_far = pairs(lax.axis_size("lat"), lax.axis_size("lon"))
    flat = lambda x: x.reshape(-1, COLS)
    fields = [
        pltpu.with_memory_space_constraint(flat(x), pltpu.HBM)
        for x in (tracer, east_vel, north_vel, wet_mask, vertical_mix, bottom_level)
    ]
    own, t, u, v, m, vertical, depth = call(
        load_kernel,
        [PACK_ROWS] + [jax.ShapeDtypeStruct(x.shape, x.dtype) for x in fields],
        [],
        *fields,
        hbm=True,
        scratch=[pltpu.SemaphoreType.DMA((6,))],
    )
    far = swapped(own, lon_far)
    pay_far, pay_near, early, own_again = call(
        rows_kernel, [PAY_ROWS, PAY_ROWS, EARLY_ROWS, PACK_ROWS], [], t, u, v, m, own
    )
    counts = lax.axis_size("lat"), lax.axis_size("lon")
    lat_early = [(a, b) for a, b in lat_far if early_far(*divmod(b, counts[1]), *counts)]
    lat_late = [pair for pair in lat_far if pair not in lat_early]
    early_rows = swapped(early, lat_early)
    near = gathered(own_again, lon_near)
    pay_far, pay_near, aux, corner, *ready = call(
        outward_kernel,
        [PAY_ROWS, PAY_ROWS, AUX * ROWS, ROWS] + COLUMN_ROWS,
        [TILES * ROWS],
        own, near, far, pay_far, pay_near, t, u, v, m, vertical, depth,
        alias={3: 0, 4: 1},
    )
    far_rows = swapped(pay_far, lat_late)
    corner_rows = swapped(corner, lat_early)
    near_rows = gathered(pay_near, lat_near)
    full, both, packs, solve, coeff = call(
        column_kernel,
        COLUMN_ROWS,
        [TILES * ROWS],
        t, u, v, m, vertical, depth, aux, near_rows, *ready,
        alias={8 + i: i for i in range(len(COLUMN_ROWS))},
    )
    out, _ = call(
        last_kernel,
        [TILES * ROWS] * 2,
        [TILES * ROWS, TILES * ROWS] + [ROWS] * 5,
        early_rows, corner_rows, far_rows, near_rows, t, v, m, coeff, full, both, packs, solve, own, aux,
        alias={9: 1},
        scratch=[pltpu.SemaphoreType.DMA((NT,))],
        hbm_out=1,
    )
    return out.reshape(tracer.shape)


def solution(mesh):
    fields = P(None, "lat", "lon")
    tracers = P(None, None, "lat", "lon")
    return jax.shard_map(
        on_device,
        mesh=mesh,
        in_specs=(tracers, fields, fields, fields, P("lat", "lon"), fields),
        out_specs=tracers,
        check_vma=False,
    )
```

```python
import jax
import jax.numpy as jnp
from jax import lax
from jax.experimental import pallas as pl
from jax.experimental.pallas import tpu as pltpu
from jax.sharding import PartitionSpec as P

ROWS = 8
COLS = 128
NT = 6
K = 16
TILES = NT * K
mixing = 0.08
AXES = ("lat", "lon")

FIELDS = NT + 3
PACKS = (FIELDS + 1) // 2
PACK_ROWS = PACKS * ROWS
TPACKS = NT // 2

ROW_T = 0
ROW_P = TILES
ROW_V = 2 * TILES
ROW_M = ROW_V + K
ROW_C = ROW_M + K
PAY_ROWS = ROW_C + ROWS
EARLY_ROWS = PAY_ROWS + ROWS

AUX_T = 0
AUX_V = TPACKS
AUX_M = AUX_V + 1
AUX_F = AUX_M + 1
AUX_Q = AUX_F + TPACKS
AUX_A = AUX_Q + TPACKS
AUX_B = AUX_A + 1
AUX = AUX_B + 1


def roll(x, shift, axis):
    shift %= x.shape[axis]
    return pltpu.roll(x, shift, axis) if shift else x


def lanes(rows=ROWS):
    return lax.broadcasted_iota(jnp.int32, (rows, COLS), 1)


def row_ids():
    return lax.broadcasted_iota(jnp.int32, (ROWS, COLS), 0)


def face(speed, opening):
    return opening * (jnp.maximum(speed, 0.0) + mixing), opening * (jnp.minimum(speed, 0.0) - mixing)


def rows_at(start, size):
    return pl.ds(start if isinstance(start, int) else pl.multiple_of(start, ROWS), size)


def tile(ref, index):
    return ref[rows_at(index * ROWS, ROWS), :]


def put(ref, index, value):
    ref[rows_at(index * ROWS, ROWS), :] = value


def edge(ref, start, size, row):
    return ref[pl.ds(start * ROWS + row, size, stride=ROWS), :]


def repeat(count, body, unroll=1):
    def step(i, carry):
        body(i)
        return carry

    lax.fori_loop(0, count, step, 0, unroll=unroll)


def lane_base(field, k):
    return 64 * (field % 2) + 4 * (K - 1 - k)


def packed_edges(load, fields):
    group = lanes() // 4
    total = jnp.zeros((ROWS, COLS), jnp.float32)
    for field in fields:
        for k in range(K):
            base = lane_base(field, k)
            total = jnp.where(group == base // 4, roll(load(field, k), base - 126, 1), total)
    return total


def row_part(tracer, east, north, mask, row, inward):
    u, m = edge(east, 0, K, row), edge(mask, 0, K, row).astype(jnp.float32)
    v, v_in = edge(north, 0, K, row), edge(north, 0, K, inward)
    m_in = edge(mask, 0, K, inward).astype(jnp.float32)
    ax, bx = face(0.5 * (u + roll(u, -1, 1)), jnp.where(lanes(K) < COLS - 1, m * roll(m, -1, 1), 0.0))
    ay, by = face(0.5 * (v + v_in), m * m_in)
    ts, sums = [], []
    for f in range(NT):
        t, t_in = edge(tracer, f * K, K, row), edge(tracer, f * K, K, inward)
        fe = ax * t + bx * roll(t, -1, 1)
        g = -(ay * t + by * t_in) if inward > row else ay * t_in + by * t
        ts.append(t)
        sums.append(t + ((roll(fe, 1, 1) - fe) + g))
    return ts + sums + [v, m]


def load_kernel(tracer, east, north, mask, mix, bottom, pack, t, u, v, m, vertical, depth, sems):
    copies = [
        pltpu.make_async_copy(src, dst, sems.at[i])
        for i, (src, dst) in enumerate(
            ((tracer, t), (east, u), (north, v), (mask, m), (mix, vertical), (bottom, depth))
        )
    ]
    for copy in copies:
        copy.start()

    def load(field, k):
        if field < NT:
            return tile(t, field * K + k)
        if field == NT:
            return tile(u, k)
        if field == NT + 1:
            return tile(m, k).astype(jnp.float32)
        return tile(v, k)

    for copy in copies[1:4]:
        copy.wait()
    for p in range(TPACKS, PACKS):
        put(pack, p, packed_edges(load, range(2 * p, min(2 * p + 2, FIELDS))))
    copies[0].wait()
    for p in range(TPACKS):
        put(pack, p, packed_edges(load, range(2 * p, 2 * p + 2)))
    for copy in copies[4:]:
        copy.wait()


def rows_kernel(t, u, v, m, own, pay_far, pay_near, early, own_out):
    odd = lax.rem(lax.axis_index("lat"), 2) == 1
    upper = row_part(t, u, v, m, ROWS - 1, ROWS - 2)
    lower = row_part(t, u, v, m, 0, 1)
    for i, (x, y) in enumerate(zip(upper, lower)):
        pay_far[i * K : (i + 1) * K, :] = jnp.where(odd, x, y)
        pay_near[i * K : (i + 1) * K, :] = jnp.where(odd, y, x)
    for pay in (pay_far, pay_near):
        pay[ROW_C:, :] = jnp.zeros((ROWS, COLS), jnp.float32)

    @pl.when(lax.axis_index("lat") == lax.axis_size("lat") - 1)
    def _():
        x = flipped(pay_far[:ROW_C, :])
        pay_far[:ROW_V, :] = x[:ROW_V]
        pay_far[ROW_V:ROW_M, :] = -x[ROW_V:ROW_M]
        pay_far[ROW_M:ROW_C, :] = x[ROW_M:]

    early[:ROW_C, :] = pay_far[:ROW_C, :]
    early[ROW_C:, :] = jnp.zeros((EARLY_ROWS - ROW_C, COLS), jnp.float32)
    own_out[...] = own[...]


def level_faces(east, north, mask, k):
    u, v, m = tile(east, k), tile(north, k), tile(mask, k).astype(jnp.float32)
    open_x = jnp.where(lanes() < COLS - 1, m * roll(m, -1, 1), 0.0)
    open_y = jnp.where(row_ids() < ROWS - 1, m * roll(m, -1, 0), 0.0)
    ax, bx = face(0.5 * (u + roll(u, -1, 1)), open_x)
    ay, by = face(0.5 * (v + roll(v, -1, 0)), open_y)
    middle = (roll(bx, 1, 1) - ax) + (roll(by, 1, 0) - ay)
    return middle, roll(ax, 1, 1), -bx, roll(ay, 1, 0), -by


def inner_sum(t, faces):
    middle, west, east, south, north = faces
    sides = (west * roll(t, 1, 1) + east * roll(t, -1, 1)) + (south * roll(t, 1, 0) + north * roll(t, -1, 0))
    return middle * t + sides


def flipped(x):
    lane = lanes(x.shape[0])
    for step in (1, 2, 4, 8, 16, 32, 64):
        x = jnp.where((lane & step) != 0, roll(x, step, 1), roll(x, -step, 1))
    return x


def both_halves(x, half):
    swapped = roll(x, 64, 1)
    low = lanes() < 64
    return jnp.where(low, x, swapped) if half == 0 else jnp.where(low, swapped, x)


def edge_sign():
    lane = lanes()
    return jnp.where(lane == 0, 1.0, jnp.where(lane == COLS - 1, -1.0, 0.0))


def outward_kernel(
    own, near, far, far_in, near_in, tracer, east, north, mask, mix, bottom,
    pay_far, pay_near, aux, corner_far, *refs,
):
    lat_odd = lax.rem(lax.axis_index("lat"), 2)
    lon_odd = lax.rem(lax.axis_index("lon"), 2)
    is_top = lax.axis_index("lat") == lax.axis_size("lat") - 1
    place = lanes() & 3
    at_east = place == 1
    even = lon_odd == 0
    offset = pl.multiple_of((1 - lon_odd) * PACK_ROWS, ROWS)
    here, one, two = [], [], []
    for p in range(PACKS):
        a = near[pl.ds(pl.multiple_of(offset + p * ROWS, ROWS), ROWS), :]
        b = tile(far, p)
        e = jnp.where(even, a, b)
        w = jnp.where(even, b, a)
        here.append(tile(own, p))
        one.append(jnp.where(at_east, roll(e, -1, 1), roll(w, 1, 1)))
        two.append(jnp.where(at_east, roll(e, -2, 1), roll(w, 2, 1)))
    u0, m0 = both_halves(here[TPACKS], 0), both_halves(here[TPACKS], 1)
    u1, m1 = both_halves(one[TPACKS], 0), both_halves(one[TPACKS], 1)
    u2, m2 = both_halves(two[TPACKS], 0), both_halves(two[TPACKS], 1)
    v0, v1 = both_halves(here[TPACKS + 1], 0), both_halves(one[TPACKS + 1], 0)
    a1, b1 = face(0.5 * (u0 + u1), m0 * m1)
    a2, b2 = face(0.5 * (u1 + u2), m1 * m2)
    inner_y = row_ids() < ROWS - 1
    ay, by = face(0.5 * (v1 + roll(v1, -1, 0)), jnp.where(inner_y, m1 * roll(m1, -1, 0), 0.0))

    def corner(mine, halo):
        return jnp.where(
            place == 0, roll(mine, -1, 1), jnp.where(place == 3, roll(mine, 1, 1), halo)
        )

    for p in range(TPACKS):
        t0, t1, t2 = here[p], one[p], two[p]
        f1 = a1 * jnp.where(at_east, t0, t1) + b1 * jnp.where(at_east, t1, t0)
        f2 = a2 * jnp.where(at_east, t1, t2) + b2 * jnp.where(at_east, t2, t1)
        gn = ay * t1 + by * roll(t1, -1, 0)
        put(aux, AUX_F + p, f1)
        put(aux, AUX_Q + p, t1 + jnp.where(at_east, -f2, f2) + (roll(gn, 1, 0) - gn))
        put(aux, AUX_T + p, corner(t0, t1))
    put(aux, AUX_V, corner(v0, v1))
    put(aux, AUX_M, corner(m0, m1))
    put(aux, AUX_A, a1)
    put(aux, AUX_B, b1)

    del far_in, near_in
    pay_near[ROW_C:, :] = aux[pl.ds(AUX_T * ROWS + (ROWS - 1) * (1 - lat_odd), ROWS, stride=ROWS), :]
    c = aux[pl.ds(AUX_T * ROWS + (ROWS - 1) * lat_odd, ROWS, stride=ROWS), :]
    turned = jnp.where(
        place == 0,
        roll(c, -3, 1),
        jnp.where(place == 1, roll(c, -1, 1), jnp.where(place == 2, roll(c, 1, 1), roll(c, 3, 1))),
    )
    rows = row_ids()
    turned = jnp.where((rows == AUX_V) | (rows >= AUX_F), -turned, turned)
    c = jnp.where(is_top, turned, c)
    pay_far[ROW_C:, :] = c
    corner_far[...] = c

    @pl.when(ahead_of_partner())
    def _():
        columns(tracer, east, north, mask, mix, bottom, aux, *refs)


def spread_out(spread, packed, sign):
    def pair(p):
        x = packed(p)
        for f in (0, 1):
            for k in range(K):
                put(spread, (2 * p + f) * K + k, sign * roll(x, COLS - 1 - (lane_base(f, k) + 1), 1))

    for p in range(TPACKS):
        pair(p)


def columns(tracer, east, north, mask, mix, bottom, aux, full, both, packs, solve, coeff, spread):
    sign = edge_sign()
    spread_out(spread, lambda p: tile(aux, AUX_F + p), sign)

    def level(k):
        faces = level_faces(east, north, mask, k)
        for i in range(5):
            put(coeff, i * K + k, faces[i])
        for f in range(NT):
            index = f * K + k
            t = tile(tracer, index)
            x = t + (inner_sum(t, faces) + tile(spread, index))
            put(full, index, x)
            put(both, index, t + x)

    repeat(K, level, unroll=8)
    for p in range(TPACKS):
        put(packs, p, packed_edges(lambda f, k: tile(full, f * K + k), (2 * p, 2 * p + 1)))
    depth = bottom[...]
    lower = ratio = None
    for k in range(K):
        denom = 1.0
        upper = None
        if k + 1 < K:
            upper = jnp.where(k + 1 < depth, tile(mix, k), 0.0)
            denom = denom + upper
        if k:
            denom = denom + lower + lower * ratio
        inverse = 1.0 / denom
        put(solve, k, 0.5 * inverse)
        if k:
            put(solve, K + k, lower * inverse)
        else:
            put(solve, K + k, jnp.zeros((ROWS, COLS), jnp.float32))
        ratio = -upper * inverse if upper is not None else jnp.zeros((ROWS, COLS), jnp.float32)
        put(solve, 2 * K + k, ratio)
        lower = upper


COLUMN_ROWS = [TILES * ROWS, TILES * ROWS, TPACKS * ROWS, 3 * K * ROWS, 5 * K * ROWS]


def ahead_of_partner():
    lat = lax.axis_index("lat")
    return (lat >= 2) & (lat < 4) & (lax.axis_index("lon") < 2)


class Edge:
    def __init__(self, is_north, tracer, north, mask, other):
        self.is_north, self.tracer, self.other = is_north, tracer, other
        self.row = jnp.where(is_north, ROWS - 1, 0)
        first, second = face(
            0.5 * (edge(north, 0, K, self.row) + other(ROW_V, K)),
            edge(mask, 0, K, self.row).astype(jnp.float32) * other(ROW_M, K),
        )
        self.mine = jnp.where(is_north, -first, second)
        self.theirs = jnp.where(is_north, -second, first)

    def place(self, f):
        return pl.ds(f * K * ROWS + self.row, K, stride=ROWS)

    def fluxes(self, f, flux_row, before):
        line = jnp.broadcast_to(flux_row, (ROWS, COLS))
        sign = edge_sign()
        added = [
            sign * pltpu.roll(line, COLS - 1 - (lane_base(f, k) + 1), 1, stride=4, stride_axis=0) for k in (0, ROWS)
        ]
        beyond = self.other(ROW_P + f * K, K) + jnp.concatenate(added, axis=0)
        g = self.mine * edge(self.tracer, f * K, K, self.row) + self.theirs * self.other(ROW_T + f * K, K)
        s = before + g
        return g, s, self.mine * s + self.theirs * (beyond - g)


def column_kernel(tracer, east, north, mask, mix, bottom, aux, near, *refs):
    count = len(COLUMN_ROWS)

    @pl.when(jnp.logical_not(ahead_of_partner()))
    def _():
        columns(tracer, east, north, mask, mix, bottom, aux, *refs[count:])

    full, sums, _, _, coeff = refs[count : 2 * count]
    lat_odd = lax.rem(lax.axis_index("lat"), 2)
    offset = pl.multiple_of((1 - lat_odd) * PAY_ROWS, ROWS)
    side = Edge(lat_odd == 0, tracer, north, mask, lambda start, size: near[rows_at(offset + start, size), :])
    for f in range(NT):
        place = side.place(f)
        g, s, h = side.fluxes(f, near[pl.ds(offset + ROW_C + AUX_F + f // 2, 1), :], full[place, :])
        full[place, :] = s
        sums[place, :] = sums[place, :] + (g + h)

    def level(k):
        faces = [tile(coeff, i * K + k) for i in range(5)]
        for f in range(NT):
            index = f * K + k
            put(sums, index, tile(sums, index) + inner_sum(tile(full, index), faces))

    repeat(K, level, unroll=8)


def last_kernel(
    early, corner, far, near, tracer, north, mask, coeff, full, sums_in, packs, solve, own, aux,
    result, sums, spread, out, line_1, line_2, line_3, line_4, line_5, sems,
):
    del sums_in
    lines_refs = (line_1, line_2, line_3, line_4)
    lat_odd = lax.rem(lax.axis_index("lat"), 2)
    odd = lat_odd == 1
    offset = pl.multiple_of((1 - lat_odd) * PAY_ROWS, ROWS)
    place = lanes() & 3
    at_east = place == 1
    rows = row_ids()
    at_south, at_north = rows == 0, rows == ROWS - 1

    is_early = early_far(lax.axis_index("lat"), lax.axis_index("lon"), lax.axis_size("lat"), lax.axis_size("lon"))

    def beyond(start, size):
        return jnp.where(is_early, early[start : start + size, :], far[start : start + size, :])

    c_far = jnp.where(is_early, corner[...], far[ROW_C:, :])
    c_near = near[rows_at(offset + ROW_C, ROWS), :]
    c_n, c_s = jnp.where(odd, c_far, c_near), jnp.where(odd, c_near, c_far)
    line_5[...] = c_far

    def inner_columns(c):
        return jnp.where(at_east, roll(c, 1, 1), roll(c, -1, 1))

    d_n, d_s = inner_columns(c_n), inner_columns(c_s)
    v0, m0 = both_halves(tile(own, TPACKS + 1), 0), both_halves(tile(own, TPACKS), 1)
    v1, m1 = tile(aux, AUX_V), tile(aux, AUX_M)

    def corner_faces(v, m, north_rows, south_rows):
        v_n, v_s = north_rows[AUX_V : AUX_V + 1], south_rows[AUX_V : AUX_V + 1]
        m_n, m_s = north_rows[AUX_M : AUX_M + 1], south_rows[AUX_M : AUX_M + 1]
        an, bn = face(0.5 * (v + v_n), jnp.where(at_north, m * m_n, 0.0))
        as_, bs = face(0.5 * (v_s + v), jnp.where(at_south, m_s * m, 0.0))
        return lambda t, t_n, t_s: (as_ * t_s + bs * t) - (an * t + bn * t_n)

    halo_sum = corner_faces(v1, m1, c_n, c_s)
    own_sum = corner_faces(v0, m0, d_n, d_s)
    a1, b1 = tile(aux, AUX_A), tile(aux, AUX_B)
    sign = edge_sign()

    def corner_row(c, ref, p):
        del c
        return ref[pl.ds(p, 1), :]

    for c, ref in zip((c_n, c_s, d_n, d_s), lines_refs):
        ref[...] = c

    def flux_of(p):
        lines = [corner_row(c, ref, p) for c, ref in zip((c_n, c_s, d_n, d_s), lines_refs)]
        f1 = tile(aux, AUX_F + p)
        s1 = tile(aux, AUX_Q + p) + jnp.where(at_east, f1, -f1)
        s1 = s1 + halo_sum(tile(aux, AUX_T + p), lines[0], lines[1])
        s0 = tile(packs, p) + own_sum(tile(own, p), lines[2], lines[3])
        return a1 * jnp.where(at_east, s0, s1) + b1 * jnp.where(at_east, s1, s0)

    spread_out(spread, flux_of, sign)

    side = Edge(odd, tracer, north, mask, beyond)
    inward = jnp.where(odd, ROWS - 2, 1)
    middle, west, east = (edge(coeff, i * K, K, side.row) for i in range(3))
    beside = jnp.where(odd, edge(coeff, 4 * K, K, ROWS - 2), edge(coeff, 3 * K, K, 1))
    for f in range(NT):
        place = side.place(f)
        g, _, h = side.fluxes(f, line_5[AUX_F + f // 2 : AUX_F + f // 2 + 1, :], full[place, :])
        sums[place, :] = sums[place, :] + (g + h + (middle * g + (west * roll(g, 1, 1) + east * roll(g, -1, 1))))
        place = pl.ds(f * K * ROWS + inward, K, stride=ROWS)
        sums[place, :] = sums[place, :] + beside * g

    def copy_of(f):
        place = rows_at(f * K * ROWS, K * ROWS)
        return pltpu.make_async_copy(out.at[place, :], result.at[place, :], sems.at[f])

    def tracer_columns(fields):
        values = {}
        for k in range(K):
            for f in fields:
                index = f * K + k
                value = (tile(sums, index) + tile(spread, index)) * tile(solve, k)
                if k:
                    value = value + tile(solve, K + k) * values[f]
                values[f] = value
                put(out, index, value)
        for k in range(K - 2, -1, -1):
            for f in fields:
                index = f * K + k
                values[f] = tile(out, index) - tile(solve, 2 * K + k) * values[f]
                put(out, index, values[f])
        for f in fields:
            copy_of(f).start()

    for start in range(0, NT, 6):
        tracer_columns(range(start, start + 6))
    for f in range(NT):
        copy_of(f).wait()


def early_far(lat, lon, lat_count, lon_count):
    mirrored = lon_count - 1 - lon
    return (lon % 8 >= 4) & ((lat < lat_count - 1) | (mirrored % 8 >= 4))


def call(kernel, outs, scratch_rows, *operands, hbm=False, hbm_out=0, scratch=(), alias=None):
    vmem = pl.BlockSpec(memory_space=pltpu.VMEM)
    in_hbm = pl.BlockSpec(memory_space=pltpu.HBM)
    shapes = [
        x if isinstance(x, jax.ShapeDtypeStruct) else jax.ShapeDtypeStruct((x, COLS), jnp.float32)
        for x in outs
    ]
    return pl.pallas_call(
        kernel,
        out_shape=shapes,
        in_specs=[in_hbm if hbm else vmem] * len(operands),
        out_specs=[in_hbm] * hbm_out + [vmem] * (len(shapes) - hbm_out),
        scratch_shapes=[pltpu.VMEM((rows, COLS), jnp.float32) for rows in scratch_rows] + list(scratch),
        compiler_params=pltpu.CompilerParams(vmem_limit_bytes=24 * 1024 * 1024),
        input_output_aliases=alias or {},
    )(*operands)


def pairs(lat_count, lon_count):
    def at(i, j):
        return i * lon_count + j % lon_count

    lon_near = [(at(i, j), at(i, j + 1)) for i in range(lat_count) for j in range(0, lon_count, 2)]
    lon_far = [(at(i, j), at(i, j + 1)) for i in range(lat_count) for j in range(1, lon_count, 2)]
    lat_near = [(at(i, j), at(i + 1, j)) for i in range(0, lat_count, 2) for j in range(lon_count)]
    lat_far = [(at(i, j), at(i + 1, j)) for i in range(1, lat_count - 1, 2) for j in range(lon_count)]
    top = lat_count - 1
    lat_far += [(at(top, j), at(top, lon_count - 1 - j)) for j in range(lon_count // 2)]
    return lon_near, lon_far, lat_near, lat_far


def swapped(x, groups):
    return lax.ppermute(x, AXES, [(a, b) for a, b in groups] + [(b, a) for a, b in groups])


def gathered(x, groups):
    both = lax.all_gather(x, AXES, axis_index_groups=[list(g) for g in groups])
    return both.reshape(-1, COLS)


def on_device(tracer, east_vel, north_vel, wet_mask, bottom_level, vertical_mix):
    lon_near, lon_far, lat_near, lat_far = pairs(lax.axis_size("lat"), lax.axis_size("lon"))
    flat = lambda x: x.reshape(-1, COLS)
    fields = [
        pltpu.with_memory_space_constraint(flat(x), pltpu.HBM)
        for x in (tracer, east_vel, north_vel, wet_mask, vertical_mix, bottom_level)
    ]
    own, t, u, v, m, vertical, depth = call(
        load_kernel,
        [PACK_ROWS] + [jax.ShapeDtypeStruct(x.shape, x.dtype) for x in fields],
        [],
        *fields,
        hbm=True,
        scratch=[pltpu.SemaphoreType.DMA((6,))],
    )
    far = swapped(own, lon_far)
    pay_far, pay_near, early, own_again = call(
        rows_kernel, [PAY_ROWS, PAY_ROWS, EARLY_ROWS, PACK_ROWS], [], t, u, v, m, own
    )
    counts = lax.axis_size("lat"), lax.axis_size("lon")
    lat_early = [(a, b) for a, b in lat_far if early_far(*divmod(b, counts[1]), *counts)]
    lat_late = [pair for pair in lat_far if pair not in lat_early]
    early_rows = swapped(early, lat_early)
    near = gathered(own_again, lon_near)
    pay_far, pay_near, aux, corner, *ready = call(
        outward_kernel,
        [PAY_ROWS, PAY_ROWS, AUX * ROWS, ROWS] + COLUMN_ROWS,
        [TILES * ROWS],
        own, near, far, pay_far, pay_near, t, u, v, m, vertical, depth,
        alias={3: 0, 4: 1},
    )
    far_rows = swapped(pay_far, lat_late)
    corner_rows = swapped(corner, lat_early)
    near_rows = gathered(pay_near, lat_near)
    full, both, packs, solve, coeff = call(
        column_kernel,
        COLUMN_ROWS,
        [TILES * ROWS],
        t, u, v, m, vertical, depth, aux, near_rows, *ready,
        alias={8 + i: i for i in range(len(COLUMN_ROWS))},
    )
    out, _ = call(
        last_kernel,
        [TILES * ROWS] * 2,
        [TILES * ROWS, TILES * ROWS] + [ROWS] * 5,
        early_rows, corner_rows, far_rows, near_rows, t, v, m, coeff, full, both, packs, solve, own, aux,
        alias={9: 1},
        scratch=[pltpu.SemaphoreType.DMA((NT,))],
        hbm_out=1,
    )
    return out.reshape(tracer.shape)


def solution(mesh):
    fields = P(None, "lat", "lon")
    tracers = P(None, None, "lat", "lon")
    return jax.shard_map(
        on_device,
        mesh=mesh,
        in_specs=(tracers, fields, fields, fields, P("lat", "lon"), fields),
        out_specs=tracers,
        check_vma=False,
    )
```
